32 devices in a mesh: groups: 2 (over y), dp: 4 (over x, core), proj: 4 (over z).
Axes of the slice: x: 2, y: 2, z: 4, core: 2. Of those that a mesh axis runs over, the one named last changes fastest.
Arguments:
- queries: bfloat16 [2048, 64, 128], P(('groups', 'dp'), 'proj'), parts along dimension 0, may hold values from -6 to 6
- train_grads: bfloat16 [4096, 64, 128], P(('groups', 'dp'), 'proj'), parts along dimension 0, may hold values from -0.0625 to 0.0625
- out_basis: float32 [64, 64], replicated, may hold values from -1 to 2
- in_basis: float32 [128, 128], replicated, may hold values from -1 to 2
- corrections: float32 [64, 128], replicated, may hold values from 0.25 to 4
Outputs:
- scores: float32 [2048, 2048], P(('groups', 'proj'), 'dp'), parts along dimension 0
The draws below stay inside these ranges and needn't reach their ends.
There are 2 independent parts, one for each index of `groups`. The reference program is written for one: setup_inputs(seed, part) draws one part's arguments, and reference() takes and returns one part's arrays. A program takes and returns all parts, laid end to end along the dimension named above; an argument that names none is the same for every part. Nothing has to cross between parts.
All inputs are finite; a program needn't handle non-finite values.
Results may differ from the reference program's by a relative error of at most 0.0085.
Values may be sent and summed in bfloat16 or wider, within the bound.
No kernel may reach another device: no remote copies, remote signals or barrier semaphores. Data moves between devices by JAX's collectives and lax.ppermute only.
A program may use at most 64 MiB of HBM per device.

```python
import math
import jax
import jax.numpy as jnp
from jax import lax

K_OUT = 64
K_IN = 128
QUERIES = 1024
TRAIN = 2048
N_PROJ = 4


def basis_noise(key, order, spread):
    noise = jnp.clip(jax.random.normal(key, (order, order), jnp.float32), -4.0, 4.0)
    return jnp.eye(order, dtype=jnp.float32) + spread * noise / math.sqrt(order)


def draw_out_basis(key, part):
    key = jax.random.fold_in(key, 11)
    return basis_noise(key, K_OUT, 0.5)


def draw_in_basis(key, part):
    key = jax.random.fold_in(key, 23)
    return basis_noise(key, K_IN, 0.5)


def shard_levels(own_key, extent, split, smallest, largest):
    level, own = 1.0, jax.random.fold_in(own_key, 6)
    for axis_at, shards_of in split:
        heights = jnp.exp(jax.random.uniform(jax.random.fold_in(own, axis_at), (shards_of,), jnp.float32, smallest / len(split), largest / len(split)))
        level = level * jnp.repeat(heights, extent[axis_at] // shards_of).reshape([-1 if axis == axis_at else 1 for axis in range(len(extent))])
    return level


def bell_draw(own_key, shape, scale, limit, pieces=(), kind=jnp.bfloat16):
    drawn = scale * jax.random.normal(own_key, shape, jnp.float32)
    if pieces:
        drawn = drawn * shard_levels(own_key, shape, pieces, -0.22, 0.18)
    return jnp.clip(drawn, -limit, limit).astype(kind)


def setup_inputs(seed: int = 0, part: int = 0) -> dict:
    splits = jax.random.split(jax.random.key(seed), 6)
    part_splits = jax.random.split(jax.random.fold_in(splits[5], part), 6)
    return {
        "queries": bell_draw(part_splits[0], (QUERIES, K_OUT, K_IN), 1.0, 6.0, ((0, 4), (1, 4))),
        "train_grads": bell_draw(part_splits[1], (TRAIN, K_OUT, K_IN), (K_OUT * K_IN) ** -0.5, 0.0625, ((0, 4), (1, 4))),
        "out_basis": draw_out_basis(jax.random.fold_in(splits[5], 71), part),
        "in_basis": draw_in_basis(jax.random.fold_in(splits[5], 71), part),
        "corrections": jnp.clip(jnp.exp(jax.random.uniform(splits[4], (K_OUT, K_IN), jnp.float32, math.log(0.25), math.log(4.0))), 0.25, 4.0),
    }


damping_term = 0.05


def condition(block, out_basis, in_basis, corrections):
    highest = lax.Precision.HIGHEST
    values = block.astype(jnp.float32)
    inner = jnp.einsum('qbc,cd->qbd', values, in_basis.astype(jnp.float32), precision=highest)
    rotated = jnp.einsum('ba,qbd->qad', out_basis.astype(jnp.float32), inner, precision=highest)
    scaled = rotated / (corrections + damping_term)
    back = jnp.einsum('qad,ed->qae', scaled, in_basis.astype(jnp.float32), precision=highest)
    result = jnp.einsum('ba,qae->qbe', out_basis.astype(jnp.float32), back, precision=highest)
    return result.astype(jnp.bfloat16)


def reference(queries, train_grads, out_basis, in_basis, corrections):
    conditioned = condition(queries, out_basis, in_basis, corrections)
    slice_rows = K_OUT // N_PROJ
    width = slice_rows * K_IN
    left = conditioned.reshape(QUERIES, N_PROJ, width)
    right = train_grads.reshape(TRAIN, N_PROJ, width)
    total = jnp.zeros((QUERIES, TRAIN), jnp.float32)
    for index in range(N_PROJ):
        partial_value = jnp.dot(left[:, index, :], right[:, index, :].T, preferred_element_type=jnp.float32)
        total = total + partial_value.astype(jnp.bfloat16).astype(jnp.float32)
    return total
```

```python
import jax
import jax.numpy as jnp
from jax import lax
from jax.sharding import PartitionSpec as P

damping_term = 0.05


def condition(block, out_basis, in_basis, corrections):
    high = lax.Precision.HIGH
    values = block.astype(jnp.float32)
    inner = jnp.einsum("qbc,cd->qbd", values, in_basis, precision=high)
    rotated = jnp.einsum("ba,qbd->qad", out_basis, inner, precision=high)
    scaled = rotated / (corrections + damping_term)
    back = jnp.einsum("qad,ed->qae", scaled, in_basis, precision=high)
    result = jnp.einsum("ba,qae->qbe", out_basis, back, precision=high)
    return result.astype(jnp.bfloat16)


def body(queries, train_grads, out_basis, in_basis, corrections):
    rows_here = queries.shape[1]
    width = rows_here * queries.shape[2]
    whole = lax.all_to_all(queries, "proj", split_axis=0, concat_axis=1, tiled=True)
    conditioned = condition(whole, out_basis, in_basis, corrections)
    mine = lax.all_to_all(conditioned, "proj", split_axis=1, concat_axis=0, tiled=True)
    flat = mine.reshape(mine.shape[0], width)
    train_flat = train_grads.reshape(train_grads.shape[0], width)
    contract = (((1,), (1,)), ((), ()))
    partial_value = lax.dot_general(
        lax.all_gather(flat, "dp", axis=0, tiled=True),
        train_flat,
        contract,
        preferred_element_type=jnp.float32,
    )
    scores = lax.psum_scatter(
        partial_value.astype(jnp.bfloat16), "proj", scatter_dimension=0, tiled=True
    ).astype(jnp.float32)
    return scores


def solution(mesh):
    in_specs = (P(("groups", "dp"), "proj", None), P(("groups", "dp"), "proj", None), P(), P(), P())
    out_specs = P(("groups", "proj"), "dp")
    return jax.shard_map(body, mesh=mesh, in_specs=in_specs, out_specs=out_specs, check_vma=False)
```

```python
import jax
import jax.numpy as jnp
from jax import lax
from jax.sharding import PartitionSpec as P

damping_term = 0.05
CHUNKS = 2


def condition(block, out_basis, in_basis, corrections):
    high = lax.Precision.HIGH
    values = block.astype(jnp.float32)
    inner = jnp.einsum("qbc,cd->qbd", values, in_basis, precision=high)
    rotated = jnp.einsum("ba,qbd->qad", out_basis, inner, precision=high)
    scaled = rotated / (corrections + damping_term)
    back = jnp.einsum("qad,ed->qae", scaled, in_basis, precision=high)
    result = jnp.einsum("ba,qae->qbe", out_basis, back, precision=high)
    return result.astype(jnp.bfloat16)


def body(queries, train_grads, out_basis, in_basis, corrections):
    slices = lax.axis_size("proj")
    shares = lax.axis_size("dp")
    count, rows_here, columns = queries.shape
    width = rows_here * columns
    part = count // CHUNKS
    owned = shares // slices
    train_count = train_grads.shape[0]
    train_flat = lax.optimization_barrier(train_grads.reshape(train_count, width))
    contract = (((1,), (1,)), ((), ()))
    results = []
    for chunk in range(CHUNKS):
        raw = queries[chunk * part:(chunk + 1) * part]
        whole = lax.all_to_all(raw, "proj", split_axis=0, concat_axis=1, tiled=True)
        conditioned = condition(whole, out_basis, in_basis, corrections)
        mine = lax.all_to_all(conditioned, "proj", split_axis=1, concat_axis=0, tiled=True)
        flat = mine.reshape(part, width)
        left = lax.all_gather(flat, "dp", axis=0, tiled=True)
        partial_value = lax.dot_general(left, train_flat, contract, preferred_element_type=jnp.float32)
        sent = partial_value.astype(jnp.bfloat16).reshape(slices, owned * part, train_count)
        arrived = lax.all_to_all(sent, "proj", split_axis=0, concat_axis=0, tiled=True)
        total = jnp.sum(arrived.astype(jnp.float32), axis=0)
        results.append(total.reshape(owned, part, train_count))
    return jnp.concatenate(results, axis=1).reshape(owned * count, train_count)


def solution(mesh):
    in_specs = (P(("groups", "dp"), "proj", None), P(("groups", "dp"), "proj", None), P(), P(), P())
    out_specs = P(("groups", "proj"), "dp")
    return jax.shard_map(body, mesh=mesh, in_specs=in_specs, out_specs=out_specs, check_vma=False)
```

```python
import jax
import jax.numpy as jnp
from jax import lax
from jax.sharding import PartitionSpec as P

damping_term = 0.05
CHUNKS = 2
CORES = 2


def condition(block, enter, leave, in_basis, divisor):
    high = lax.Precision.HIGH
    values = block.astype(jnp.float32)
    inner = jnp.einsum("qbc,cd->qbd", values, in_basis, precision=high)
    rotated = jnp.einsum("ba,qbd->qad", enter, inner, precision=high)
    scaled = rotated / divisor
    back = jnp.einsum("qad,ed->qae", scaled, in_basis, precision=high)
    result = jnp.einsum("ba,qae->qbe", leave, back, precision=high)
    return result.astype(jnp.bfloat16)


def shifted(value, axis, size, step):
    return lax.ppermute(value, axis, [(at, (at + step) % size) for at in range(size)])


def pick(blocks, index):
    return lax.dynamic_index_in_dim(blocks, index, 0, keepdims=False)


def body(queries, train_grads, out_basis, in_basis, corrections):
    slices = lax.axis_size("proj")
    shares = lax.axis_size("dp")
    cores = CORES if shares % CORES == 0 else 1
    here = lax.axis_index("proj")
    share = lax.axis_index("dp")
    count, rows_here, columns = queries.shape
    width = rows_here * columns
    part = count // CHUNKS
    each = part // slices
    owned = shares // slices
    train_count = train_grads.shape[0]
    train_flat = lax.optimization_barrier(train_grads.reshape(train_count, width))
    contract = (((1,), (1,)), ((), ()))
    order = jnp.arange(slices)
    row_blocks = out_basis.reshape(slices, rows_here, -1)
    enter = row_blocks[(here - order) % slices].reshape(out_basis.shape)
    leave = row_blocks[(here + order) % slices].reshape(out_basis.shape)
    divisor = corrections + damping_term
    results = []
    for chunk in range(CHUNKS):
        raw = queries[chunk * part:(chunk + 1) * part].reshape(slices, each, rows_here, columns)
        rows = [pick(raw, here)]
        for step in range(1, slices):
            rows.append(shifted(pick(raw, (here + step) % slices), "proj", slices, step))
        conditioned = condition(jnp.concatenate(rows, axis=1), enter, leave, in_basis, divisor)
        mine = jnp.zeros((slices, each, width), jnp.bfloat16)
        for step in range(slices):
            piece = conditioned[:, step * rows_here:(step + 1) * rows_here].reshape(each, width)
            if step:
                piece = shifted(piece, "proj", slices, step)
            mine = lax.dynamic_update_index_in_dim(mine, piece, (here - step) % slices, 0)
        mine = mine.reshape(part, width)
        near = [mine]
        for step in range(cores, shares, cores):
            near.append(shifted(mine, "dp", shares, step))
        near = jnp.concatenate(near, axis=0)
        swap = [(at, at // cores * cores + (at + 1) % cores) for at in range(shares)]
        held = [near] if cores == 1 else [near, lax.ppermute(near, "dp", swap)]
        partial_scores = jnp.zeros((shares, part, train_count), jnp.bfloat16)
        for turn, block in enumerate(held):
            value = lax.dot_general(block, train_flat, contract, preferred_element_type=jnp.float32)
            value = value.astype(jnp.bfloat16).reshape(shares // cores, part, train_count)
            lane = share // cores * cores + (share + turn) % cores
            for step in range(shares // cores):
                at = (lane - step * cores) % shares
                partial_scores = lax.dynamic_update_index_in_dim(partial_scores, value[step], at, 0)
        sent = partial_scores.reshape(slices, owned, part, train_count)
        total = pick(sent, here).astype(jnp.float32)
        for step in range(1, slices):
            total = total + shifted(pick(sent, (here + step) % slices), "proj", slices, step).astype(jnp.float32)
        results.append(total)
    return jnp.concatenate(results, axis=1).reshape(owned * count, train_count)


def solution(mesh):
    in_specs = (P(("groups", "dp"), "proj", None), P(("groups", "dp"), "proj", None), P(), P(), P())
    out_specs = P(("groups", "proj"), "dp")
    return jax.shard_map(body, mesh=mesh, in_specs=in_specs, out_specs=out_specs, check_vma=False)
```

```python
import functools
import jax
import jax.numpy as jnp
from jax import lax
from jax.experimental import pallas as pl
from jax.experimental.pallas import tpu as pltpu
from jax.sharding import PartitionSpec as P

damping_term = 0.05
CHUNKS = 4
BLOCK = 32


def halves(value):
    high = value.astype(jnp.bfloat16)
    return high, (value - high.astype(jnp.float32)).astype(jnp.bfloat16)


def times(left, right):
    return jnp.dot(left, right, preferred_element_type=jnp.float32)


def three_wide(matrix):
    high, low = halves(matrix)
    return jnp.concatenate([high, low, high], axis=1)


def three_deep(matrix):
    high, low = halves(matrix)
    return jnp.concatenate([high, high, low], axis=0)


def condition_kernel(slices, rows_here, *refs):
    pieces = refs[:slices]
    enter, leave, right, back, inverse, own, other, stage = refs[slices:]
    count, _, columns = pieces[0].shape
    out_rows = 2 * rows_here
    parts = []
    for piece in pieces:
        flat = piece[...].reshape(count * rows_here, columns)
        parts.append(halves(times(flat, right[0]) + times(flat, right[1])))
    scale = jnp.concatenate([inverse[...]] * 2, axis=1)

    def gathered(at, which):
        rows = slice(at * rows_here, (at + 1) * rows_here)
        return jnp.concatenate([part[which][rows] for part in parts], axis=0)

    for at in range(0, count, 2):
        high = jnp.concatenate([gathered(at, 0), gathered(at + 1, 0)], axis=1)
        low = jnp.concatenate([gathered(at, 1), gathered(at + 1, 1)], axis=1)
        rotated = times(enter[...], jnp.concatenate([high, high, low], axis=0))
        result = times(leave[...], three_deep(rotated * scale))
        stage[at * out_rows:(at + 1) * out_rows, :] = result[:, :columns]
        stage[(at + 1) * out_rows:(at + 2) * out_rows, :] = result[:, columns:]
    high, low = halves(stage[...])
    stage[...] = times(high, back[0]) + times(low, back[0]) + times(high, back[1])
    for row in range(out_rows):
        value = stage[pl.ds(row, count, stride=out_rows), :].astype(jnp.bfloat16)
        target = own if row < rows_here else other
        at = row % rows_here * columns
        target[:, at:at + columns] = value


def condition_fast(pieces, enter, leave, in_basis, inverse):
    slices = len(pieces)
    count, rows_here, columns = pieces[0].shape
    block = min(BLOCK, count)
    width = rows_here * columns
    piece_spec = pl.BlockSpec((block, rows_here, columns), lambda step: (step, 0, 0))
    out_spec = pl.BlockSpec((block, width), lambda step: (step, 0))
    whole = pl.BlockSpec(memory_space=pltpu.VMEM)
    order = enter.shape[0]
    flops = 2 * count * columns * order * (3 * columns + 5 * order)
    return pl.pallas_call(
        functools.partial(condition_kernel, slices, rows_here),
        grid=(count // block,),
        in_specs=[piece_spec] * slices + [whole] * 5,
        out_specs=[out_spec] * 2,
        out_shape=[jax.ShapeDtypeStruct((count, width), jnp.bfloat16)] * 2,
        scratch_shapes=[pltpu.VMEM((block * 2 * rows_here, columns), jnp.float32)],
        compiler_params=pltpu.CompilerParams(vmem_limit_bytes=32 * 1024 * 1024),
        cost_estimate=pl.CostEstimate(flops=flops, bytes_accessed=(slices + 2) * count * width * 2, transcendentals=0),
    )(
        *pieces,
        three_wide(enter.T),
        three_wide(leave),
        jnp.stack(halves(in_basis)),
        jnp.stack(halves(in_basis.T)),
        inverse,
    )


def condition_plain(pieces, enter, leave, in_basis, inverse):
    high = lax.Precision.HIGH
    count, rows_here, columns = pieces[0].shape
    values = jnp.concatenate(pieces, axis=1).astype(jnp.float32)
    inner = jnp.einsum("qbc,cd->qbd", values, in_basis, precision=high)
    rotated = jnp.einsum("ba,qbd->qad", enter, inner, precision=high)
    left = jnp.einsum("ba,qad->qbd", leave, rotated * inverse, precision=high)
    result = jnp.einsum("qbd,ed->qbe", left, in_basis, precision=high).astype(jnp.bfloat16)
    flat = [result[:, at:at + rows_here].reshape(count, rows_here * columns) for at in (0, rows_here)]
    return flat


def crossed(value, axis, size, mask):
    return lax.ppermute(value, axis, [(at, at ^ mask) for at in range(size)])


def body(queries, train_grads, out_basis, in_basis, corrections):
    slices = lax.axis_size("proj")
    shares = lax.axis_size("dp")
    here = lax.axis_index("proj")
    share = lax.axis_index("dp")
    count, rows_here, columns = queries.shape
    width = rows_here * columns
    part = count // CHUNKS
    each = part // 2
    owned = shares // slices
    odd = here % 2
    train_count = train_grads.shape[0]
    train_flat = lax.optimization_barrier(train_grads.reshape(train_count, width))
    contract = (((1,), (1,)), ((), ()))
    row_blocks = out_basis.reshape(slices, rows_here, -1)
    enter = row_blocks[here ^ jnp.arange(slices)].reshape(out_basis.shape)
    leave = row_blocks[here ^ jnp.arange(2)].reshape(2 * rows_here, -1)
    inverse = 1.0 / (corrections + damping_term)
    condition = condition_fast if rows_here % 16 == 0 else condition_plain
    results = []
    token = None
    for chunk in range(CHUNKS):
        mine = lax.dynamic_slice_in_dim(queries, chunk * part + odd * each, each, 0)
        theirs = lax.dynamic_slice_in_dim(queries, chunk * part + (1 - odd) * each, each, 0)
        if token is not None:
            mine, theirs, pieces[2] = lax.optimization_barrier((mine, theirs, pieces[2]))
        if token is not None:
            waiting.append(pieces)
        else:
            waiting = []
        pieces = [mine]
        for mask in range(1, slices):
            pieces.append(crossed(theirs if mask % 2 else mine, "proj", slices, mask))
        token = pieces[-1]
    waiting.append(pieces)
    for chunk, pieces in enumerate(waiting):
        own, other = condition(pieces, enter, leave, in_basis, inverse)
        near = [own, crossed(other, "proj", slices, 1)]
        near = jnp.concatenate(near, axis=0)
        near = [near] + [crossed(near, "dp", shares, mask) for mask in range(2, shares, 2)]
        near = jnp.concatenate(near, axis=0)
        far = crossed(near, "dp", shares, 1)
        values = []
        for block in (near, far):
            value = lax.dot_general(block, train_flat, contract, preferred_element_type=jnp.float32)
            values.append(value.astype(jnp.bfloat16).reshape(shares // 2, 2, each, train_count))
        blocks = [values[at % 2][at // 2] for at in range(shares)]
        held = [jnp.stack(blocks[at * owned:(at + 1) * owned]) for at in range(slices)]
        place = share // owned
        mask = 1
        while mask < slices:
            swap = (here // mask % 2) != (place // mask % 2)
            keep = [jnp.where(swap, second, first) for first, second in zip(held[::2], held[1::2])]
            send = [jnp.where(swap, first, second) for first, second in zip(held[::2], held[1::2])]
            send = jnp.stack(send)
            if mask == 1:
                send = jnp.concatenate([send[:, :, 1:], send[:, :, :1]], axis=2)
            arrived = crossed(send, "proj", slices, mask)
            mask *= 2
            kind = jnp.bfloat16 if mask < slices else jnp.float32
            held = [(value.astype(jnp.float32) + arrived[at].astype(jnp.float32)).astype(kind) for at, value in enumerate(keep)]
        total = held[0]
        total = jnp.where(odd == 1, jnp.concatenate([total[:, 1:], total[:, :1]], axis=1), total)
        mask = 1
        while mask < owned:
            swapped = total.reshape(owned // (2 * mask), 2, mask, 2, each, train_count)
            swapped = jnp.concatenate([swapped[:, 1:], swapped[:, :1]], axis=1).reshape(total.shape)
            total = jnp.where(share // mask % 2 == 1, swapped, total)
            mask *= 2
        results.append(total.reshape(owned, part, train_count))
    return jnp.concatenate(results, axis=1).reshape(owned * count, train_count)


def solution(mesh):
    in_specs = (P(("groups", "dp"), "proj", None), P(("groups", "dp"), "proj", None), P(), P(), P())
    out_specs = P(("groups", "proj"), "dp")
    return jax.shard_map(body, mesh=mesh, in_specs=in_specs, out_specs=out_specs, check_vma=False)
```

```python
import functools
import jax
import jax.numpy as jnp
from jax import lax
from jax.experimental import pallas as pl
from jax.experimental.pallas import tpu as pltpu
from jax.sharding import PartitionSpec as P

damping_term = 0.05
CHUNKS = (6, 4, 4, 2)
BLOCK = 64


def halves(value):
    high = value.astype(jnp.bfloat16)
    return high, (value - high.astype(jnp.float32)).astype(jnp.bfloat16)


def basis_halves(matrix):
    high = lax.reduce_precision(matrix, 8, 7)
    return high.astype(jnp.bfloat16), (matrix - high).astype(jnp.bfloat16)


def times(left, right):
    return jnp.dot(left, right, preferred_element_type=jnp.float32)


def three_wide(matrix):
    high, low = basis_halves(matrix)
    return jnp.concatenate([high, low, high], axis=1)


def three_deep(matrix):
    high, low = halves(matrix)
    return jnp.concatenate([high, high, low], axis=0)


def condition_kernel(slices, rows_here, *refs):
    pieces = refs[:slices]
    enter, leave, right, back, inverse, own, other, stage = refs[slices:]
    count, _, columns = pieces[0].shape
    out_rows = 2 * rows_here
    parts = []
    for piece in pieces:
        flat = piece[...].reshape(count * rows_here, columns)
        parts.append(halves(times(flat, right[0]) + times(flat, right[1])))
    scale = jnp.concatenate([inverse[...]] * 2, axis=1)

    def gathered(at, which):
        rows = slice(at * rows_here, (at + 1) * rows_here)
        return jnp.concatenate([part[which][rows] for part in parts], axis=0)

    for at in range(0, count, 2):
        high = jnp.concatenate([gathered(at, 0), gathered(at + 1, 0)], axis=1)
        low = jnp.concatenate([gathered(at, 1), gathered(at + 1, 1)], axis=1)
        rotated = times(enter[...], jnp.concatenate([high, high, low], axis=0))
        result = times(leave[...], three_deep(rotated * scale))
        stage[at * out_rows:(at + 1) * out_rows, :] = result[:, :columns]
        stage[(at + 1) * out_rows:(at + 2) * out_rows, :] = result[:, columns:]
    high, low = halves(stage[...])
    stage[...] = times(high, back[0]) + times(low, back[0]) + times(high, back[1])
    for row in range(out_rows):
        value = stage[pl.ds(row, count, stride=out_rows), :].astype(jnp.bfloat16)
        target = own if row < rows_here else other
        at = row % rows_here * columns
        target[:, at:at + columns] = value


def condition_fast(pieces, enter, leave, in_basis, inverse):
    slices = len(pieces)
    count, rows_here, columns = pieces[0].shape
    block = min(BLOCK, count)
    width = rows_here * columns
    piece_spec = pl.BlockSpec((block, rows_here, columns), lambda step: (step, 0, 0))
    out_spec = pl.BlockSpec((block, width), lambda step: (step, 0))
    whole = pl.BlockSpec(memory_space=pltpu.VMEM)
    order = enter.shape[0]
    flops = 2 * count * columns * order * (3 * columns + 5 * order)
    return pl.pallas_call(
        functools.partial(condition_kernel, slices, rows_here),
        grid=(count // block,),
        in_specs=[piece_spec] * slices + [whole] * 5,
        out_specs=[out_spec] * 2,
        out_shape=[jax.ShapeDtypeStruct((count, width), jnp.bfloat16)] * 2,
        scratch_shapes=[pltpu.VMEM((block * 2 * rows_here, columns), jnp.float32)],
        compiler_params=pltpu.CompilerParams(vmem_limit_bytes=32 * 1024 * 1024),
        cost_estimate=pl.CostEstimate(flops=flops, bytes_accessed=(slices + 2) * count * width * 2, transcendentals=0),
    )(
        *pieces,
        three_wide(enter.T),
        three_wide(leave),
        jnp.stack(basis_halves(in_basis)),
        jnp.stack(basis_halves(in_basis.T)),
        inverse,
    )


def condition_plain(pieces, enter, leave, in_basis, inverse):
    high = lax.Precision.HIGH
    count, rows_here, columns = pieces[0].shape
    values = jnp.concatenate(pieces, axis=1).astype(jnp.float32)
    inner = jnp.einsum("qbc,cd->qbd", values, in_basis, precision=high)
    rotated = jnp.einsum("ba,qbd->qad", enter, inner, precision=high)
    left = jnp.einsum("ba,qad->qbd", leave, rotated * inverse, precision=high)
    result = jnp.einsum("qbd,ed->qbe", left, in_basis, precision=high).astype(jnp.bfloat16)
    flat = [result[:, at:at + rows_here].reshape(count, rows_here * columns) for at in (0, rows_here)]
    return flat


def crossed(value, axis, size, mask):
    return lax.ppermute(value, axis, [(at, at ^ mask) for at in range(size)])


def exchange_queries(mine, theirs, slices):
    pieces = [mine]
    for mask in range(1, slices):
        pieces.append(crossed(theirs if mask % 2 else mine, "proj", slices, mask))
    return pieces


def spread_rows(own, other, slices):
    return jnp.concatenate([own, crossed(other, "proj", slices, 1)], axis=0)


def spread_shares(near, shares):
    return jnp.concatenate([near] + [crossed(near, "dp", shares, mask) for mask in range(2, shares, 2)], axis=0)


def products(near, train_flat, shares):
    far = crossed(near, "dp", shares, 1)
    contract = (((1,), (1,)), ((), ()))
    values = []
    for block in (near, far):
        value = lax.dot_general(block, train_flat, contract, preferred_element_type=jnp.float32)
        values.append(value.astype(jnp.bfloat16).reshape(shares // 2, 2, -1, train_flat.shape[0]))
    return [values[at % 2][at // 2] for at in range(shares)]


def split_scores(held, mask, here, place):
    swap = (here // mask % 2) != (place // mask % 2)
    keep = [jnp.where(swap, second, first) for first, second in zip(held[::2], held[1::2])]
    send = jnp.stack([jnp.where(swap, first, second) for first, second in zip(held[::2], held[1::2])])
    if mask == 1:
        send = jnp.concatenate([send[:, :, 1:], send[:, :, :1]], axis=2)
    return keep, send


def add_scores(keep, send, mask, slices):
    arrived = crossed(send, "proj", slices, mask)
    kind = jnp.bfloat16 if 2 * mask < slices else jnp.float32
    return [(value.astype(jnp.float32) + arrived[at].astype(jnp.float32)).astype(kind) for at, value in enumerate(keep)]


def after(value, *tokens):
    tokens = [token for token in tokens if token is not None]
    return lax.optimization_barrier((value, tokens))[0] if tokens else value


def in_order(total, odd, share):
    owned, _, each, train_count = total.shape
    total = jnp.where(odd == 1, jnp.concatenate([total[:, 1:], total[:, :1]], axis=1), total)
    mask = 1
    while mask < owned:
        swapped = total.reshape(owned // (2 * mask), 2, mask, 2, each, train_count)
        swapped = jnp.concatenate([swapped[:, 1:], swapped[:, :1]], axis=1).reshape(total.shape)
        total = jnp.where(share // mask % 2 == 1, swapped, total)
        mask *= 2
    return total.reshape(owned, 2 * each, train_count)


def body(queries, train_grads, out_basis, in_basis, corrections):
    slices = lax.axis_size("proj")
    shares = lax.axis_size("dp")
    here = lax.axis_index("proj")
    share = lax.axis_index("dp")
    count, rows_here, columns = queries.shape
    width = rows_here * columns
    owned = shares // slices
    place = share // owned
    odd = here % 2
    train_count = train_grads.shape[0]
    train_flat = lax.optimization_barrier(train_grads.reshape(train_count, width))
    row_blocks = out_basis.reshape(slices, rows_here, -1)
    enter = row_blocks[here ^ jnp.arange(slices)].reshape(out_basis.shape)
    leave = row_blocks[here ^ jnp.arange(2)].reshape(2 * rows_here, -1)
    inverse = 1.0 / (corrections + damping_term)
    condition = condition_fast if rows_here % 16 == 0 else condition_plain
    parts = [count * size // sum(CHUNKS) for size in CHUNKS]
    chunks = len(parts)
    source = queries
    raw = []
    for chunk, part in enumerate(parts):
        first, each = sum(parts[:chunk]), part // 2
        mine = lax.dynamic_slice_in_dim(source, first + odd * each, each, 0)
        theirs = lax.dynamic_slice_in_dim(source, first + (1 - odd) * each, each, 0)
        if chunk == 0:
            mine, theirs, source = lax.optimization_barrier((mine, theirs, source))
        raw.append((mine, theirs))
    pieces, rows, near, sent = {}, {}, {}, {}
    results = []
    for chunk in range(chunks):
        earlier = pieces[chunk - 1][1] if chunk else None
        mine, theirs = after(raw[chunk], earlier, rows.get(chunk - 2), near.get(chunk - 3))
        pieces[chunk] = exchange_queries(mine, theirs, slices)
        ready = after(pieces[chunk], near.get(chunk - 1), sent.get((chunk - 2, 1)))
        rows[chunk] = condition(ready, enter, leave, in_basis, inverse)
        own, other = rows[chunk]
        near[chunk] = after(spread_rows(own, other, slices), sent.get((chunk - 2, 2)))
        full = after(spread_shares(near[chunk], shares), sent.get((chunk - 1, 1)))
        blocks = products(full, train_flat, shares)
        now = [jnp.stack(blocks[at * owned:(at + 1) * owned]) for at in range(slices)]
        mask = 1
        while mask < slices:
            keep, send = split_scores(now, mask, here, place)
            sent[chunk, mask] = send
            now = add_scores(keep, send, mask, slices)
            mask *= 2
        results.append(in_order(now[0], odd, share))
    return jnp.concatenate(results, axis=1).reshape(owned * count, train_count)


def solution(mesh):
    in_specs = (P(("groups", "dp"), "proj", None), P(("groups", "dp"), "proj", None), P(), P(), P())
    out_specs = P(("groups", "proj"), "dp")
    return jax.shard_map(body, mesh=mesh, in_specs=in_specs, out_specs=out_specs, check_vma=False)
```

```python
import functools
import jax
import jax.numpy as jnp
from jax import lax
from jax.experimental import pallas as pl
from jax.experimental.pallas import tpu as pltpu
from jax.sharding import PartitionSpec as P

damping_term = 0.05
CHUNKS = (8, 8)
BLOCK = 64


def halves(value):
    high = value.astype(jnp.bfloat16)
    return high, (value - high.astype(jnp.float32)).astype(jnp.bfloat16)


def basis_halves(matrix):
    high = lax.reduce_precision(matrix, 8, 7)
    return high.astype(jnp.bfloat16), (matrix - high).astype(jnp.bfloat16)


def times(left, right):
    return jnp.dot(left, right, preferred_element_type=jnp.float32)


def three_wide(matrix):
    high, low = basis_halves(matrix)
    return jnp.concatenate([high, low, high], axis=1)


def three_deep(matrix):
    high, low = halves(matrix)
    return jnp.concatenate([high, high, low], axis=0)


def condition_kernel(slices, rows_here, *refs):
    pieces = refs[:slices]
    enter, leave, right, back, inverse = refs[slices:slices + 5]
    outs, stage = refs[slices + 5:-1], refs[-1]
    count, _, columns = pieces[0].shape
    out_rows = slices * rows_here
    parts = []
    for piece in pieces:
        flat = piece[...].reshape(count * rows_here, columns)
        parts.append(halves(times(flat, right[0]) + times(flat, right[1])))
    scale = jnp.concatenate([inverse[...]] * 2, axis=1)

    def gathered(at, which):
        rows = slice(at * rows_here, (at + 1) * rows_here)
        return jnp.concatenate([part[which][rows] for part in parts], axis=0)

    for at in range(0, count, 2):
        high = jnp.concatenate([gathered(at, 0), gathered(at + 1, 0)], axis=1)
        low = jnp.concatenate([gathered(at, 1), gathered(at + 1, 1)], axis=1)
        rotated = times(enter[...], jnp.concatenate([high, high, low], axis=0))
        result = times(leave[...], three_deep(rotated * scale))
        stage[at * out_rows:(at + 1) * out_rows, :] = result[:, :columns]
        stage[(at + 1) * out_rows:(at + 2) * out_rows, :] = result[:, columns:]
    high, low = halves(stage[...])
    stage[...] = times(high, back[0]) + times(low, back[0]) + times(high, back[1])
    for row in range(out_rows):
        value = stage[pl.ds(row, count, stride=out_rows), :].astype(jnp.bfloat16)
        at = row % rows_here * columns
        outs[row // rows_here][:, at:at + columns] = value


def condition_fast(pieces, enter, leave, in_basis, inverse):
    slices = len(pieces)
    count, rows_here, columns = pieces[0].shape
    block = min(BLOCK, count)
    width = rows_here * columns
    piece_spec = pl.BlockSpec((block, rows_here, columns), lambda step: (step, 0, 0))
    out_spec = pl.BlockSpec((block, width), lambda step: (step, 0))
    whole = pl.BlockSpec(memory_space=pltpu.VMEM)
    order = enter.shape[0]
    return pl.pallas_call(
        functools.partial(condition_kernel, slices, rows_here),
        grid=(count // block,),
        in_specs=[piece_spec] * slices + [whole] * 5,
        out_specs=[out_spec] * slices,
        out_shape=[jax.ShapeDtypeStruct((count, width), jnp.bfloat16)] * slices,
        scratch_shapes=[pltpu.VMEM((block * order, columns), jnp.float32)],
        compiler_params=pltpu.CompilerParams(vmem_limit_bytes=32 * 1024 * 1024),
        cost_estimate=pl.CostEstimate(flops=0, bytes_accessed=0, transcendentals=0),
    )(
        *pieces,
        three_wide(enter.T),
        three_wide(leave),
        jnp.stack(basis_halves(in_basis)),
        jnp.stack(basis_halves(in_basis.T)),
        inverse,
    )


def condition_plain(pieces, enter, leave, in_basis, inverse):
    high = lax.Precision.HIGH
    count, rows_here, columns = pieces[0].shape
    values = jnp.concatenate(pieces, axis=1).astype(jnp.float32)
    inner = jnp.einsum("qbc,cd->qbd", values, in_basis, precision=high)
    rotated = jnp.einsum("ba,qbd->qad", enter, inner, precision=high)
    left = jnp.einsum("ba,qad->qbd", leave, rotated * inverse, precision=high)
    result = jnp.einsum("qbd,ed->qbe", left, in_basis, precision=high).astype(jnp.bfloat16)
    starts = range(0, enter.shape[0], rows_here)
    return [result[:, at:at + rows_here].reshape(count, rows_here * columns) for at in starts]


def crossed(value, axis, size, mask):
    return lax.ppermute(value, axis, [(at, at ^ mask) for at in range(size)])


def after(value, *tokens):
    return lax.optimization_barrier((value, tokens))[0]


def spread_shares(near, shares):
    return jnp.concatenate([near] + [crossed(near, "dp", shares, mask) for mask in range(2, shares, 2)], axis=0)


def products(near, far, train_flat, shares):
    contract = (((1,), (1,)), ((), ()))
    values = []
    for block in (near, far):
        value = lax.dot_general(block, train_flat, contract, preferred_element_type=jnp.float32)
        values.append(value.astype(jnp.bfloat16).reshape(shares // 2, -1, train_flat.shape[0]))
    return [values[at % 2][at // 2] for at in range(shares)]


def turned(blocks, mask):
    bit = 1
    while bit < len(blocks):
        swap = mask // bit % 2 == 1
        blocks = [jnp.where(swap, blocks[at ^ bit], blocks[at]) for at in range(len(blocks))]
        bit *= 2
    return blocks


def body(queries, train_grads, out_basis, in_basis, corrections):
    slices = lax.axis_size("proj")
    shares = lax.axis_size("dp")
    here = lax.axis_index("proj")
    share = lax.axis_index("dp")
    count, rows_here, columns = queries.shape
    width = rows_here * columns
    owned = shares // slices
    train_count = train_grads.shape[0]
    train_flat = lax.optimization_barrier(train_grads.reshape(train_count, width))
    row_blocks = out_basis.reshape(slices, rows_here, -1)
    basis = jnp.concatenate(turned([row_blocks[at] for at in range(slices)], here), axis=0)
    inverse = 1.0 / (corrections + damping_term)
    condition = condition_fast if rows_here % 16 == 0 else condition_plain
    parts = [count * size // sum(CHUNKS) for size in CHUNKS]
    firsts = [sum(parts[:chunk]) for chunk in range(len(parts))]
    pieces, rows, blocks, results = [], [], [], []
    source = queries
    for first, part in zip(firsts, parts):
        each = part // slices
        raw = [lax.dynamic_slice_in_dim(source, first + (here ^ mask) * each, each, 0) for mask in range(slices)]
        if pieces:
            raw = after(raw, pieces[-1][1])
        else:
            raw, source = lax.optimization_barrier((raw, source))
        pieces.append([raw[0]] + [crossed(raw[mask], "proj", slices, mask) for mask in range(1, slices)])
    for chunk in range(len(parts)):
        made = condition(pieces[chunk], basis, basis, in_basis, inverse)
        rows.append([made[0]] + [crossed(made[mask], "proj", slices, mask) for mask in range(1, slices)])
    for chunk, part in enumerate(parts):
        near = spread_shares(jnp.concatenate(rows[chunk], axis=0), shares)
        near = after(near, *blocks[-1:])
        far = crossed(near, "dp", shares, 1)
        values = products(near, far, train_flat, shares)
        values = [jnp.stack(values[at * owned:(at + 1) * owned]) for at in range(slices)]
        blocks.append(turned(values, here ^ (share // owned)))
    for part, block in zip(parts, blocks):
        came = [block[0]] + [crossed(block[mask], "proj", slices, mask) for mask in range(1, slices)]
        came = [value.reshape(owned, slices, part // slices, train_count) for value in came]
        total = [sum(came[mask][:, at ^ mask].astype(jnp.float32) for mask in range(slices)) for at in range(slices)]
        total = jnp.stack(turned(total, here), axis=1)
        total = jnp.stack(turned([total[at] for at in range(owned)], share % owned))
        results.append(total.reshape(owned, part, train_count))
    return jnp.concatenate(results, axis=1).reshape(owned * count, train_count)


def solution(mesh):
    in_specs = (P(("groups", "dp"), "proj", None), P(("groups", "dp"), "proj", None), P(), P(), P())
    out_specs = P(("groups", "proj"), "dp")
    return jax.shard_map(body, mesh=mesh, in_specs=in_specs, out_specs=out_specs, check_vma=False)
```

```python
import functools
import jax
import jax.numpy as jnp
from jax import lax
from jax.experimental import pallas as pl
from jax.experimental.pallas import tpu as pltpu
from jax.sharding import PartitionSpec as P

damping_term = 0.05
BLOCK = 64
SPLIT = 2


def halves(value):
    high = value.astype(jnp.bfloat16)
    return high, (value - high.astype(jnp.float32)).astype(jnp.bfloat16)


def basis_halves(matrix):
    high = lax.reduce_precision(matrix, 8, 7)
    return high.astype(jnp.bfloat16), (matrix - high).astype(jnp.bfloat16)


def times(left, right):
    return jnp.dot(left, right, preferred_element_type=jnp.float32)


def three_wide(matrix):
    high, low = basis_halves(matrix)
    return jnp.concatenate([high, low, high], axis=1)


def three_deep(matrix):
    high, low = halves(matrix)
    return jnp.concatenate([high, high, low], axis=0)


def condition_kernel(slices, rows_here, *refs):
    pieces = refs[:slices]
    enter, leave, right, back, inverse = refs[slices:slices + 5]
    outs, stage = refs[slices + 5:-1], refs[-1]
    count, _, columns = pieces[0].shape
    out_rows = slices * rows_here
    parts = []
    for piece in pieces:
        flat = piece[...].reshape(count * rows_here, columns)
        parts.append(halves(times(flat, right[0]) + times(flat, right[1])))
    scale = jnp.concatenate([inverse[...]] * 2, axis=1)

    def gathered(at, which):
        rows = slice(at * rows_here, (at + 1) * rows_here)
        return jnp.concatenate([part[which][rows] for part in parts], axis=0)

    for at in range(0, count, 2):
        high = jnp.concatenate([gathered(at, 0), gathered(at + 1, 0)], axis=1)
        low = jnp.concatenate([gathered(at, 1), gathered(at + 1, 1)], axis=1)
        rotated = times(enter[...], jnp.concatenate([high, high, low], axis=0))
        result = times(leave[...], three_deep(rotated * scale))
        stage[at * out_rows:(at + 1) * out_rows, :] = result[:, :columns]
        stage[(at + 1) * out_rows:(at + 2) * out_rows, :] = result[:, columns:]
    high, low = halves(stage[...])
    stage[...] = times(high, back[0]) + times(low, back[0]) + times(high, back[1])
    for row in range(out_rows):
        value = stage[pl.ds(row, count, stride=out_rows), :].astype(jnp.bfloat16)
        at = row % rows_here * columns
        outs[row // rows_here][:, at:at + columns] = value


def condition_fast(pieces, enter, leave, in_basis, inverse):
    slices = len(pieces)
    count, rows_here, columns = pieces[0].shape
    block = min(BLOCK, count)
    width = rows_here * columns
    piece_spec = pl.BlockSpec((block, rows_here, columns), lambda step: (step, 0, 0))
    out_spec = pl.BlockSpec((block, width), lambda step: (step, 0))
    whole = pl.BlockSpec(memory_space=pltpu.VMEM)
    order = enter.shape[0]
    return pl.pallas_call(
        functools.partial(condition_kernel, slices, rows_here),
        grid=(count // block,),
        in_specs=[piece_spec] * slices + [whole] * 5,
        out_specs=[out_spec] * slices,
        out_shape=[jax.ShapeDtypeStruct((count, width), jnp.bfloat16)] * slices,
        scratch_shapes=[pltpu.VMEM((block * order, columns), jnp.float32)],
        compiler_params=pltpu.CompilerParams(vmem_limit_bytes=32 * 1024 * 1024),
        cost_estimate=pl.CostEstimate(flops=0, bytes_accessed=0, transcendentals=0),
    )(
        *pieces,
        three_wide(enter.T),
        three_wide(leave),
        jnp.stack(basis_halves(in_basis)),
        jnp.stack(basis_halves(in_basis.T)),
        inverse,
    )


def condition_plain(pieces, enter, leave, in_basis, inverse):
    high = lax.Precision.HIGH
    count, rows_here, columns = pieces[0].shape
    values = jnp.concatenate(pieces, axis=1).astype(jnp.float32)
    inner = jnp.einsum("qbc,cd->qbd", values, in_basis, precision=high)
    rotated = jnp.einsum("ba,qbd->qad", enter, inner, precision=high)
    left = jnp.einsum("ba,qad->qbd", leave, rotated * inverse, precision=high)
    result = jnp.einsum("qbd,ed->qbe", left, in_basis, precision=high).astype(jnp.bfloat16)
    starts = range(0, enter.shape[0], rows_here)
    return [result[:, at:at + rows_here].reshape(count, rows_here * columns) for at in starts]


def crossed(value, axis, size, mask):
    return lax.ppermute(value, axis, [(at, at ^ mask) for at in range(size)])


def after(value, *tokens):
    return lax.optimization_barrier((value, tokens))[0]


def spread_shares(near, shares):
    return jnp.concatenate([near] + [crossed(near, "dp", shares, mask) for mask in range(2, shares, 2)], axis=0)


def products(near, far, train_flat, shares):
    contract = (((1,), (1,)), ((), ()))
    values = []
    for block in (near, far):
        value = lax.dot_general(block, train_flat, contract, preferred_element_type=jnp.float32)
        values.append(value.astype(jnp.bfloat16).reshape(shares // 2, -1, train_flat.shape[0]))
    return [values[at % 2][at // 2] for at in range(shares)]


def turned(blocks, mask):
    bit = 1
    while bit < len(blocks):
        swap = mask // bit % 2 == 1
        blocks = [jnp.where(swap, blocks[at ^ bit], blocks[at]) for at in range(len(blocks))]
        bit *= 2
    return blocks


def body(queries, train_grads, out_basis, in_basis, corrections):
    slices = lax.axis_size("proj")
    shares = lax.axis_size("dp")
    here = lax.axis_index("proj")
    share = lax.axis_index("dp")
    count, rows_here, columns = queries.shape
    width = rows_here * columns
    owned = shares // slices
    train_count = train_grads.shape[0]
    train_flat = lax.optimization_barrier(train_grads.reshape(train_count, width))
    row_blocks = out_basis.reshape(slices, rows_here, -1)
    basis = jnp.concatenate(turned([row_blocks[at] for at in range(slices)], here), axis=0)
    inverse = 1.0 / (corrections + damping_term)
    condition = condition_fast if rows_here % 16 == 0 else condition_plain
    each = count // slices
    raw = [None] * slices
    source = queries
    for mask in reversed(range(slices)):
        block = lax.dynamic_slice_in_dim(source, (here ^ mask) * each, each, 0)
        raw[mask], source = lax.optimization_barrier((block, source))
    arrived = [raw[0]] + [crossed(raw[mask], "proj", slices, mask) for mask in range(1, slices)]
    arrived, train_flat = lax.optimization_barrier((arrived, train_flat))
    made = condition(arrived, basis, basis, in_basis, inverse)
    rows = [made[0]] + [crossed(made[mask], "proj", slices, mask) for mask in range(1, slices)]
    half = slices // 2
    groups = [range(half), range(half, slices)]
    scores = [[None] * slices for _ in range(slices)]
    came = []
    for group in groups:
        own = [rows[at] for at in group]
        if not came:
            own = own[:-1] + jnp.split(own[-1], SPLIT)
        near = own
        for mask in range(2, shares, 2):
            near = near + [crossed(row, "dp", shares, mask) for row in own]
        near = after(jnp.concatenate(near, axis=0), *(came[1:-1] or rows[half:]))
        far = after(crossed(near, "dp", shares, 1), *came[-1:])
        blocks = products(near, far, train_flat, shares)
        blocks = [jnp.stack(blocks[at * owned:(at + 1) * owned]) for at in range(slices)]
        blocks = turned(blocks, here ^ (share // owned))
        came = [blocks[0]] + [crossed(blocks[mask], "proj", slices, mask) for mask in range(1, slices)]
        for mask, block in enumerate(came):
            block = block.reshape(owned, len(group), each, train_count)
            for place, at in enumerate(group):
                scores[at ^ mask][mask] = block[:, place].astype(jnp.float32)
    total = [sum(scores[at]) for at in range(slices)]
    total = jnp.stack(turned(total, here), axis=1)
    total = jnp.stack(turned([total[at] for at in range(owned)], share % owned))
    return total.reshape(owned * count, train_count)


def solution(mesh):
    in_specs = (P(("groups", "dp"), "proj", None), P(("groups", "dp"), "proj", None), P(), P(), P())
    out_specs = P(("groups", "proj"), "dp")
    return jax.shard_map(body, mesh=mesh, in_specs=in_specs, out_specs=out_specs, check_vma=False)
```

```python
import functools
import jax
import jax.numpy as jnp
from jax import lax
from jax.experimental import pallas as pl
from jax.experimental.pallas import tpu as pltpu
from jax.sharding import PartitionSpec as P

damping_term = 0.05
CHUNKS = (8, 8)
BLOCK = 64


def halves(value):
    high = value.astype(jnp.bfloat16)
    return high, (value - high.astype(jnp.float32)).astype(jnp.bfloat16)


def basis_halves(matrix):
    high = lax.reduce_precision(matrix, 8, 7)
    return high.astype(jnp.bfloat16), (matrix - high).astype(jnp.bfloat16)


def times(left, right):
    return jnp.dot(left, right, preferred_element_type=jnp.float32)


def three_wide(matrix):
    high, low = basis_halves(matrix)
    return jnp.concatenate([high, low, high], axis=1)


def three_deep(matrix):
    high, low = halves(matrix)
    return jnp.concatenate([high, high, low], axis=0)


def condition_kernel(slices, rows_here, *refs):
    pieces = refs[:slices]
    enter, leave, right, back, inverse = refs[slices:slices + 5]
    outs, stage = refs[slices + 5:-1], refs[-1]
    count, _, columns = pieces[0].shape
    out_rows = slices * rows_here
    parts = []
    for piece in pieces:
        flat = piece[...].reshape(count * rows_here, columns)
        parts.append(halves(times(flat, right[0]) + times(flat, right[1])))
    scale = jnp.concatenate([inverse[...]] * 2, axis=1)

    def gathered(at, which):
        rows = slice(at * rows_here, (at + 1) * rows_here)
        return jnp.concatenate([part[which][rows] for part in parts], axis=0)

    for at in range(0, count, 2):
        high = jnp.concatenate([gathered(at, 0), gathered(at + 1, 0)], axis=1)
        low = jnp.concatenate([gathered(at, 1), gathered(at + 1, 1)], axis=1)
        rotated = times(enter[...], jnp.concatenate([high, high, low], axis=0))
        result = times(leave[...], three_deep(rotated * scale))
        stage[at * out_rows:(at + 1) * out_rows, :] = result[:, :columns]
        stage[(at + 1) * out_rows:(at + 2) * out_rows, :] = result[:, columns:]
    high, low = halves(stage[...])
    stage[...] = times(high, back[0]) + times(low, back[0]) + times(high, back[1])
    for row in range(out_rows):
        value = stage[pl.ds(row, count, stride=out_rows), :].astype(jnp.bfloat16)
        at = row % rows_here * columns
        outs[row // rows_here][:, at:at + columns] = value


def condition_fast(pieces, enter, leave, in_basis, inverse):
    slices = len(pieces)
    count, rows_here, columns = pieces[0].shape
    block = min(BLOCK, count)
    width = rows_here * columns
    piece_spec = pl.BlockSpec((block, rows_here, columns), lambda step: (step, 0, 0))
    out_spec = pl.BlockSpec((block, width), lambda step: (step, 0))
    whole = pl.BlockSpec(memory_space=pltpu.VMEM)
    order = enter.shape[0]
    return pl.pallas_call(
        functools.partial(condition_kernel, slices, rows_here),
        grid=(count // block,),
        in_specs=[piece_spec] * slices + [whole] * 5,
        out_specs=[out_spec] * slices,
        out_shape=[jax.ShapeDtypeStruct((count, width), jnp.bfloat16)] * slices,
        scratch_shapes=[pltpu.VMEM((block * order, columns), jnp.float32)],
        compiler_params=pltpu.CompilerParams(vmem_limit_bytes=32 * 1024 * 1024),
        cost_estimate=pl.CostEstimate(flops=0, bytes_accessed=0, transcendentals=0),
    )(
        *pieces,
        three_wide(enter.T),
        three_wide(leave),
        jnp.stack(basis_halves(in_basis)),
        jnp.stack(basis_halves(in_basis.T)),
        inverse,
    )


def condition_plain(pieces, enter, leave, in_basis, inverse):
    high = lax.Precision.HIGH
    count, rows_here, columns = pieces[0].shape
    values = jnp.concatenate(pieces, axis=1).astype(jnp.float32)
    inner = jnp.einsum("qbc,cd->qbd", values, in_basis, precision=high)
    rotated = jnp.einsum("ba,qbd->qad", enter, inner, precision=high)
    left = jnp.einsum("ba,qad->qbd", leave, rotated * inverse, precision=high)
    result = jnp.einsum("qbd,ed->qbe", left, in_basis, precision=high).astype(jnp.bfloat16)
    starts = range(0, enter.shape[0], rows_here)
    return [result[:, at:at + rows_here].reshape(count, rows_here * columns) for at in starts]


def crossed(value, axis, size, mask):
    return lax.ppermute(value, axis, [(at, at ^ mask) for at in range(size)])


def exchanged(blocks, slices):
    moved = {mask: crossed(blocks[mask], "proj", slices, mask) for mask in reversed(range(1, slices))}
    return [blocks[0]] + [moved[mask] for mask in range(1, slices)]


def after(value, *tokens):
    return lax.optimization_barrier((value, tokens))[0]


def spread_shares(near, shares):
    return jnp.concatenate([near] + [crossed(near, "dp", shares, mask) for mask in range(2, shares, 2)], axis=0)


def products(near, far, train_flat, shares):
    contract = (((1,), (1,)), ((), ()))
    values = []
    for block in (near, far):
        value = lax.dot_general(block, train_flat, contract, preferred_element_type=jnp.float32)
        values.append(value.astype(jnp.bfloat16).reshape(shares // 2, -1, train_flat.shape[0]))
    return [values[at % 2][at // 2] for at in range(shares)]


def turned(blocks, mask):
    bit = 1
    while bit < len(blocks):
        swap = mask // bit % 2 == 1
        blocks = [jnp.where(swap, blocks[at ^ bit], blocks[at]) for at in range(len(blocks))]
        bit *= 2
    return blocks


def body(queries, train_grads, out_basis, in_basis, corrections):
    slices = lax.axis_size("proj")
    shares = lax.axis_size("dp")
    here = lax.axis_index("proj")
    share = lax.axis_index("dp")
    count, rows_here, columns = queries.shape
    width = rows_here * columns
    owned = shares // slices
    train_count = train_grads.shape[0]
    train_flat = lax.optimization_barrier(train_grads.reshape(train_count, width))
    row_blocks = out_basis.reshape(slices, rows_here, -1)
    basis = jnp.concatenate(turned([row_blocks[at] for at in range(slices)], here), axis=0)
    inverse = 1.0 / (corrections + damping_term)
    condition = condition_fast if rows_here % 16 == 0 else condition_plain
    parts = [count * size // sum(CHUNKS) for size in CHUNKS]
    firsts = [sum(parts[:chunk]) for chunk in range(len(parts))]
    pieces, rows, blocks, results = [], [], [], []
    source = queries
    for first, part in zip(firsts, parts):
        each = part // slices
        raw = [lax.dynamic_slice_in_dim(source, first + (here ^ mask) * each, each, 0) for mask in range(slices)]
        raw, source = lax.optimization_barrier((raw, source))
        pieces.append(exchanged(raw, slices))
    for chunk in range(len(parts)):
        pieces[chunk], train_flat = lax.optimization_barrier((pieces[chunk], train_flat))
        made = condition(pieces[chunk], basis, basis, in_basis, inverse)
        rows.append(exchanged(made, slices))
    came = []
    for chunk, part in enumerate(parts):
        near = spread_shares(jnp.concatenate(rows[chunk], axis=0), shares)
        near = after(near, *came[2:3])
        far = crossed(near, "dp", shares, 1)
        values = products(near, far, train_flat, shares)
        values = [jnp.stack(values[at * owned:(at + 1) * owned]) for at in range(slices)]
        came = exchanged(turned(values, here ^ (share // owned)), slices)
        sums = [value.reshape(owned, slices, part // slices, train_count) for value in came]
        total = [sum(sums[mask][:, at ^ mask].astype(jnp.float32) for mask in range(slices)) for at in range(slices)]
        total = jnp.stack(turned(total, here), axis=1)
        total = jnp.stack(turned([total[at] for at in range(owned)], share % owned))
        results.append(total.reshape(owned, part, train_count))
    return jnp.concatenate(results, axis=1).reshape(owned * count, train_count)


def solution(mesh):
    in_specs = (P(("groups", "dp"), "proj", None), P(("groups", "dp"), "proj", None), P(), P(), P())
    out_specs = P(("groups", "proj"), "dp")
    return jax.shard_map(body, mesh=mesh, in_specs=in_specs, out_specs=out_specs, check_vma=False)
```

```python
import functools
import jax
import jax.numpy as jnp
from jax import lax
from jax.experimental import pallas as pl
from jax.experimental.pallas import tpu as pltpu
from jax.sharding import PartitionSpec as P

damping_term = 0.05
CHUNKS = (8, 8)
BLOCK = 64


def halves(value):
    high = value.astype(jnp.bfloat16)
    return high, (value - high.astype(jnp.float32)).astype(jnp.bfloat16)


def times(left, right):
    return jnp.dot(left, right, preferred_element_type=jnp.float32)


def three_wide(matrix):
    high, low = halves(matrix)
    return jnp.concatenate([high, low, high], axis=1)


def three_deep(matrix):
    high, low = halves(matrix)
    return jnp.concatenate([high, high, low], axis=0)


def condition_kernel(slices, rows_here, *refs):
    pieces = refs[:slices]
    basis, across, right_basis, right_across, corrections = refs[slices:slices + 5]
    outs, stage = refs[slices + 5:-1], refs[-1]
    enter, leave = three_wide(across[...]), three_wide(basis[...])
    right, back = halves(right_basis[...]), halves(right_across[...])
    count, _, columns = pieces[0].shape
    out_rows = slices * rows_here
    parts = []
    for piece in pieces:
        flat = piece[...].reshape(count * rows_here, columns)
        parts.append(halves(times(flat, right[0]) + times(flat, right[1])))
    scale = jnp.concatenate([1.0 / (corrections[...] + damping_term)] * 2, axis=1)

    def gathered(at, which):
        rows = slice(at * rows_here, (at + 1) * rows_here)
        return jnp.concatenate([part[which][rows] for part in parts], axis=0)

    for at in range(0, count, 2):
        high = jnp.concatenate([gathered(at, 0), gathered(at + 1, 0)], axis=1)
        low = jnp.concatenate([gathered(at, 1), gathered(at + 1, 1)], axis=1)
        rotated = times(enter, jnp.concatenate([high, high, low], axis=0))
        result = times(leave, three_deep(rotated * scale))
        stage[at * out_rows:(at + 1) * out_rows, :] = result[:, :columns]
        stage[(at + 1) * out_rows:(at + 2) * out_rows, :] = result[:, columns:]
    high, low = halves(stage[...])
    stage[...] = times(high, back[0]) + times(low, back[0]) + times(high, back[1])
    for row in range(out_rows):
        value = stage[pl.ds(row, count, stride=out_rows), :].astype(jnp.bfloat16)
        at = row % rows_here * columns
        outs[row // rows_here][:, at:at + columns] = value


def condition_fast(pieces, basis, in_basis, corrections):
    slices = len(pieces)
    count, rows_here, columns = pieces[0].shape
    block = min(BLOCK, count)
    width = rows_here * columns
    piece_spec = pl.BlockSpec((block, rows_here, columns), lambda step: (step, 0, 0))
    out_spec = pl.BlockSpec((block, width), lambda step: (step, 0))
    whole = pl.BlockSpec(memory_space=pltpu.VMEM)
    order = basis.shape[0]
    return pl.pallas_call(
        functools.partial(condition_kernel, slices, rows_here),
        grid=(count // block,),
        in_specs=[piece_spec] * slices + [whole] * 5,
        out_specs=[out_spec] * slices,
        out_shape=[jax.ShapeDtypeStruct((count, width), jnp.bfloat16)] * slices,
        scratch_shapes=[pltpu.VMEM((block * order, columns), jnp.float32)],
        compiler_params=pltpu.CompilerParams(vmem_limit_bytes=32 * 1024 * 1024),
        cost_estimate=pl.CostEstimate(flops=0, bytes_accessed=0, transcendentals=0),
    )(*pieces, basis, basis.T, in_basis, in_basis.T, corrections)


def condition_plain(pieces, basis, in_basis, corrections):
    high = lax.Precision.HIGH
    count, rows_here, columns = pieces[0].shape
    values = jnp.concatenate(pieces, axis=1).astype(jnp.float32)
    inner = jnp.einsum("qbc,cd->qbd", values, in_basis, precision=high)
    rotated = jnp.einsum("ba,qbd->qad", basis, inner, precision=high)
    left = jnp.einsum("ba,qad->qbd", basis, rotated / (corrections + damping_term), precision=high)
    result = jnp.einsum("qbd,ed->qbe", left, in_basis, precision=high).astype(jnp.bfloat16)
    starts = range(0, basis.shape[0], rows_here)
    return [result[:, at:at + rows_here].reshape(count, rows_here * columns) for at in starts]


def crossed(value, axis, size, mask):
    return lax.ppermute(value, axis, [(at, at ^ mask) for at in range(size)])


def exchanged(blocks, slices):
    moved = {mask: crossed(blocks[mask], "proj", slices, mask) for mask in reversed(range(1, slices))}
    return [blocks[0]] + [moved[mask] for mask in range(1, slices)]


def after(value, *tokens):
    return lax.optimization_barrier((value, tokens))[0]


def spread_shares(near, shares):
    return jnp.concatenate([near] + [crossed(near, "dp", shares, mask) for mask in range(2, shares, 2)], axis=0)


def products(near, far, train_flat, shares):
    contract = (((1,), (1,)), ((), ()))
    values = []
    for block in (near, far):
        value = lax.dot_general(block, train_flat, contract, preferred_element_type=jnp.float32)
        values.append(value.astype(jnp.bfloat16).reshape(shares // 2, -1, train_flat.shape[0]))
    return [values[at % 2][at // 2] for at in range(shares)]


def turned(blocks, mask):
    bit = 1
    while bit < len(blocks):
        swap = mask // bit % 2 == 1
        blocks = [jnp.where(swap, blocks[at ^ bit], blocks[at]) for at in range(len(blocks))]
        bit *= 2
    return blocks


def body(queries, train_grads, out_basis, in_basis, corrections):
    slices = lax.axis_size("proj")
    shares = lax.axis_size("dp")
    here = lax.axis_index("proj")
    share = lax.axis_index("dp")
    count, rows_here, columns = queries.shape
    width = rows_here * columns
    owned = shares // slices
    train_count = train_grads.shape[0]
    train_flat = lax.optimization_barrier(train_grads.reshape(train_count, width))
    row_blocks = out_basis.reshape(slices, rows_here, -1)
    basis = jnp.concatenate(turned([row_blocks[at] for at in range(slices)], here), axis=0)
    condition = condition_fast if rows_here % 16 == 0 else condition_plain
    parts = [count * size // sum(CHUNKS) for size in CHUNKS]
    pieces, rows, results = [], [], []
    source = queries
    for chunk, part in enumerate(parts):
        first, each = sum(parts[:chunk]), part // slices
        raw = []
        for mask in range(slices):
            block = lax.dynamic_slice_in_dim(source, first + (here ^ mask) * each, each, 0)
            block, source = lax.optimization_barrier((block, source))
            raw.append(block)
        pieces.append(exchanged(raw, slices))
    for chunk in range(len(parts)):
        if chunk:
            pieces[chunk], train_flat = lax.optimization_barrier((pieces[chunk], train_flat))
        made = condition(pieces[chunk], basis, in_basis, corrections)
        rows.append(exchanged(made, slices))
    came = []
    half = slices // 2
    for chunk, part in enumerate(parts):
        each = part // slices
        groups = []
        for group in (rows[chunk][:half], rows[chunk][half:]):
            near = spread_shares(jnp.concatenate(group, axis=0), shares)
            near = after(near, *came[2:3])
            far = crossed(near, "dp", shares, 1)
            groups.append(products(near, far, train_flat, shares))
        values = [jnp.concatenate(pair, axis=0) for pair in zip(*groups)]
        values = [jnp.stack(values[at * owned:(at + 1) * owned]) for at in range(slices)]
        came = exchanged(turned(values, here ^ (share // owned)), slices)
        sums = [value.reshape(owned, slices, each, train_count) for value in came]
        total = [sum(sums[mask][:, at ^ mask].astype(jnp.float32) for mask in range(slices)) for at in range(slices)]
        total = jnp.stack(turned(total, here), axis=1)
        total = jnp.stack(turned([total[at] for at in range(owned)], share % owned))
        results.append(total.reshape(owned, part, train_count))
    return jnp.concatenate(results, axis=1).reshape(owned * count, train_count)


def solution(mesh):
    in_specs = (P(("groups", "dp"), "proj", None), P(("groups", "dp"), "proj", None), P(), P(), P())
    out_specs = P(("groups", "proj"), "dp")
    return jax.shard_map(body, mesh=mesh, in_specs=in_specs, out_specs=out_specs, check_vma=False)
```

```python
import functools
import jax
import jax.numpy as jnp
from jax import lax
from jax.experimental import pallas as pl
from jax.experimental.pallas import tpu as pltpu
from jax.sharding import PartitionSpec as P

damping_term = 0.05
CHUNKS = (8, 8)
BLOCK = 64


def halves(value):
    high = value.astype(jnp.bfloat16)
    return high, (value - high.astype(jnp.float32)).astype(jnp.bfloat16)


def times(left, right):
    return jnp.dot(left, right, preferred_element_type=jnp.float32)


def three_wide(matrix):
    high, low = halves(matrix)
    return jnp.concatenate([high, low, high], axis=1)


def three_deep(matrix):
    high, low = halves(matrix)
    return jnp.concatenate([high, high, low], axis=0)


def condition_kernel(slices, rows_here, *refs):
    pieces = refs[:slices]
    basis, across, right_basis, right_across, corrections = refs[slices:slices + 5]
    outs, stage = refs[slices + 5:-1], refs[-1]
    enter, leave = three_wide(across[...]), three_wide(basis[...])
    right, back = halves(right_basis[...]), halves(right_across[...])
    count, _, columns = pieces[0].shape
    out_rows = slices * rows_here
    parts = []
    for piece in pieces:
        flat = piece[...].reshape(count * rows_here, columns)
        parts.append(halves(times(flat, right[0]) + times(flat, right[1])))
    scale = jnp.concatenate([1.0 / (corrections[...] + damping_term)] * 2, axis=1)

    def gathered(at, which):
        rows = slice(at * rows_here, (at + 1) * rows_here)
        return jnp.concatenate([part[which][rows] for part in parts], axis=0)

    for at in range(0, count, 2):
        high = jnp.concatenate([gathered(at, 0), gathered(at + 1, 0)], axis=1)
        low = jnp.concatenate([gathered(at, 1), gathered(at + 1, 1)], axis=1)
        rotated = times(enter, jnp.concatenate([high, high, low], axis=0))
        result = times(leave, three_deep(rotated * scale))
        stage[at * out_rows:(at + 1) * out_rows, :] = result[:, :columns]
        stage[(at + 1) * out_rows:(at + 2) * out_rows, :] = result[:, columns:]
    high, low = halves(stage[...])
    stage[...] = times(high, back[0]) + times(low, back[0]) + times(high, back[1])
    for row in range(out_rows):
        value = stage[pl.ds(row, count, stride=out_rows), :].astype(jnp.bfloat16)
        at = row % rows_here * columns
        outs[row // rows_here][:, at:at + columns] = value


def condition_fast(pieces, basis, in_basis, corrections):
    slices = len(pieces)
    count, rows_here, columns = pieces[0].shape
    block = min(BLOCK, count)
    width = rows_here * columns
    piece_spec = pl.BlockSpec((block, rows_here, columns), lambda step: (step, 0, 0))
    out_spec = pl.BlockSpec((block, width), lambda step: (step, 0))
    whole = pl.BlockSpec(memory_space=pltpu.VMEM)
    order = basis.shape[0]
    return pl.pallas_call(
        functools.partial(condition_kernel, slices, rows_here),
        grid=(count // block,),
        in_specs=[piece_spec] * slices + [whole] * 5,
        out_specs=[out_spec] * slices,
        out_shape=[jax.ShapeDtypeStruct((count, width), jnp.bfloat16)] * slices,
        scratch_shapes=[pltpu.VMEM((block * order, columns), jnp.float32)],
        compiler_params=pltpu.CompilerParams(vmem_limit_bytes=32 * 1024 * 1024),
        cost_estimate=pl.CostEstimate(flops=0, bytes_accessed=0, transcendentals=0),
    )(*pieces, basis, basis.T, in_basis, in_basis.T, corrections)


def condition_plain(pieces, basis, in_basis, corrections):
    high = lax.Precision.HIGH
    count, rows_here, columns = pieces[0].shape
    values = jnp.concatenate(pieces, axis=1).astype(jnp.float32)
    inner = jnp.einsum("qbc,cd->qbd", values, in_basis, precision=high)
    rotated = jnp.einsum("ba,qbd->qad", basis, inner, precision=high)
    left = jnp.einsum("ba,qad->qbd", basis, rotated / (corrections + damping_term), precision=high)
    result = jnp.einsum("qbd,ed->qbe", left, in_basis, precision=high).astype(jnp.bfloat16)
    starts = range(0, basis.shape[0], rows_here)
    return [result[:, at:at + rows_here].reshape(count, rows_here * columns) for at in starts]


def crossed(value, axis, size, mask):
    return lax.ppermute(value, axis, [(at, at ^ mask) for at in range(size)])


def exchanged(blocks, slices):
    moved = {mask: crossed(blocks[mask], "proj", slices, mask) for mask in reversed(range(1, slices))}
    return [blocks[0]] + [moved[mask] for mask in range(1, slices)]


def after(value, *tokens):
    return lax.optimization_barrier((value, tokens))[0]


def spread_shares(near, shares):
    return jnp.concatenate([near] + [crossed(near, "dp", shares, mask) for mask in range(2, shares, 2)], axis=0)


def products(near, far, train_flat, shares):
    contract = (((1,), (1,)), ((), ()))
    values = []
    for block in (near, far):
        value = lax.dot_general(block, train_flat, contract, preferred_element_type=jnp.float32)
        values.append(value.astype(jnp.bfloat16).reshape(shares // 2, -1, train_flat.shape[0]))
    return [values[at % 2][at // 2] for at in range(shares)]


def turned(blocks, mask):
    bit = 1
    while bit < len(blocks):
        swap = mask // bit % 2 == 1
        blocks = [jnp.where(swap, blocks[at ^ bit], blocks[at]) for at in range(len(blocks))]
        bit *= 2
    return blocks


def body(queries, train_grads, out_basis, in_basis, corrections):
    slices = lax.axis_size("proj")
    shares = lax.axis_size("dp")
    here = lax.axis_index("proj")
    share = lax.axis_index("dp")
    count, rows_here, columns = queries.shape
    width = rows_here * columns
    owned = shares // slices
    train_count = train_grads.shape[0]
    train_flat = lax.optimization_barrier(train_grads.reshape(train_count, width))
    row_blocks = out_basis.reshape(slices, rows_here, -1)
    basis = jnp.concatenate(turned([row_blocks[at] for at in range(slices)], here), axis=0)
    condition = condition_fast if rows_here % 16 == 0 else condition_plain
    parts = [count * size // sum(CHUNKS) for size in CHUNKS]
    half = slices // 2
    pieces, rows, results = [], [], []
    source = queries
    for chunk, part in enumerate(parts):
        first, each = sum(parts[:chunk]), part // slices
        if chunk:
            source, pieces[0][1], train_flat = lax.optimization_barrier((source, pieces[0][1], train_flat))
        raw = []
        for mask in range(slices):
            block = lax.dynamic_slice_in_dim(source, first + (here ^ mask) * each, each, 0)
            block, source = lax.optimization_barrier((block, source))
            raw.append(block)
        pieces.append(exchanged(raw, slices))
    for chunk in range(len(parts)):
        made = condition(pieces[chunk], basis, in_basis, corrections)
        rows.append(exchanged(made, slices))
    rows[0][:half], made = lax.optimization_barrier((rows[0][:half], made))
    came = []
    for chunk, part in enumerate(parts):
        each = part // slices
        groups = []
        for group in (rows[chunk][:half], rows[chunk][half:]):
            near = spread_shares(jnp.concatenate(group, axis=0), shares)
            near = after(near, *came[2:3])
            far = crossed(near, "dp", shares, 1)
            groups.append(products(near, far, train_flat, shares))
        values = [jnp.concatenate(pair, axis=0) for pair in zip(*groups)]
        values = [jnp.stack(values[at * owned:(at + 1) * owned]) for at in range(slices)]
        came = exchanged(turned(values, here ^ (share // owned)), slices)
        sums = [value.reshape(owned, slices, each, train_count) for value in came]
        total = [sum(sums[mask][:, at ^ mask].astype(jnp.float32) for mask in range(slices)) for at in range(slices)]
        total = jnp.stack(turned(total, here), axis=1)
        total = jnp.stack(turned([total[at] for at in range(owned)], share % owned))
        results.append(total.reshape(owned, part, train_count))
    return jnp.concatenate(results, axis=1).reshape(owned * count, train_count)


def solution(mesh):
    in_specs = (P(("groups", "dp"), "proj", None), P(("groups", "dp"), "proj", None), P(), P(), P())
    out_specs = P(("groups", "proj"), "dp")
    return jax.shard_map(body, mesh=mesh, in_specs=in_specs, out_specs=out_specs, check_vma=False)
```

```python
import functools
import jax
import jax.numpy as jnp
from jax import lax
from jax.experimental import pallas as pl
from jax.experimental.pallas import tpu as pltpu
from jax.sharding import PartitionSpec as P

damping_term = 0.05
CHUNKS = (8, 8)
BLOCK = 64


def halves(value):
    high = value.astype(jnp.bfloat16)
    return high, (value - high.astype(jnp.float32)).astype(jnp.bfloat16)


def times(left, right):
    return jnp.dot(left, right, preferred_element_type=jnp.float32)


def three_wide(matrix):
    high, low = halves(matrix)
    return jnp.concatenate([high, low, high], axis=1)


def three_deep(matrix):
    high, low = halves(matrix)
    return jnp.concatenate([high, high, low], axis=0)


def condition_kernel(slices, rows_here, *refs):
    pieces = refs[:slices][::-1]
    basis, across, right_basis, right_across, corrections = refs[slices:slices + 5]
    outs, stage = refs[slices + 5:-1], refs[-1]
    enter, leave = three_wide(across[...]), three_wide(basis[...])
    right, back = halves(right_basis[...]), halves(right_across[...])
    count, _, columns = pieces[0].shape
    out_rows = slices * rows_here
    parts = []
    for piece in pieces:
        flat = piece[...].reshape(count * rows_here, columns)
        parts.append(halves(times(flat, right[0]) + times(flat, right[1])))
    scale = jnp.concatenate([1.0 / (corrections[...] + damping_term)] * 2, axis=1)

    def gathered(at, which):
        rows = slice(at * rows_here, (at + 1) * rows_here)
        return jnp.concatenate([part[which][rows] for part in parts], axis=0)

    for at in range(0, count, 2):
        high = jnp.concatenate([gathered(at, 0), gathered(at + 1, 0)], axis=1)
        low = jnp.concatenate([gathered(at, 1), gathered(at + 1, 1)], axis=1)
        rotated = times(enter, jnp.concatenate([high, high, low], axis=0))
        result = times(leave, three_deep(rotated * scale))
        stage[at * out_rows:(at + 1) * out_rows, :] = result[:, :columns]
        stage[(at + 1) * out_rows:(at + 2) * out_rows, :] = result[:, columns:]
    high, low = halves(stage[...])
    stage[...] = times(high, back[0]) + times(low, back[0]) + times(high, back[1])
    for row in range(out_rows):
        value = stage[pl.ds(row, count, stride=out_rows), :].astype(jnp.bfloat16)
        at = row % rows_here * columns
        outs[row // rows_here][:, at:at + columns] = value


def condition_fast(pieces, basis, in_basis, corrections):
    slices = len(pieces)
    count, rows_here, columns = pieces[0].shape
    block = min(BLOCK, count)
    width = rows_here * columns
    piece_spec = pl.BlockSpec((block, rows_here, columns), lambda step: (step, 0, 0))
    out_spec = pl.BlockSpec((block, width), lambda step: (step, 0))
    whole = pl.BlockSpec(memory_space=pltpu.VMEM)
    order = basis.shape[0]
    return pl.pallas_call(
        functools.partial(condition_kernel, slices, rows_here),
        grid=(count // block,),
        in_specs=[piece_spec] * slices + [whole] * 5,
        out_specs=[out_spec] * slices,
        out_shape=[jax.ShapeDtypeStruct((count, width), jnp.bfloat16)] * slices,
        scratch_shapes=[pltpu.VMEM((block * order, columns), jnp.float32)],
        compiler_params=pltpu.CompilerParams(vmem_limit_bytes=32 * 1024 * 1024),
        cost_estimate=pl.CostEstimate(flops=0, bytes_accessed=0, transcendentals=0),
    )(*pieces[::-1], basis, basis.T, in_basis, in_basis.T, corrections)


def condition_plain(pieces, basis, in_basis, corrections):
    high = lax.Precision.HIGH
    count, rows_here, columns = pieces[0].shape
    values = jnp.concatenate(pieces, axis=1).astype(jnp.float32)
    inner = jnp.einsum("qbc,cd->qbd", values, in_basis, precision=high)
    rotated = jnp.einsum("ba,qbd->qad", basis, inner, precision=high)
    left = jnp.einsum("ba,qad->qbd", basis, rotated / (corrections + damping_term), precision=high)
    result = jnp.einsum("qbd,ed->qbe", left, in_basis, precision=high).astype(jnp.bfloat16)
    starts = range(0, basis.shape[0], rows_here)
    return [result[:, at:at + rows_here].reshape(count, rows_here * columns) for at in starts]


def crossed(value, axis, size, mask):
    return lax.ppermute(value, axis, [(at, at ^ mask) for at in range(size)])


def exchanged(blocks, slices):
    moved = {mask: crossed(blocks[mask], "proj", slices, mask) for mask in reversed(range(1, slices))}
    return [blocks[0]] + [moved[mask] for mask in range(1, slices)]


def after(value, *tokens):
    return lax.optimization_barrier((value, tokens))[0]


def spread_shares(near, shares, tokens):
    parts = [near] + [crossed(near, "dp", shares, mask) for mask in range(2, shares, 2)]
    return lax.optimization_barrier(jnp.concatenate(after(parts, *tokens), axis=0))


def products(near, far, train_flat, shares):
    contract = (((1,), (1,)), ((), ()))
    values = []
    for block in (near, far):
        value = lax.dot_general(block, train_flat, contract, preferred_element_type=jnp.float32)
        values.append(value.astype(jnp.bfloat16).reshape(shares // 2, -1, train_flat.shape[0]))
    return [values[at % 2][at // 2] for at in range(shares)]


def turned(blocks, mask):
    bit = 1
    while bit < len(blocks):
        swap = mask // bit % 2 == 1
        blocks = [jnp.where(swap, blocks[at ^ bit], blocks[at]) for at in range(len(blocks))]
        bit *= 2
    return blocks


def body(queries, train_grads, out_basis, in_basis, corrections):
    slices = lax.axis_size("proj")
    shares = lax.axis_size("dp")
    here = lax.axis_index("proj")
    share = lax.axis_index("dp")
    count, rows_here, columns = queries.shape
    width = rows_here * columns
    owned = shares // slices
    train_count = train_grads.shape[0]
    train_flat = lax.optimization_barrier(train_grads.reshape(train_count, width))
    row_blocks = out_basis.reshape(slices, rows_here, -1)
    basis = jnp.concatenate(turned([row_blocks[at] for at in range(slices)], here), axis=0)
    condition = condition_fast if rows_here % 16 == 0 else condition_plain
    parts = [count * size // sum(CHUNKS) for size in CHUNKS]
    half = slices // 2
    pieces, rows, results = [], [], []
    source = queries
    for chunk, part in enumerate(parts):
        first, each = sum(parts[:chunk]), part // slices
        if chunk:
            source, pieces[0][-1], train_flat = lax.optimization_barrier((source, pieces[0][-1], train_flat))
        raw = {}
        for mask in (reversed(range(slices)) if chunk else range(slices)):
            block = lax.dynamic_slice_in_dim(source, first + (here ^ mask) * each, each, 0)
            raw[mask], source = lax.optimization_barrier((block, source))
        pieces.append(exchanged(raw, slices))
    for chunk in range(len(parts)):
        made = condition(pieces[chunk], basis, in_basis, corrections)
        rows.append(exchanged(made, slices))
    rows[0][:half], made = lax.optimization_barrier((rows[0][:half], made))
    came = []
    for chunk, part in enumerate(parts):
        each = part // slices
        groups = []
        for group in (rows[chunk][:half], rows[chunk][half:]):
            if chunk and groups:
                group = after(group, near_before)
            near = spread_shares(jnp.concatenate(group, axis=0), shares, came[2:3])
            far = crossed(near, "dp", shares, 1)
            groups.append(products(near, far, train_flat, shares))
        near_before = near
        values = [jnp.concatenate(pair, axis=0) for pair in zip(*groups)]
        values = [jnp.stack(values[at * owned:(at + 1) * owned]) for at in range(slices)]
        came = exchanged(turned(values, here ^ (share // owned)), slices)
        sums = [value.reshape(owned, slices, each, train_count) for value in came]
        total = [sum(sums[mask][:, at ^ mask].astype(jnp.float32) for mask in range(slices)) for at in range(slices)]
        total = jnp.stack(turned(total, here), axis=1)
        total = jnp.stack(turned([total[at] for at in range(owned)], share % owned))
        results.append(total.reshape(owned, part, train_count))
    return jnp.concatenate(results, axis=1).reshape(owned * count, train_count)


def solution(mesh):
    in_specs = (P(("groups", "dp"), "proj", None), P(("groups", "dp"), "proj", None), P(), P(), P())
    out_specs = P(("groups", "proj"), "dp")
    return jax.shard_map(body, mesh=mesh, in_specs=in_specs, out_specs=out_specs, check_vma=False)
```

```python
import functools
import jax
import jax.numpy as jnp
from jax import lax
from jax.experimental import pallas as pl
from jax.experimental.pallas import tpu as pltpu
from jax.sharding import PartitionSpec as P

damping_term = 0.05
CHUNKS = (8, 8)
BLOCK = 64


def halves(value):
    high = value.astype(jnp.bfloat16)
    return high, (value - high.astype(jnp.float32)).astype(jnp.bfloat16)


def times(left, right):
    return jnp.dot(left, right, preferred_element_type=jnp.float32)


def three_wide(matrix):
    high, low = halves(matrix)
    return jnp.concatenate([high, low, high], axis=1)


def three_deep(matrix):
    high, low = halves(matrix)
    return jnp.concatenate([high, high, low], axis=0)


def condition_kernel(slices, rows_here, *refs):
    pieces = refs[:slices][::-1]
    basis, across, right_basis, right_across, corrections = refs[slices:slices + 5]
    outs, stage = refs[slices + 5:-1], refs[-1]
    enter, leave = three_wide(across[...]), three_wide(basis[...])
    right, back = halves(right_basis[...]), halves(right_across[...])
    count, _, columns = pieces[0].shape
    out_rows = slices * rows_here
    parts = []
    for piece in pieces:
        flat = piece[...].reshape(count * rows_here, columns)
        parts.append(halves(times(flat, right[0]) + times(flat, right[1])))
    scale = jnp.concatenate([1.0 / (corrections[...] + damping_term)] * 2, axis=1)

    def gathered(at, which):
        rows = slice(at * rows_here, (at + 1) * rows_here)
        return jnp.concatenate([part[which][rows] for part in parts], axis=0)

    for at in range(0, count, 2):
        high = jnp.concatenate([gathered(at, 0), gathered(at + 1, 0)], axis=1)
        low = jnp.concatenate([gathered(at, 1), gathered(at + 1, 1)], axis=1)
        rotated = times(enter, jnp.concatenate([high, high, low], axis=0))
        result = times(leave, three_deep(rotated * scale))
        stage[at * out_rows:(at + 1) * out_rows, :] = result[:, :columns]
        stage[(at + 1) * out_rows:(at + 2) * out_rows, :] = result[:, columns:]
    high, low = halves(stage[...])
    stage[...] = times(high, back[0]) + times(low, back[0]) + times(high, back[1])
    for row in range(out_rows):
        value = stage[pl.ds(row, count, stride=out_rows), :].astype(jnp.bfloat16)
        at = row % rows_here * columns
        outs[row // rows_here][:, at:at + columns] = value


def condition_fast(pieces, basis, in_basis, corrections):
    slices = len(pieces)
    count, rows_here, columns = pieces[0].shape
    block = min(BLOCK, count)
    width = rows_here * columns
    piece_spec = pl.BlockSpec((block, rows_here, columns), lambda step: (step, 0, 0))
    out_spec = pl.BlockSpec((block, width), lambda step: (step, 0))
    whole = pl.BlockSpec(memory_space=pltpu.VMEM)
    order = basis.shape[0]
    return pl.pallas_call(
        functools.partial(condition_kernel, slices, rows_here),
        grid=(count // block,),
        in_specs=[piece_spec] * slices + [whole] * 5,
        out_specs=[out_spec] * slices,
        out_shape=[jax.ShapeDtypeStruct((count, width), jnp.bfloat16)] * slices,
        scratch_shapes=[pltpu.VMEM((block * order, columns), jnp.float32)],
        compiler_params=pltpu.CompilerParams(vmem_limit_bytes=32 * 1024 * 1024),
        cost_estimate=pl.CostEstimate(flops=0, bytes_accessed=0, transcendentals=0),
    )(*pieces[::-1], basis, basis.T, in_basis, in_basis.T, corrections)


def condition_plain(pieces, basis, in_basis, corrections):
    high = lax.Precision.HIGH
    count, rows_here, columns = pieces[0].shape
    values = jnp.concatenate(pieces, axis=1).astype(jnp.float32)
    inner = jnp.einsum("qbc,cd->qbd", values, in_basis, precision=high)
    rotated = jnp.einsum("ba,qbd->qad", basis, inner, precision=high)
    left = jnp.einsum("ba,qad->qbd", basis, rotated / (corrections + damping_term), precision=high)
    result = jnp.einsum("qbd,ed->qbe", left, in_basis, precision=high).astype(jnp.bfloat16)
    starts = range(0, basis.shape[0], rows_here)
    return [result[:, at:at + rows_here].reshape(count, rows_here * columns) for at in starts]


def crossed(value, axis, size, mask):
    return lax.ppermute(value, axis, [(at, at ^ mask) for at in range(size)])


def exchanged(blocks, slices):
    moved = {mask: crossed(blocks[mask], "proj", slices, mask) for mask in reversed(range(1, slices))}
    return [blocks[0]] + [moved[mask] for mask in range(1, slices)]


def after(value, *tokens):
    return lax.optimization_barrier((value, tokens))[0]


def over_shares(rows, shares):
    near = jnp.concatenate(rows, axis=0)
    return [near] + [crossed(near, "dp", shares, mask) for mask in range(2, shares, 2)]


def products(near, far, train_flat, shares):
    contract = (((1,), (1,)), ((), ()))
    values = []
    for block in (near, far):
        value = lax.dot_general(block, train_flat, contract, preferred_element_type=jnp.float32)
        values.append(value.astype(jnp.bfloat16).reshape(shares // 2, -1, train_flat.shape[0]))
    return [values[at % 2][at // 2] for at in range(shares)]


def turned(blocks, mask):
    bit = 1
    while bit < len(blocks):
        swap = mask // bit % 2 == 1
        blocks = [jnp.where(swap, blocks[at ^ bit], blocks[at]) for at in range(len(blocks))]
        bit *= 2
    return blocks


def body(queries, train_grads, out_basis, in_basis, corrections):
    slices = lax.axis_size("proj")
    shares = lax.axis_size("dp")
    here = lax.axis_index("proj")
    share = lax.axis_index("dp")
    count, rows_here, columns = queries.shape
    width = rows_here * columns
    owned = shares // slices
    train_count = train_grads.shape[0]
    train_flat = lax.optimization_barrier(train_grads.reshape(train_count, width))
    row_blocks = out_basis.reshape(slices, rows_here, -1)
    basis = jnp.concatenate(turned([row_blocks[at] for at in range(slices)], here), axis=0)
    condition = condition_fast if rows_here % 16 == 0 else condition_plain
    parts = [count * size // sum(CHUNKS) for size in CHUNKS]
    half = slices // 2
    pieces, rows, results = [], [], []
    source = queries
    for chunk, part in enumerate(parts):
        first, each = sum(parts[:chunk]), part // slices
        if chunk:
            source, pieces[0][-1], train_flat = lax.optimization_barrier((source, pieces[0][-1], train_flat))
        raw = {}
        for mask in (reversed(range(slices)) if chunk else range(slices)):
            block = lax.dynamic_slice_in_dim(source, first + (here ^ mask) * each, each, 0)
            raw[mask], source = lax.optimization_barrier((block, source))
        pieces.append(exchanged(raw, slices))
    made = condition(pieces[0], basis, in_basis, corrections)
    rows.append(exchanged(made, slices))
    rows[0][:half], pieces[1] = lax.optimization_barrier((rows[0][:half], pieces[1]))
    spread = over_shares(rows[0][:half], shares)
    made = condition(pieces[1], basis, in_basis, corrections)
    rows.append(exchanged(made, slices))
    rows[1][:half], spread = lax.optimization_barrier((rows[1][:half], spread))
    came = []
    for chunk, part in enumerate(parts):
        each = part // slices
        groups = []
        for group in (rows[chunk][:half], rows[chunk][half:]):
            if chunk and groups:
                group = after(group, near_before)
            if chunk or groups:
                spread = over_shares(group, shares)
            near = lax.optimization_barrier(jnp.concatenate(after(spread, *came[2:3]), axis=0))
            far = crossed(near, "dp", shares, 1)
            groups.append(products(near, far, train_flat, shares))
        near_before = near
        values = [jnp.concatenate(pair, axis=0) for pair in zip(*groups)]
        values = [jnp.stack(values[at * owned:(at + 1) * owned]) for at in range(slices)]
        came = exchanged(turned(values, here ^ (share // owned)), slices)
        sums = [value.reshape(owned, slices, each, train_count) for value in came]
        total = [sum(sums[mask][:, at ^ mask].astype(jnp.float32) for mask in range(slices)) for at in range(slices)]
        total = jnp.stack(turned(total, here), axis=1)
        total = jnp.stack(turned([total[at] for at in range(owned)], share % owned))
        results.append(total.reshape(owned, part, train_count))
    return jnp.concatenate(results, axis=1).reshape(owned * count, train_count)


def solution(mesh):
    in_specs = (P(("groups", "dp"), "proj", None), P(("groups", "dp"), "proj", None), P(), P(), P())
    out_specs = P(("groups", "proj"), "dp")
    return jax.shard_map(body, mesh=mesh, in_specs=in_specs, out_specs=out_specs, check_vma=False)
```

```python
import functools
import jax
import jax.numpy as jnp
from jax import lax
from jax.experimental import pallas as pl
from jax.experimental.pallas import tpu as pltpu
from jax.sharding import PartitionSpec as P

damping_term = 0.05
CHUNKS = (8, 8)
BLOCK = 64


def halves(value):
    high = value.astype(jnp.bfloat16)
    return high, (value - high.astype(jnp.float32)).astype(jnp.bfloat16)


def times(left, right):
    return jnp.dot(left, right, preferred_element_type=jnp.float32)


def three_wide(matrix):
    high, low = halves(matrix)
    return jnp.concatenate([high, low, high], axis=1)


def three_deep(matrix):
    high, low = halves(matrix)
    return jnp.concatenate([high, high, low], axis=0)


def condition_kernel(slices, rows_here, *refs):
    pieces = refs[:slices][::-1]
    basis, across, right_basis, right_across, corrections = refs[slices:slices + 5]
    outs, stage = refs[slices + 5:-1], refs[-1]
    enter, leave = three_wide(across[...]), three_wide(basis[...])
    right, back = halves(right_basis[...]), halves(right_across[...])
    count, _, columns = pieces[0].shape
    out_rows = slices * rows_here
    parts = []
    for piece in pieces:
        flat = piece[...].reshape(count * rows_here, columns)
        parts.append(halves(times(flat, right[0]) + times(flat, right[1])))
    scale = jnp.concatenate([1.0 / (corrections[...] + damping_term)] * 2, axis=1)

    def gathered(at, which):
        rows = slice(at * rows_here, (at + 1) * rows_here)
        return jnp.concatenate([part[which][rows] for part in parts], axis=0)

    for at in range(0, count, 2):
        high = jnp.concatenate([gathered(at, 0), gathered(at + 1, 0)], axis=1)
        low = jnp.concatenate([gathered(at, 1), gathered(at + 1, 1)], axis=1)
        rotated = times(enter, jnp.concatenate([high, high, low], axis=0))
        result = times(leave, three_deep(rotated * scale))
        stage[at * out_rows:(at + 1) * out_rows, :] = result[:, :columns]
        stage[(at + 1) * out_rows:(at + 2) * out_rows, :] = result[:, columns:]
    high, low = halves(stage[...])
    stage[...] = times(high, back[0]) + times(low, back[0]) + times(high, back[1])
    for row in range(out_rows):
        value = stage[pl.ds(row, count, stride=out_rows), :].astype(jnp.bfloat16)
        at = row % rows_here * columns
        outs[row // rows_here][:, at:at + columns] = value


def condition_fast(pieces, basis, in_basis, corrections):
    slices = len(pieces)
    count, rows_here, columns = pieces[0].shape
    block = min(BLOCK, count)
    width = rows_here * columns
    piece_spec = pl.BlockSpec((block, rows_here, columns), lambda step: (step, 0, 0))
    out_spec = pl.BlockSpec((block, width), lambda step: (step, 0))
    whole = pl.BlockSpec(memory_space=pltpu.VMEM)
    order = basis.shape[0]
    return pl.pallas_call(
        functools.partial(condition_kernel, slices, rows_here),
        grid=(count // block,),
        in_specs=[piece_spec] * slices + [whole] * 5,
        out_specs=[out_spec] * slices,
        out_shape=[jax.ShapeDtypeStruct((count, width), jnp.bfloat16)] * slices,
        scratch_shapes=[pltpu.VMEM((block * order, columns), jnp.float32)],
        compiler_params=pltpu.CompilerParams(vmem_limit_bytes=32 * 1024 * 1024),
        cost_estimate=pl.CostEstimate(flops=0, bytes_accessed=0, transcendentals=0),
    )(*pieces[::-1], basis, basis.T, in_basis, in_basis.T, corrections)


def condition_plain(pieces, basis, in_basis, corrections):
    high = lax.Precision.HIGH
    count, rows_here, columns = pieces[0].shape
    values = jnp.concatenate(pieces, axis=1).astype(jnp.float32)
    inner = jnp.einsum("qbc,cd->qbd", values, in_basis, precision=high)
    rotated = jnp.einsum("ba,qbd->qad", basis, inner, precision=high)
    left = jnp.einsum("ba,qad->qbd", basis, rotated / (corrections + damping_term), precision=high)
    result = jnp.einsum("qbd,ed->qbe", left, in_basis, precision=high).astype(jnp.bfloat16)
    starts = range(0, basis.shape[0], rows_here)
    return [result[:, at:at + rows_here].reshape(count, rows_here * columns) for at in starts]


def crossed(value, axis, size, mask):
    return lax.ppermute(value, axis, [(at, at ^ mask) for at in range(size)])


def exchanged(blocks, slices):
    moved = {mask: crossed(blocks[mask], "proj", slices, mask) for mask in reversed(range(1, slices))}
    return [blocks[0]] + [moved[mask] for mask in range(1, slices)]


def in_turn(blocks):
    done = []
    for block in reversed(blocks):
        done.append(after(block, *done[-1:]))
    return done[::-1]


def after(value, *tokens):
    return lax.optimization_barrier((value, tokens))[0]


def over_shares(rows, shares):
    near = jnp.concatenate(rows, axis=0)
    return [near] + [crossed(near, "dp", shares, mask) for mask in range(2, shares, 2)]


def products(near, far, train_flat, shares):
    contract = (((1,), (1,)), ((), ()))
    values = []
    for block in (near, far):
        value = lax.dot_general(block, train_flat, contract, preferred_element_type=jnp.float32)
        values.append(value.astype(jnp.bfloat16).reshape(shares // 2, -1, train_flat.shape[0]))
    return [values[at % 2][at // 2] for at in range(shares)]


def turned(blocks, mask):
    bit = 1
    while bit < len(blocks):
        swap = mask // bit % 2 == 1
        blocks = [jnp.where(swap, blocks[at ^ bit], blocks[at]) for at in range(len(blocks))]
        bit *= 2
    return blocks


def body(queries, train_grads, out_basis, in_basis, corrections):
    slices = lax.axis_size("proj")
    shares = lax.axis_size("dp")
    here = lax.axis_index("proj")
    share = lax.axis_index("dp")
    count, rows_here, columns = queries.shape
    width = rows_here * columns
    owned = shares // slices
    train_count = train_grads.shape[0]
    train_flat = lax.optimization_barrier(train_grads.reshape(train_count, width))
    row_blocks = out_basis.reshape(slices, rows_here, -1)
    basis = jnp.concatenate(turned([row_blocks[at] for at in range(slices)], here), axis=0)
    condition = condition_fast if rows_here % 16 == 0 else condition_plain
    parts = [count * size // sum(CHUNKS) for size in CHUNKS]
    half = slices // 2
    pieces, rows, results = [], [], []
    source = queries
    for chunk, part in enumerate(parts):
        first, each = sum(parts[:chunk]), part // slices
        if chunk:
            source, pieces[0][-1], train_flat = lax.optimization_barrier((source, pieces[0][-1], train_flat))
        raw = {}
        for mask in (reversed(range(slices)) if chunk else range(slices)):
            block = lax.dynamic_slice_in_dim(source, first + (here ^ mask) * each, each, 0)
            raw[mask], source = lax.optimization_barrier((block, source))
        pieces.append(exchanged(raw, slices))
    made = condition(pieces[0], basis, in_basis, corrections)
    rows.append(exchanged(made, slices))
    rows[0][:half], pieces[1] = lax.optimization_barrier((rows[0][:half], pieces[1]))
    spread = over_shares(rows[0][:half], shares)
    made = condition(pieces[1], basis, in_basis, corrections)
    rows.append(exchanged(made, slices))
    rows[1][:half], spread = lax.optimization_barrier((rows[1][:half], spread))
    near_rows, far_rows = list(range(half)), list(range(half, slices))
    orders = [(near_rows, far_rows)] * 2
    came = []
    for chunk, part in enumerate(parts):
        each = part // slices
        groups = []
        order = sum(orders[chunk], [])
        for members in orders[chunk]:
            group = [rows[chunk][at] for at in members]
            if chunk and groups:
                group = after(group, near_before)
            if chunk or groups:
                spread = over_shares(group, shares)
            near = lax.optimization_barrier(jnp.concatenate(after(spread, *(came[2:3] if groups else came[:1])), axis=0))
            far = crossed(near, "dp", shares, 1)
            groups.append(products(near, far, train_flat, shares))
        near_before = near
        values = [jnp.concatenate(pair, axis=0) for pair in zip(*groups)]
        values = [jnp.stack(values[at * owned:(at + 1) * owned]) for at in range(slices)]
        came = exchanged(in_turn(turned(values, here ^ (share // owned))), slices)
        sums = [value.reshape(owned, slices, each, train_count) for value in came]
        total = [
            sum(sums[mask][:, order.index(at ^ mask)].astype(jnp.float32) for mask in range(slices))
            for at in range(slices)
        ]
        total = jnp.stack(turned(total, here), axis=1)
        total = jnp.stack(turned([total[at] for at in range(owned)], share % owned))
        results.append(total.reshape(owned, part, train_count))
    return jnp.concatenate(results, axis=1).reshape(owned * count, train_count)


def solution(mesh):
    in_specs = (P(("groups", "dp"), "proj", None), P(("groups", "dp"), "proj", None), P(), P(), P())
    out_specs = P(("groups", "proj"), "dp")
    return jax.shard_map(body, mesh=mesh, in_specs=in_specs, out_specs=out_specs, check_vma=False)
```

```python
import functools
import jax
import jax.numpy as jnp
from jax import lax
from jax.experimental import pallas as pl
from jax.experimental.pallas import tpu as pltpu
from jax.sharding import PartitionSpec as P

damping_term = 0.05
CHUNKS = (8, 8)
BLOCK = 64


def halves(value):
    high = value.astype(jnp.bfloat16)
    return high, (value - high.astype(jnp.float32)).astype(jnp.bfloat16)


def times(left, right):
    return jnp.dot(left, right, preferred_element_type=jnp.float32)


def three_wide(matrix):
    high, low = halves(matrix)
    return jnp.concatenate([high, low, high], axis=1)


def three_deep(matrix):
    high, low = halves(matrix)
    return jnp.concatenate([high, high, low], axis=0)


def condition_kernel(slices, rows_here, *refs):
    pieces = refs[:slices][::-1]
    basis, across, right_basis, right_across, corrections = refs[slices:slices + 5]
    outs, stage = refs[slices + 5:-1], refs[-1]
    enter, leave = three_wide(across[...]), three_wide(basis[...])
    right, back = halves(right_basis[...]), halves(right_across[...])
    count, _, columns = pieces[0].shape
    out_rows = slices * rows_here
    parts = []
    for piece in pieces:
        flat = piece[...].reshape(count * rows_here, columns)
        parts.append(halves(times(flat, right[0]) + times(flat, right[1])))
    scale = jnp.concatenate([1.0 / (corrections[...] + damping_term)] * 2, axis=1)

    def gathered(at, which):
        rows = slice(at * rows_here, (at + 1) * rows_here)
        return jnp.concatenate([part[which][rows] for part in parts], axis=0)

    for at in range(0, count, 2):
        high = jnp.concatenate([gathered(at, 0), gathered(at + 1, 0)], axis=1)
        low = jnp.concatenate([gathered(at, 1), gathered(at + 1, 1)], axis=1)
        rotated = times(enter, jnp.concatenate([high, high, low], axis=0))
        result = times(leave, three_deep(rotated * scale))
        stage[at * out_rows:(at + 1) * out_rows, :] = result[:, :columns]
        stage[(at + 1) * out_rows:(at + 2) * out_rows, :] = result[:, columns:]
    high, low = halves(stage[...])
    stage[...] = times(high, back[0]) + times(low, back[0]) + times(high, back[1])
    for row in range(out_rows):
        value = stage[pl.ds(row, count, stride=out_rows), :].astype(jnp.bfloat16)
        at = row % rows_here * columns
        outs[row // rows_here][:, at:at + columns] = value


def condition_fast(pieces, basis, in_basis, corrections):
    slices = len(pieces)
    count, rows_here, columns = pieces[0].shape
    block = min(BLOCK, count)
    width = rows_here * columns
    piece_spec = pl.BlockSpec((block, rows_here, columns), lambda step: (step, 0, 0))
    out_spec = pl.BlockSpec((block, width), lambda step: (step, 0))
    whole = pl.BlockSpec(memory_space=pltpu.VMEM)
    order = basis.shape[0]
    return pl.pallas_call(
        functools.partial(condition_kernel, slices, rows_here),
        grid=(count // block,),
        in_specs=[piece_spec] * slices + [whole] * 5,
        out_specs=[out_spec] * slices,
        out_shape=[jax.ShapeDtypeStruct((count, width), jnp.bfloat16)] * slices,
        scratch_shapes=[pltpu.VMEM((block * order, columns), jnp.float32)],
        compiler_params=pltpu.CompilerParams(vmem_limit_bytes=32 * 1024 * 1024),
        cost_estimate=pl.CostEstimate(flops=0, bytes_accessed=0, transcendentals=0),
    )(*pieces[::-1], basis, basis.T, in_basis, in_basis.T, corrections)


def condition_plain(pieces, basis, in_basis, corrections):
    high = lax.Precision.HIGH
    count, rows_here, columns = pieces[0].shape
    values = jnp.concatenate(pieces, axis=1).astype(jnp.float32)
    inner = jnp.einsum("qbc,cd->qbd", values, in_basis, precision=high)
    rotated = jnp.einsum("ba,qbd->qad", basis, inner, precision=high)
    left = jnp.einsum("ba,qad->qbd", basis, rotated / (corrections + damping_term), precision=high)
    result = jnp.einsum("qbd,ed->qbe", left, in_basis, precision=high).astype(jnp.bfloat16)
    starts = range(0, basis.shape[0], rows_here)
    return [result[:, at:at + rows_here].reshape(count, rows_here * columns) for at in starts]


def crossed(value, axis, size, mask):
    return lax.ppermute(value, axis, [(at, at ^ mask) for at in range(size)])


def exchanged(blocks, slices):
    moved = {mask: crossed(blocks[mask], "proj", slices, mask) for mask in reversed(range(1, slices))}
    return [blocks[0]] + [moved[mask] for mask in range(1, slices)]


def in_turn(blocks):
    done = []
    for block in reversed(blocks):
        done.append(after(block, *done[-1:]))
    return done[::-1]


def after(value, *tokens):
    return lax.optimization_barrier((value, tokens))[0]


def over_shares(rows, shares):
    near = jnp.concatenate(rows, axis=0)
    return [near] + [crossed(near, "dp", shares, mask) for mask in range(2, shares, 2)]


def products(near, far, train_flat, shares):
    contract = (((1,), (1,)), ((), ()))
    values = []
    for block in (near, far):
        value = lax.dot_general(block, train_flat, contract, preferred_element_type=jnp.float32)
        values.append(value.astype(jnp.bfloat16).reshape(shares // 2, -1, train_flat.shape[0]))
    return [values[at % 2][at // 2] for at in range(shares)]


def turned(blocks, mask):
    bit = 1
    while bit < len(blocks):
        swap = mask // bit % 2 == 1
        blocks = [jnp.where(swap, blocks[at ^ bit], blocks[at]) for at in range(len(blocks))]
        bit *= 2
    return blocks


def body(queries, train_grads, out_basis, in_basis, corrections):
    slices = lax.axis_size("proj")
    shares = lax.axis_size("dp")
    here = lax.axis_index("proj")
    share = lax.axis_index("dp")
    count, rows_here, columns = queries.shape
    width = rows_here * columns
    owned = shares // slices
    train_count = train_grads.shape[0]
    train_flat = lax.optimization_barrier(train_grads.reshape(train_count, width))
    row_blocks = out_basis.reshape(slices, rows_here, -1)
    basis = jnp.concatenate(turned([row_blocks[at] for at in range(slices)], here), axis=0)
    condition = condition_fast if rows_here % 16 == 0 else condition_plain
    parts = [count * size // sum(CHUNKS) for size in CHUNKS]
    half = slices // 2
    pieces, rows, results = [], [], []
    source = queries
    for chunk, part in enumerate(parts):
        first, each = sum(parts[:chunk]), part // slices
        if chunk:
            source, pieces[0][-1], train_flat = lax.optimization_barrier((source, pieces[0][-1], train_flat))
        raw = {}
        for mask in (reversed(range(slices)) if chunk else range(slices)):
            block = lax.dynamic_slice_in_dim(source, first + (here ^ mask) * each, each, 0)
            raw[mask], source = lax.optimization_barrier((block, source))
        pieces.append(exchanged(raw, slices))
    made = condition(pieces[0], basis, in_basis, corrections)
    rows.append(exchanged(made, slices))
    rows[0][:half], pieces[1] = lax.optimization_barrier((rows[0][:half], pieces[1]))
    spread = over_shares(rows[0][:half], shares)
    made = condition(pieces[1], basis, in_basis, corrections)
    rows.append(exchanged(made, slices))
    rows[1][:half], spread = lax.optimization_barrier((rows[1][:half], spread))
    near_rows, far_rows = list(range(half)), list(range(half, slices))
    orders = [(near_rows, far_rows)] * 2
    came = []
    for chunk, part in enumerate(parts):
        each = part // slices
        groups = []
        order = sum(orders[chunk], [])
        for members in orders[chunk]:
            group = [rows[chunk][at] for at in members]
            if chunk and groups:
                group = after(group, near_before)
            if chunk or groups:
                spread = over_shares(group, shares)
            near = lax.optimization_barrier(jnp.concatenate(after(spread, *came[:1]), axis=0))
            far = crossed(near, "dp", shares, 1)
            groups.append(products(near, far, train_flat, shares))
        near_before = near
        values = [jnp.concatenate(pair, axis=0) for pair in zip(*groups)]
        values = [jnp.stack(values[at * owned:(at + 1) * owned]) for at in range(slices)]
        came = exchanged(in_turn(turned(values, here ^ (share // owned))), slices)
        sums = [value.reshape(owned, slices, each, train_count) for value in came]
        total = [
            sum(sums[mask][:, order.index(at ^ mask)].astype(jnp.float32) for mask in range(slices))
            for at in range(slices)
        ]
        total = jnp.stack(turned(total, here), axis=1)
        total = jnp.stack(turned([total[at] for at in range(owned)], share % owned))
        results.append(total.reshape(owned, part, train_count))
    return jnp.concatenate(results, axis=1).reshape(owned * count, train_count)


def solution(mesh):
    in_specs = (P(("groups", "dp"), "proj", None), P(("groups", "dp"), "proj", None), P(), P(), P())
    out_specs = P(("groups", "proj"), "dp")
    return jax.shard_map(body, mesh=mesh, in_specs=in_specs, out_specs=out_specs, check_vma=False)
```

```python
import functools
import jax
import jax.numpy as jnp
from jax import lax
from jax.experimental import pallas as pl
from jax.experimental.pallas import tpu as pltpu
from jax.sharding import PartitionSpec as P

damping_term = 0.05
CHUNKS = (8, 8)
BLOCK = 64


def halves(value):
    high = value.astype(jnp.bfloat16)
    return high, (value - high.astype(jnp.float32)).astype(jnp.bfloat16)


def times(left, right):
    return jnp.dot(left, right, preferred_element_type=jnp.float32)


def three_wide(matrix):
    high, low = halves(matrix)
    return jnp.concatenate([high, low, high], axis=1)


def three_deep(matrix):
    high, low = halves(matrix)
    return jnp.concatenate([high, high, low], axis=0)


def condition_kernel(slices, rows_here, *refs):
    pieces = refs[:slices][::-1]
    basis, across, right_basis, right_across, corrections = refs[slices:slices + 5]
    outs, stage = refs[slices + 5:-1], refs[-1]
    enter, leave = three_wide(across[...]), three_wide(basis[...])
    right, back = halves(right_basis[...]), halves(right_across[...])
    count, _, columns = pieces[0].shape
    out_rows = slices * rows_here
    parts = []
    for piece in pieces:
        flat = piece[...].reshape(count * rows_here, columns)
        parts.append(halves(times(flat, right[0]) + times(flat, right[1])))
    scale = jnp.concatenate([1.0 / (corrections[...] + damping_term)] * 2, axis=1)

    def gathered(at, which):
        rows = slice(at * rows_here, (at + 1) * rows_here)
        return jnp.concatenate([part[which][rows] for part in parts], axis=0)

    for at in range(0, count, 2):
        high = jnp.concatenate([gathered(at, 0), gathered(at + 1, 0)], axis=1)
        low = jnp.concatenate([gathered(at, 1), gathered(at + 1, 1)], axis=1)
        rotated = times(enter, jnp.concatenate([high, high, low], axis=0))
        result = times(leave, three_deep(rotated * scale))
        stage[at * out_rows:(at + 1) * out_rows, :] = result[:, :columns]
        stage[(at + 1) * out_rows:(at + 2) * out_rows, :] = result[:, columns:]
    high, low = halves(stage[...])
    stage[...] = times(high, back[0]) + times(low, back[0]) + times(high, back[1])
    for row in range(out_rows):
        value = stage[pl.ds(row, count, stride=out_rows), :].astype(jnp.bfloat16)
        at = row % rows_here * columns
        outs[row // rows_here][:, at:at + columns] = value


def condition_fast(pieces, basis, in_basis, corrections):
    slices = len(pieces)
    count, rows_here, columns = pieces[0].shape
    block = min(BLOCK, count)
    width = rows_here * columns
    piece_spec = pl.BlockSpec((block, rows_here, columns), lambda step: (step, 0, 0))
    out_spec = pl.BlockSpec((block, width), lambda step: (step, 0))
    whole = pl.BlockSpec(memory_space=pltpu.VMEM)
    order = basis.shape[0]
    return pl.pallas_call(
        functools.partial(condition_kernel, slices, rows_here),
        grid=(count // block,),
        in_specs=[piece_spec] * slices + [whole] * 5,
        out_specs=[out_spec] * slices,
        out_shape=[jax.ShapeDtypeStruct((count, width), jnp.bfloat16)] * slices,
        scratch_shapes=[pltpu.VMEM((block * order, columns), jnp.float32)],
        compiler_params=pltpu.CompilerParams(vmem_limit_bytes=32 * 1024 * 1024),
        cost_estimate=pl.CostEstimate(flops=0, bytes_accessed=0, transcendentals=0),
    )(*pieces[::-1], basis, basis.T, in_basis, in_basis.T, corrections)


def condition_plain(pieces, basis, in_basis, corrections):
    high = lax.Precision.HIGH
    count, rows_here, columns = pieces[0].shape
    values = jnp.concatenate(pieces, axis=1).astype(jnp.float32)
    inner = jnp.einsum("qbc,cd->qbd", values, in_basis, precision=high)
    rotated = jnp.einsum("ba,qbd->qad", basis, inner, precision=high)
    left = jnp.einsum("ba,qad->qbd", basis, rotated / (corrections + damping_term), precision=high)
    result = jnp.einsum("qbd,ed->qbe", left, in_basis, precision=high).astype(jnp.bfloat16)
    starts = range(0, basis.shape[0], rows_here)
    return [result[:, at:at + rows_here].reshape(count, rows_here * columns) for at in starts]


def crossed(value, axis, size, mask):
    return lax.ppermute(value, axis, [(at, at ^ mask) for at in range(size)])


def exchanged(blocks, slices):
    moved = {mask: crossed(blocks[mask], "proj", slices, mask) for mask in reversed(range(1, slices))}
    return [blocks[0]] + [moved[mask] for mask in range(1, slices)]


def in_turn(blocks):
    done = []
    for block in reversed(blocks):
        done.append(after(block, *done[-1:]))
    return done[::-1]


def after(value, *tokens):
    return lax.optimization_barrier((value, tokens))[0]


def over_shares(rows, shares):
    near = jnp.concatenate(rows, axis=0)
    return [near] + [crossed(near, "dp", shares, mask) for mask in range(2, shares, 2)]


def products(near, far, train_flat, shares):
    contract = (((1,), (1,)), ((), ()))
    values = []
    for block in (near, far):
        value = lax.dot_general(block, train_flat, contract, preferred_element_type=jnp.float32)
        values.append(value.astype(jnp.bfloat16))
    return values


def split_shares(values, shares):
    values = [value.reshape(shares // 2, -1, value.shape[1]) for value in values]
    return [values[at % 2][at // 2] for at in range(shares)]


def turned(blocks, mask):
    bit = 1
    while bit < len(blocks):
        swap = mask // bit % 2 == 1
        blocks = [jnp.where(swap, blocks[at ^ bit], blocks[at]) for at in range(len(blocks))]
        bit *= 2
    return blocks


def body(queries, train_grads, out_basis, in_basis, corrections):
    slices = lax.axis_size("proj")
    shares = lax.axis_size("dp")
    here = lax.axis_index("proj")
    share = lax.axis_index("dp")
    count, rows_here, columns = queries.shape
    width = rows_here * columns
    owned = shares // slices
    train_count = train_grads.shape[0]
    train_flat = lax.optimization_barrier(train_grads.reshape(train_count, width))
    row_blocks = out_basis.reshape(slices, rows_here, -1)
    basis = jnp.concatenate(turned([row_blocks[at] for at in range(slices)], here), axis=0)
    condition = condition_fast if rows_here % 16 == 0 else condition_plain
    parts = [count * size // sum(CHUNKS) for size in CHUNKS]
    half = slices // 2
    pieces, rows, results = [], [], []
    source = queries
    for chunk, part in enumerate(parts):
        first, each = sum(parts[:chunk]), part // slices
        if chunk:
            source, pieces[0][-1], train_flat = lax.optimization_barrier((source, pieces[0][-1], train_flat))
        raw = {}
        for mask in (reversed(range(slices)) if chunk else range(slices)):
            block = lax.dynamic_slice_in_dim(source, first + (here ^ mask) * each, each, 0)
            raw[mask], source = lax.optimization_barrier((block, source))
        pieces.append(exchanged(raw, slices))
    made = condition(pieces[0], basis, in_basis, corrections)
    rows.append(exchanged(made, slices))
    rows[0][:half], pieces[1] = lax.optimization_barrier((rows[0][:half], pieces[1]))
    spread = over_shares(rows[0][:half], shares)
    made = condition(pieces[1], basis, in_basis, corrections)
    rows.append(exchanged(made, slices))
    rows[1][:half], spread = lax.optimization_barrier((rows[1][:half], spread))
    orders = [(range(half), range(half, slices))] * 2
    ahead = over_shares(rows[1][:half], shares)
    came = []
    for chunk, part in enumerate(parts):
        each = part // slices
        groups = []
        order = list(range(slices))
        for members in orders[chunk]:
            group = [rows[chunk][at] for at in members]
            if groups:
                spread = over_shares(after(group, near_before) if chunk else group, shares)
            elif chunk:
                spread = ahead
            if groups and not chunk:
                spread, ahead = lax.optimization_barrier((spread, ahead))
            tokens = came[:1]
            if chunk and groups:
                tokens = groups[0][:1]
            near = lax.optimization_barrier(jnp.concatenate(after(spread, *tokens), axis=0))
            far = crossed(near, "dp", shares, 1)
            groups.append(products(near, far, train_flat, shares))
        near_before = near
        groups = [split_shares(values, shares) for values in groups]
        values = [jnp.concatenate(pair, axis=0) for pair in zip(*groups)]
        values = [jnp.stack(values[at * owned:(at + 1) * owned]) for at in range(slices)]
        came = exchanged(in_turn(turned(values, here ^ (share // owned))), slices)
        sums = [value.reshape(owned, slices, each, train_count) for value in came]
        total = [
            sum(sums[mask][:, order.index(at ^ mask)].astype(jnp.float32) for mask in range(slices))
            for at in range(slices)
        ]
        total = jnp.stack(turned(total, here), axis=1)
        total = jnp.stack(turned([total[at] for at in range(owned)], share % owned))
        results.append(total.reshape(owned, part, train_count))
    return jnp.concatenate(results, axis=1).reshape(owned * count, train_count)


def solution(mesh):
    in_specs = (P(("groups", "dp"), "proj", None), P(("groups", "dp"), "proj", None), P(), P(), P())
    out_specs = P(("groups", "proj"), "dp")
    return jax.shard_map(body, mesh=mesh, in_specs=in_specs, out_specs=out_specs, check_vma=False)
```

```python
import functools
import jax
import jax.numpy as jnp
from jax import lax
from jax.experimental import pallas as pl
from jax.experimental.pallas import tpu as pltpu
from jax.sharding import PartitionSpec as P

damping_term = 0.05
CHUNKS = (8, 8)
BLOCK = 64


def halves(value):
    high = value.astype(jnp.bfloat16)
    return high, (value - high.astype(jnp.float32)).astype(jnp.bfloat16)


def times(left, right):
    return jnp.dot(left, right, preferred_element_type=jnp.float32)


def three_wide(matrix):
    high, low = halves(matrix)
    return jnp.concatenate([high, low, high], axis=1)


def three_deep(matrix):
    high, low = halves(matrix)
    return jnp.concatenate([high, high, low], axis=0)


def condition_kernel(slices, rows_here, *refs):
    pieces = refs[:slices][::-1]
    basis, across, right_basis, right_across, corrections = refs[slices:slices + 5]
    outs, stage = refs[slices + 5:-1], refs[-1]
    enter, leave = three_wide(across[...]), three_wide(basis[...])
    right, back = halves(right_basis[...]), halves(right_across[...])
    count, _, columns = pieces[0].shape
    out_rows = slices * rows_here
    parts = []
    for piece in pieces:
        flat = piece[...].reshape(count * rows_here, columns)
        parts.append(halves(times(flat, right[0]) + times(flat, right[1])))
    scale = jnp.concatenate([1.0 / (corrections[...] + damping_term)] * 2, axis=1)

    def gathered(at, which):
        rows = slice(at * rows_here, (at + 1) * rows_here)
        return jnp.concatenate([part[which][rows] for part in parts], axis=0)

    for at in range(0, count, 2):
        high = jnp.concatenate([gathered(at, 0), gathered(at + 1, 0)], axis=1)
        low = jnp.concatenate([gathered(at, 1), gathered(at + 1, 1)], axis=1)
        rotated = times(enter, jnp.concatenate([high, high, low], axis=0))
        result = times(leave, three_deep(rotated * scale))
        stage[at * out_rows:(at + 1) * out_rows, :] = result[:, :columns]
        stage[(at + 1) * out_rows:(at + 2) * out_rows, :] = result[:, columns:]
    high, low = halves(stage[...])
    stage[...] = times(high, back[0]) + times(low, back[0]) + times(high, back[1])
    for row in range(out_rows):
        value = stage[pl.ds(row, count, stride=out_rows), :].astype(jnp.bfloat16)
        at = row % rows_here * columns
        outs[row // rows_here][:, at:at + columns] = value


def condition_fast(pieces, basis, in_basis, corrections):
    slices = len(pieces)
    count, rows_here, columns = pieces[0].shape
    block = min(BLOCK, count)
    width = rows_here * columns
    piece_spec = pl.BlockSpec((block, rows_here, columns), lambda step: (step, 0, 0))
    out_spec = pl.BlockSpec((block, width), lambda step: (step, 0))
    whole = pl.BlockSpec(memory_space=pltpu.VMEM)
    order = basis.shape[0]
    return pl.pallas_call(
        functools.partial(condition_kernel, slices, rows_here),
        grid=(count // block,),
        in_specs=[piece_spec] * slices + [whole] * 5,
        out_specs=[out_spec] * slices,
        out_shape=[jax.ShapeDtypeStruct((count, width), jnp.bfloat16)] * slices,
        scratch_shapes=[pltpu.VMEM((block * order, columns), jnp.float32)],
        compiler_params=pltpu.CompilerParams(vmem_limit_bytes=32 * 1024 * 1024),
        cost_estimate=pl.CostEstimate(flops=0, bytes_accessed=0, transcendentals=0),
    )(*pieces[::-1], basis, basis.T, in_basis, in_basis.T, corrections)


def condition_plain(pieces, basis, in_basis, corrections):
    high = lax.Precision.HIGH
    count, rows_here, columns = pieces[0].shape
    values = jnp.concatenate(pieces, axis=1).astype(jnp.float32)
    inner = jnp.einsum("qbc,cd->qbd", values, in_basis, precision=high)
    rotated = jnp.einsum("ba,qbd->qad", basis, inner, precision=high)
    left = jnp.einsum("ba,qad->qbd", basis, rotated / (corrections + damping_term), precision=high)
    result = jnp.einsum("qbd,ed->qbe", left, in_basis, precision=high).astype(jnp.bfloat16)
    starts = range(0, basis.shape[0], rows_here)
    return [result[:, at:at + rows_here].reshape(count, rows_here * columns) for at in starts]


def crossed(value, axis, size, mask):
    return lax.ppermute(value, axis, [(at, at ^ mask) for at in range(size)])


def exchanged(blocks, slices):
    moved = {mask: crossed(blocks[mask], "proj", slices, mask) for mask in reversed(range(1, slices))}
    return [blocks[0]] + [moved[mask] for mask in range(1, slices)]


def in_turn(blocks):
    done = []
    for block in reversed(blocks):
        done.append(after(block, *done[-1:]))
    return done[::-1]


def after(value, *tokens):
    return lax.optimization_barrier((value, tokens))[0]


def over_shares(rows, shares):
    near = jnp.concatenate(rows, axis=0)
    return [near] + [crossed(near, "dp", shares, mask) for mask in range(2, shares, 2)]


def products(near, far, train_flat, shares):
    contract = (((1,), (1,)), ((), ()))
    values = []
    for block in (near, far):
        value = lax.dot_general(block, train_flat, contract, preferred_element_type=jnp.float32)
        values.append(value.astype(jnp.bfloat16).reshape(shares // 2, -1, train_flat.shape[0]))
    return [values[at % 2][at // 2] for at in range(shares)]


def turned(blocks, mask):
    bit = 1
    while bit < len(blocks):
        swap = mask // bit % 2 == 1
        blocks = [jnp.where(swap, blocks[at ^ bit], blocks[at]) for at in range(len(blocks))]
        bit *= 2
    return blocks


def body(queries, train_grads, out_basis, in_basis, corrections):
    slices = lax.axis_size("proj")
    shares = lax.axis_size("dp")
    here = lax.axis_index("proj")
    share = lax.axis_index("dp")
    count, rows_here, columns = queries.shape
    width = rows_here * columns
    owned = shares // slices
    train_count = train_grads.shape[0]
    train_flat = lax.optimization_barrier(train_grads.reshape(train_count, width))
    row_blocks = out_basis.reshape(slices, rows_here, -1)
    basis = jnp.concatenate(turned([row_blocks[at] for at in range(slices)], here), axis=0)
    condition = condition_fast if rows_here % 16 == 0 else condition_plain
    parts = [count * size // sum(CHUNKS) for size in CHUNKS]
    half = slices // 2
    pieces, rows, results = [], [], []
    source = queries
    for chunk, part in enumerate(parts):
        first, each = sum(parts[:chunk]), part // slices
        raw = {}
        for mask in (reversed(range(slices)) if chunk else range(slices)):
            block = lax.dynamic_slice_in_dim(source, first + (here ^ mask) * each, each, 0)
            raw[mask], source = lax.optimization_barrier((block, source))
        if chunk:
            raw[1], pieces[0][-1] = lax.optimization_barrier((raw[1], pieces[0][-1]))
        pieces.append(exchanged(raw, slices))
    pieces[0], train_flat = lax.optimization_barrier((pieces[0], train_flat))
    made = condition(pieces[0], basis, in_basis, corrections)
    rows.append(exchanged(made, slices))
    rows[0][:half], pieces[1] = lax.optimization_barrier((rows[0][:half], pieces[1]))
    spread = over_shares(rows[0][:half], shares)
    made = condition(pieces[1], basis, in_basis, corrections)
    rows.append(exchanged(made, slices))
    rows[1][:half], spread = lax.optimization_barrier((rows[1][:half], spread))
    near_rows, far_rows = list(range(half)), list(range(half, slices))
    orders = [(near_rows, far_rows)] * 2
    came = []
    for chunk, part in enumerate(parts):
        each = part // slices
        groups = []
        order = sum(orders[chunk], [])
        for members in orders[chunk]:
            group = [rows[chunk][at] for at in members]
            if chunk and groups:
                group = after(group, near_before)
            if chunk or groups:
                spread = over_shares(group, shares)
            near = lax.optimization_barrier(jnp.concatenate(after(spread, *came[:1]), axis=0))
            far = crossed(near, "dp", shares, 1)
            groups.append(products(near, far, train_flat, shares))
        near_before = near
        values = [jnp.concatenate(pair, axis=0) for pair in zip(*groups)]
        values = [jnp.stack(values[at * owned:(at + 1) * owned]) for at in range(slices)]
        came = exchanged(in_turn(turned(values, here ^ (share // owned))), slices)
        sums = [value.reshape(owned, slices, each, train_count) for value in came]
        total = [
            sum(sums[mask][:, order.index(at ^ mask)].astype(jnp.float32) for mask in range(slices))
            for at in range(slices)
        ]
        total = jnp.stack(turned(total, here), axis=1)
        total = jnp.stack(turned([total[at] for at in range(owned)], share % owned))
        results.append(total.reshape(owned, part, train_count))
    return jnp.concatenate(results, axis=1).reshape(owned * count, train_count)


def solution(mesh):
    in_specs = (P(("groups", "dp"), "proj", None), P(("groups", "dp"), "proj", None), P(), P(), P())
    out_specs = P(("groups", "proj"), "dp")
    return jax.shard_map(body, mesh=mesh, in_specs=in_specs, out_specs=out_specs, check_vma=False)
```

```python
import functools
import jax
import jax.numpy as jnp
from jax import lax
from jax.experimental import pallas as pl
from jax.experimental.pallas import tpu as pltpu
from jax.sharding import PartitionSpec as P

damping_term = 0.05
CHUNKS = (8, 8)
BLOCK = 64


def halves(value):
    high = value.astype(jnp.bfloat16)
    return high, (value - high.astype(jnp.float32)).astype(jnp.bfloat16)


def times(left, right):
    return jnp.dot(left, right, preferred_element_type=jnp.float32)


def three_wide(matrix):
    high, low = halves(matrix)
    return jnp.concatenate([high, low, high], axis=1)


def three_deep(matrix):
    high, low = halves(matrix)
    return jnp.concatenate([high, high, low], axis=0)


def condition_kernel(slices, rows_here, *refs):
    pieces = refs[:slices][::-1]
    basis, across, right_basis, right_across, corrections = refs[slices:slices + 5]
    outs, stage = refs[slices + 5:-1], refs[-1]
    enter, leave = three_wide(across[...]), three_wide(basis[...])
    right, back = halves(right_basis[...]), halves(right_across[...])
    count, _, columns = pieces[0].shape
    out_rows = slices * rows_here
    parts = []
    for piece in pieces:
        flat = piece[...].reshape(count * rows_here, columns)
        parts.append(halves(times(flat, right[0]) + times(flat, right[1])))
    scale = jnp.concatenate([1.0 / (corrections[...] + damping_term)] * 2, axis=1)

    def gathered(at, which):
        rows = slice(at * rows_here, (at + 1) * rows_here)
        return jnp.concatenate([part[which][rows] for part in parts], axis=0)

    for at in range(0, count, 2):
        high = jnp.concatenate([gathered(at, 0), gathered(at + 1, 0)], axis=1)
        low = jnp.concatenate([gathered(at, 1), gathered(at + 1, 1)], axis=1)
        rotated = times(enter, jnp.concatenate([high, high, low], axis=0))
        result = times(leave, three_deep(rotated * scale))
        stage[at * out_rows:(at + 1) * out_rows, :] = result[:, :columns]
        stage[(at + 1) * out_rows:(at + 2) * out_rows, :] = result[:, columns:]
    high, low = halves(stage[...])
    stage[...] = times(high, back[0]) + times(low, back[0]) + times(high, back[1])
    for row in range(out_rows):
        value = stage[pl.ds(row, count, stride=out_rows), :].astype(jnp.bfloat16)
        at = row % rows_here * columns
        outs[row // rows_here][:, at:at + columns] = value


def condition_fast(pieces, basis, in_basis, corrections):
    slices = len(pieces)
    count, rows_here, columns = pieces[0].shape
    block = min(BLOCK, count)
    width = rows_here * columns
    piece_spec = pl.BlockSpec((block, rows_here, columns), lambda step: (step, 0, 0))
    out_spec = pl.BlockSpec((block, width), lambda step: (step, 0))
    whole = pl.BlockSpec(memory_space=pltpu.VMEM)
    order = basis.shape[0]
    return pl.pallas_call(
        functools.partial(condition_kernel, slices, rows_here),
        grid=(count // block,),
        in_specs=[piece_spec] * slices + [whole] * 5,
        out_specs=[out_spec] * slices,
        out_shape=[jax.ShapeDtypeStruct((count, width), jnp.bfloat16)] * slices,
        scratch_shapes=[pltpu.VMEM((block * order, columns), jnp.float32)],
        compiler_params=pltpu.CompilerParams(vmem_limit_bytes=32 * 1024 * 1024),
        cost_estimate=pl.CostEstimate(flops=1000000000, bytes_accessed=0, transcendentals=0),
    )(*pieces[::-1], basis, basis.T, in_basis, in_basis.T, corrections)


def condition_plain(pieces, basis, in_basis, corrections):
    high = lax.Precision.HIGH
    count, rows_here, columns = pieces[0].shape
    values = jnp.concatenate(pieces, axis=1).astype(jnp.float32)
    inner = jnp.einsum("qbc,cd->qbd", values, in_basis, precision=high)
    rotated = jnp.einsum("ba,qbd->qad", basis, inner, precision=high)
    left = jnp.einsum("ba,qad->qbd", basis, rotated / (corrections + damping_term), precision=high)
    result = jnp.einsum("qbd,ed->qbe", left, in_basis, precision=high).astype(jnp.bfloat16)
    starts = range(0, basis.shape[0], rows_here)
    return [result[:, at:at + rows_here].reshape(count, rows_here * columns) for at in starts]


def crossed(value, axis, size, mask):
    return lax.ppermute(value, axis, [(at, at ^ mask) for at in range(size)])


def exchanged(blocks, slices):
    moved = {mask: crossed(blocks[mask], "proj", slices, mask) for mask in reversed(range(1, slices))}
    return [blocks[0]] + [moved[mask] for mask in range(1, slices)]


def in_turn(blocks):
    done = []
    for block in reversed(blocks):
        done.append(after(block, *done[-1:]))
    return done[::-1]


def met(block, mask, count):
    rows = jnp.split(block, count, axis=1)
    return jnp.concatenate([rows[at ^ mask] for at in range(count)], axis=1)


def paired(blocks, mask, slices, kind):
    arrived = crossed(jnp.stack(blocks[1::2]), "proj", slices, mask)
    kept = blocks[::2]
    moved = [met(arrived[at], mask, kept[at].shape[1]).astype(jnp.float32) for at in range(len(kept))]
    return [(value.astype(jnp.float32) + other).astype(kind) for value, other in zip(kept, moved)]


def after(value, *tokens):
    return lax.optimization_barrier((value, tokens))[0]


def over_shares(rows, shares):
    near = jnp.concatenate(rows, axis=0)
    return [near] + [crossed(near, "dp", shares, mask) for mask in range(2, shares, 2)]


def products(near, far, train_flat, shares):
    contract = (((1,), (1,)), ((), ()))
    values = []
    for block in (near, far):
        value = lax.dot_general(block, train_flat, contract, preferred_element_type=jnp.float32)
        values.append(value.astype(jnp.bfloat16))
    return values


def split_shares(values, shares):
    values = [value.reshape(shares // 2, -1, value.shape[1]) for value in values]
    return [values[at % 2][at // 2] for at in range(shares)]


def turned(blocks, mask):
    bit = 1
    while bit < len(blocks):
        swap = mask // bit % 2 == 1
        blocks = [jnp.where(swap, blocks[at ^ bit], blocks[at]) for at in range(len(blocks))]
        bit *= 2
    return blocks


def body(queries, train_grads, out_basis, in_basis, corrections):
    slices = lax.axis_size("proj")
    shares = lax.axis_size("dp")
    here = lax.axis_index("proj")
    share = lax.axis_index("dp")
    count, rows_here, columns = queries.shape
    width = rows_here * columns
    owned = shares // slices
    train_count = train_grads.shape[0]
    train_flat = lax.optimization_barrier(train_grads.reshape(train_count, width))
    row_blocks = out_basis.reshape(slices, rows_here, -1)
    basis = jnp.concatenate(turned([row_blocks[at] for at in range(slices)], here), axis=0)
    condition = condition_fast if rows_here % 16 == 0 else condition_plain
    parts = [count * size // sum(CHUNKS) for size in CHUNKS]
    source = queries
    half = slices // 2
    pieces, results = [], []
    for chunk, part in enumerate(parts):
        first, each = sum(parts[:chunk]), part // slices
        if chunk:
            source, pieces[0][-1] = lax.optimization_barrier((source, pieces[0][-1]))
        raw = {}
        for mask in (range(slices) if chunk else reversed(range(slices))):
            block = lax.dynamic_slice_in_dim(source, first + (here ^ mask) * each, each, 0)
            raw[mask], source = lax.optimization_barrier((block, source))
        pieces.append(exchanged(raw, slices))
    made = condition(pieces[0], basis, in_basis, corrections)
    first_rows = exchanged(made, slices)
    first_rows[:half], pieces[1] = lax.optimization_barrier((first_rows[:half], pieces[1]))
    spread_a1 = over_shares(first_rows[:half], shares)
    made = condition(pieces[1], basis, in_basis, corrections)
    last_rows = exchanged(made, slices)
    first_rows[half:], last_rows[1] = lax.optimization_barrier((first_rows[half:], last_rows[1]))
    spread_a2 = over_shares(first_rows[half:], shares)
    last_rows[:half], spread_a1 = lax.optimization_barrier((last_rows[:half], spread_a1))
    place = here ^ (share // owned)
    spread_a1 = after(spread_a1, last_rows[1])
    near_a1 = lax.optimization_barrier(jnp.concatenate(spread_a1, axis=0))
    far_a1 = crossed(near_a1, "dp", shares, 1)
    val_a1 = products(near_a1, far_a1, train_flat, shares)
    spread_b1 = over_shares(last_rows[:half], shares)
    near_a2 = lax.optimization_barrier(jnp.concatenate(spread_a2, axis=0))
    far_a2 = crossed(near_a2, "dp", shares, 1)
    val_a2 = products(near_a2, far_a2, train_flat, shares)
    part_a1 = split_shares(val_a1, shares)
    part_a1 = [jnp.concatenate(part_a1[at * owned:(at + 1) * owned]) for at in range(slices)]
    part_a1 = [value.reshape(owned, half, -1, train_count) for value in part_a1]
    part_a2 = split_shares(val_a2, shares)
    part_a2 = [jnp.concatenate(part_a2[at * owned:(at + 1) * owned]) for at in range(slices)]
    part_a2 = [value.reshape(owned, half, -1, train_count) for value in part_a2]
    blocks = turned([jnp.concatenate(pair, axis=1) for pair in zip(part_a1, part_a2)], place)
    blocks = in_turn(blocks)
    came = exchanged(blocks, slices)
    group = after(last_rows[half:], far_a1)
    spread_b2 = over_shares(group, shares)
    spread_b1 = after(spread_b1, came[0])
    near_b1 = lax.optimization_barrier(jnp.concatenate(spread_b1, axis=0))
    far_b1 = crossed(near_b1, "dp", shares, 1)
    val_b1 = products(near_b1, far_b1, train_flat, shares)
    spread_b2 = after(spread_b2, came[0])
    near_b2 = lax.optimization_barrier(jnp.concatenate(spread_b2, axis=0))
    far_b2 = crossed(near_b2, "dp", shares, 1)
    val_b2 = products(near_b2, far_b2, train_flat, shares)
    part_b1 = split_shares(val_b1, shares)
    part_b1 = [jnp.concatenate(part_b1[at * owned:(at + 1) * owned]) for at in range(slices)]
    part_b1 = [value.reshape(owned, half, -1, train_count) for value in part_b1]
    part_b2 = split_shares(val_b2, shares)
    part_b2 = [jnp.concatenate(part_b2[at * owned:(at + 1) * owned]) for at in range(slices)]
    part_b2 = [value.reshape(owned, half, -1, train_count) for value in part_b2]
    blocks = turned([jnp.concatenate(pair, axis=1) for pair in zip(part_b1, part_b2)], place)
    blocks = in_turn(blocks)
    left = exchanged(blocks, slices)
    last = [sum(left[mask][:, at ^ mask].astype(jnp.float32) for mask in range(slices)) for at in range(slices)]
    whole = [sum(came[mask][:, at ^ mask].astype(jnp.float32) for mask in range(slices)) for at in range(slices)]
    for part, total in zip(parts, (whole, last)):
        total = jnp.stack(turned(total, here), axis=1)
        total = jnp.stack(turned([total[at] for at in range(owned)], share % owned))
        results.append(total.reshape(owned, part, train_count))
    return jnp.concatenate(results, axis=1).reshape(owned * count, train_count)


def solution(mesh):
    in_specs = (P(("groups", "dp"), "proj", None), P(("groups", "dp"), "proj", None), P(), P(), P())
    out_specs = P(("groups", "proj"), "dp")
    return jax.shard_map(body, mesh=mesh, in_specs=in_specs, out_specs=out_specs, check_vma=False)
```

```python
import functools
import jax
import jax.numpy as jnp
from jax import lax
from jax.experimental import pallas as pl
from jax.experimental.pallas import tpu as pltpu
from jax.sharding import PartitionSpec as P

damping_term = 0.05
CHUNKS = (8, 8)
BLOCK = 64
FLAT = 64


def halves(value):
    high = value.astype(jnp.bfloat16)
    return high, (value - high.astype(jnp.float32)).astype(jnp.bfloat16)


def times(left, right):
    return jnp.dot(left, right, preferred_element_type=jnp.float32)


def three_wide(matrix):
    high, low = halves(matrix)
    return jnp.concatenate([high, low, high], axis=1)


def three_deep(matrix):
    high, low = halves(matrix)
    return jnp.concatenate([high, high, low], axis=0)


def condition_kernel(slices, rows_here, *refs):
    pieces = refs[:slices][::-1]
    basis, across, right_basis, right_across, corrections = refs[slices:slices + 5]
    outs, stage = refs[slices + 5:-1], refs[-1]
    enter, leave = three_wide(across[...]), three_wide(basis[...])
    right, back = halves(right_basis[...]), halves(right_across[...])
    count, _, columns = pieces[0].shape
    out_rows = slices * rows_here
    parts = []
    for piece in pieces:
        flat = piece[...].reshape(count * rows_here, columns)
        parts.append(halves(times(flat, right[0]) + times(flat, right[1])))
    scale = jnp.concatenate([1.0 / (corrections[...] + damping_term)] * 2, axis=1)

    def gathered(at, which):
        rows = slice(at * rows_here, (at + 1) * rows_here)
        return jnp.concatenate([part[which][rows] for part in parts], axis=0)

    for at in range(0, count, 2):
        high = jnp.concatenate([gathered(at, 0), gathered(at + 1, 0)], axis=1)
        low = jnp.concatenate([gathered(at, 1), gathered(at + 1, 1)], axis=1)
        rotated = times(enter, jnp.concatenate([high, high, low], axis=0))
        result = times(leave, three_deep(rotated * scale))
        stage[at * out_rows:(at + 1) * out_rows, :] = result[:, :columns]
        stage[(at + 1) * out_rows:(at + 2) * out_rows, :] = result[:, columns:]
    high, low = halves(stage[...])
    stage[...] = times(high, back[0]) + times(low, back[0]) + times(high, back[1])
    for row in range(out_rows):
        value = stage[pl.ds(row, count, stride=out_rows), :].astype(jnp.bfloat16)
        at = row % rows_here * columns
        outs[row // rows_here][:, at:at + columns] = value


def condition_fast(pieces, basis, in_basis, corrections):
    slices = len(pieces)
    count, rows_here, columns = pieces[0].shape
    block = min(BLOCK, count)
    width = rows_here * columns
    piece_spec = pl.BlockSpec((block, rows_here, columns), lambda step: (step, 0, 0))
    out_spec = pl.BlockSpec((block, width), lambda step: (step, 0))
    whole = pl.BlockSpec(memory_space=pltpu.VMEM)
    order = basis.shape[0]
    return pl.pallas_call(
        functools.partial(condition_kernel, slices, rows_here),
        grid=(count // block,),
        in_specs=[piece_spec] * slices + [whole] * 5,
        out_specs=[out_spec] * slices,
        out_shape=[jax.ShapeDtypeStruct((count, width), jnp.bfloat16)] * slices,
        scratch_shapes=[pltpu.VMEM((block * order, columns), jnp.float32)],
        compiler_params=pltpu.CompilerParams(vmem_limit_bytes=32 * 1024 * 1024),
        cost_estimate=pl.CostEstimate(flops=1000000000, bytes_accessed=0, transcendentals=0),
    )(*pieces[::-1], basis, basis.T, in_basis, in_basis.T, corrections)


def flatten_kernel(rows, flat, stage):
    count, each, columns = rows.shape
    stage[...] = rows[...].reshape(count * each, columns).astype(jnp.float32)
    for row in range(each):
        flat[:, row * columns:(row + 1) * columns] = stage[pl.ds(row, count, stride=each), :].astype(flat.dtype)


def flatten(rows):
    count, each, columns = rows.shape
    if each % 16 or count % FLAT:
        return rows.reshape(count, each * columns)
    return pl.pallas_call(
        flatten_kernel,
        grid=(count // FLAT,),
        in_specs=[pl.BlockSpec((FLAT, each, columns), lambda step: (step, 0, 0))],
        out_specs=pl.BlockSpec((FLAT, each * columns), lambda step: (step, 0)),
        out_shape=jax.ShapeDtypeStruct((count, each * columns), rows.dtype),
        scratch_shapes=[pltpu.VMEM((FLAT * each, columns), jnp.float32)],
        compiler_params=pltpu.CompilerParams(vmem_limit_bytes=32 * 1024 * 1024),
        cost_estimate=pl.CostEstimate(flops=1000000000, bytes_accessed=0, transcendentals=0),
    )(rows)


def condition_plain(pieces, basis, in_basis, corrections):
    high = lax.Precision.HIGH
    count, rows_here, columns = pieces[0].shape
    values = jnp.concatenate(pieces, axis=1).astype(jnp.float32)
    inner = jnp.einsum("qbc,cd->qbd", values, in_basis, precision=high)
    rotated = jnp.einsum("ba,qbd->qad", basis, inner, precision=high)
    left = jnp.einsum("ba,qad->qbd", basis, rotated / (corrections + damping_term), precision=high)
    result = jnp.einsum("qbd,ed->qbe", left, in_basis, precision=high).astype(jnp.bfloat16)
    starts = range(0, basis.shape[0], rows_here)
    return [result[:, at:at + rows_here].reshape(count, rows_here * columns) for at in starts]


def crossed(value, axis, size, mask):
    return lax.ppermute(value, axis, [(at, at ^ mask) for at in range(size)])


def exchanged(blocks, slices):
    moved = {mask: crossed(blocks[mask], "proj", slices, mask) for mask in reversed(range(1, slices))}
    return [blocks[0]] + [moved[mask] for mask in range(1, slices)]


def in_turn(blocks):
    done = []
    for block in reversed(blocks):
        done.append(after(block, *done[-1:]))
    return done[::-1]


def met(block, mask, count):
    rows = jnp.split(block, count, axis=1)
    return jnp.concatenate([rows[at ^ mask] for at in range(count)], axis=1)


def paired(blocks, mask, slices, kind):
    arrived = crossed(jnp.stack(blocks[1::2]), "proj", slices, mask)
    kept = blocks[::2]
    moved = [met(arrived[at], mask, kept[at].shape[1]).astype(jnp.float32) for at in range(len(kept))]
    return [(value.astype(jnp.float32) + other).astype(kind) for value, other in zip(kept, moved)]


def after(value, *tokens):
    return lax.optimization_barrier((value, tokens))[0]


def over_shares(rows, shares):
    near = jnp.concatenate(rows, axis=0)
    return [near] + [crossed(near, "dp", shares, mask) for mask in range(2, shares, 2)]


def products(near, far, train_flat, shares):
    contract = (((1,), (1,)), ((), ()))
    values = []
    for block in (near, far):
        value = lax.dot_general(block, train_flat, contract, preferred_element_type=jnp.float32)
        values.append(value.astype(jnp.bfloat16))
    return values


def split_shares(values, shares):
    values = [value.reshape(shares // 2, -1, value.shape[1]) for value in values]
    return [values[at % 2][at // 2] for at in range(shares)]


def turned(blocks, mask):
    bit = 1
    while bit < len(blocks):
        swap = mask // bit % 2 == 1
        blocks = [jnp.where(swap, blocks[at ^ bit], blocks[at]) for at in range(len(blocks))]
        bit *= 2
    return blocks


def body(queries, train_grads, out_basis, in_basis, corrections):
    slices = lax.axis_size("proj")
    shares = lax.axis_size("dp")
    here = lax.axis_index("proj")
    share = lax.axis_index("dp")
    count, rows_here, columns = queries.shape
    width = rows_here * columns
    owned = shares // slices
    train_count = train_grads.shape[0]
    train_flat = flatten(train_grads)
    row_blocks = out_basis.reshape(slices, rows_here, -1)
    basis = jnp.concatenate(turned([row_blocks[at] for at in range(slices)], here), axis=0)
    condition = condition_fast if rows_here % 16 == 0 else condition_plain
    parts = [count * size // sum(CHUNKS) for size in CHUNKS]
    source = queries
    half = slices // 2
    pieces, results = [], []
    for chunk, part in enumerate(parts):
        first, each = sum(parts[:chunk]), part // slices
        if chunk:
            source, pieces[0][-1], train_flat = lax.optimization_barrier((source, pieces[0][-1], train_flat))
        raw = {}
        for mask in (reversed(range(slices)) if chunk else reversed(range(slices))):
            block = lax.dynamic_slice_in_dim(source, first + (here ^ mask) * each, each, 0)
            raw[mask], source = lax.optimization_barrier((block, source))
        pieces.append(exchanged(raw, slices))
    made = condition(pieces[0], basis, in_basis, corrections)
    first_rows = exchanged(made, slices)
    first_rows[:half], pieces[1] = lax.optimization_barrier((first_rows[:half], pieces[1]))
    spread_a1 = over_shares(first_rows[:half], shares)
    made = condition(pieces[1], basis, in_basis, corrections)
    last_rows = exchanged(made, slices)
    first_rows[half:], last_rows[1] = lax.optimization_barrier((first_rows[half:], last_rows[1]))
    spread_a2 = over_shares(first_rows[half:], shares)
    last_rows[:half], spread_a1 = lax.optimization_barrier((last_rows[:half], spread_a1))
    place = here ^ (share // owned)
    spread_a1 = after(spread_a1, last_rows[1])
    near_a1 = lax.optimization_barrier(jnp.concatenate(spread_a1, axis=0))
    far_a1 = crossed(near_a1, "dp", shares, 1)
    val_a1 = products(near_a1, far_a1, train_flat, shares)
    spread_b1 = over_shares(last_rows[:half], shares)
    near_a2 = lax.optimization_barrier(jnp.concatenate(spread_a2, axis=0))
    far_a2 = crossed(near_a2, "dp", shares, 1)
    val_a2 = products(near_a2, far_a2, train_flat, shares)
    part_a1 = split_shares(val_a1, shares)
    part_a1 = [jnp.concatenate(part_a1[at * owned:(at + 1) * owned]) for at in range(slices)]
    part_a1 = [value.reshape(owned, half, -1, train_count) for value in part_a1]
    part_a2 = split_shares(val_a2, shares)
    part_a2 = [jnp.concatenate(part_a2[at * owned:(at + 1) * owned]) for at in range(slices)]
    part_a2 = [value.reshape(owned, half, -1, train_count) for value in part_a2]
    blocks = turned([jnp.concatenate(pair, axis=1) for pair in zip(part_a1, part_a2)], place)
    blocks = in_turn(blocks)
    came = exchanged(blocks, slices)
    group = after(last_rows[half:], near_a2)
    spread_b2 = over_shares(group, shares)
    spread_b1 = after(spread_b1, came[0])
    near_b1 = lax.optimization_barrier(jnp.concatenate(spread_b1, axis=0))
    far_b1 = crossed(near_b1, "dp", shares, 1)
    val_b1 = products(near_b1, far_b1, train_flat, shares)
    spread_b2 = after(spread_b2, came[0])
    near_b2 = lax.optimization_barrier(jnp.concatenate(spread_b2, axis=0))
    far_b2 = crossed(near_b2, "dp", shares, 1)
    val_b2 = products(near_b2, far_b2, train_flat, shares)
    part_b1 = split_shares(val_b1, shares)
    part_b1 = [jnp.concatenate(part_b1[at * owned:(at + 1) * owned]) for at in range(slices)]
    part_b1 = [value.reshape(owned, half, -1, train_count) for value in part_b1]
    part_b2 = split_shares(val_b2, shares)
    part_b2 = [jnp.concatenate(part_b2[at * owned:(at + 1) * owned]) for at in range(slices)]
    part_b2 = [value.reshape(owned, half, -1, train_count) for value in part_b2]
    blocks = turned([jnp.concatenate(pair, axis=1) for pair in zip(part_b1, part_b2)], place)
    blocks = in_turn(blocks)
    left = exchanged(blocks, slices)
    last = [sum(left[mask][:, at ^ mask].astype(jnp.float32) for mask in range(slices)) for at in range(slices)]
    whole = [sum(came[mask][:, at ^ mask].astype(jnp.float32) for mask in range(slices)) for at in range(slices)]
    for part, total in zip(parts, (whole, last)):
        total = jnp.stack(turned(total, here), axis=1)
        total = jnp.stack(turned([total[at] for at in range(owned)], share % owned))
        results.append(total.reshape(owned, part, train_count))
    return jnp.concatenate(results, axis=1).reshape(owned * count, train_count)


def solution(mesh):
    in_specs = (P(("groups", "dp"), "proj", None), P(("groups", "dp"), "proj", None), P(), P(), P())
    out_specs = P(("groups", "proj"), "dp")
    return jax.shard_map(body, mesh=mesh, in_specs=in_specs, out_specs=out_specs, check_vma=False)
```

```python
import functools
import jax
import jax.numpy as jnp
from jax import lax
from jax.experimental import pallas as pl
from jax.experimental.pallas import tpu as pltpu
from jax.sharding import PartitionSpec as P

damping_term = 0.05
CHUNKS = (8, 8)
BLOCK = 64
FLAT = 64


def halves(value):
    high = value.astype(jnp.bfloat16)
    return high, (value - high.astype(jnp.float32)).astype(jnp.bfloat16)


def times(left, right):
    return jnp.dot(left, right, preferred_element_type=jnp.float32)


def three_wide(matrix):
    high, low = halves(matrix)
    return jnp.concatenate([high, low, high], axis=1)


def three_deep(matrix):
    high, low = halves(matrix)
    return jnp.concatenate([high, high, low], axis=0)


def condition_kernel(slices, rows_here, *refs):
    pieces = refs[:slices][::-1]
    basis, across, right_basis, right_across, corrections = refs[slices:slices + 5]
    outs, stage = refs[slices + 5:-1], refs[-1]
    enter, leave = three_wide(across[...]), three_wide(basis[...])
    right, back = halves(right_basis[...]), halves(right_across[...])
    count, _, columns = pieces[0].shape
    out_rows = slices * rows_here
    parts = []
    for piece in pieces:
        flat = piece[...].reshape(count * rows_here, columns)
        parts.append(halves(times(flat, right[0]) + times(flat, right[1])))
    scale = jnp.concatenate([1.0 / (corrections[...] + damping_term)] * 2, axis=1)

    def gathered(at, which):
        rows = slice(at * rows_here, (at + 1) * rows_here)
        return jnp.concatenate([part[which][rows] for part in parts], axis=0)

    for at in range(0, count, 2):
        high = jnp.concatenate([gathered(at, 0), gathered(at + 1, 0)], axis=1)
        low = jnp.concatenate([gathered(at, 1), gathered(at + 1, 1)], axis=1)
        rotated = times(enter, jnp.concatenate([high, high, low], axis=0))
        result = times(leave, three_deep(rotated * scale))
        stage[at * out_rows:(at + 1) * out_rows, :] = result[:, :columns]
        stage[(at + 1) * out_rows:(at + 2) * out_rows, :] = result[:, columns:]
    high, low = halves(stage[...])
    stage[...] = times(high, back[0]) + times(low, back[0]) + times(high, back[1])
    for row in range(out_rows):
        value = stage[pl.ds(row, count, stride=out_rows), :].astype(jnp.bfloat16)
        at = row % rows_here * columns
        outs[row // rows_here][:, at:at + columns] = value


def condition_fast(pieces, basis, in_basis, corrections):
    slices = len(pieces)
    count, rows_here, columns = pieces[0].shape
    block = min(BLOCK, count)
    width = rows_here * columns
    piece_spec = pl.BlockSpec((block, rows_here, columns), lambda step: (step, 0, 0))
    out_spec = pl.BlockSpec((block, width), lambda step: (step, 0))
    whole = pl.BlockSpec(memory_space=pltpu.VMEM)
    order = basis.shape[0]
    return pl.pallas_call(
        functools.partial(condition_kernel, slices, rows_here),
        grid=(count // block,),
        in_specs=[piece_spec] * slices + [whole] * 5,
        out_specs=[out_spec] * slices,
        out_shape=[jax.ShapeDtypeStruct((count, width), jnp.bfloat16)] * slices,
        scratch_shapes=[pltpu.VMEM((block * order, columns), jnp.float32)],
        compiler_params=pltpu.CompilerParams(vmem_limit_bytes=16 * 1024 * 1024),
        cost_estimate=pl.CostEstimate(flops=1000000000, bytes_accessed=0, transcendentals=0),
    )(*pieces[::-1], basis, basis.T, in_basis, in_basis.T, corrections)


def flatten_kernel(rows, flat, stage):
    count, each, columns = rows.shape
    stage[...] = rows[...].reshape(count * each, columns).astype(jnp.float32)
    for row in range(each):
        flat[:, row * columns:(row + 1) * columns] = stage[pl.ds(row, count, stride=each), :].astype(flat.dtype)


def flatten(rows):
    count, each, columns = rows.shape
    if each % 16 or count % FLAT:
        return rows.reshape(count, each * columns)
    return pl.pallas_call(
        flatten_kernel,
        grid=(count // FLAT,),
        in_specs=[pl.BlockSpec((FLAT, each, columns), lambda step: (step, 0, 0))],
        out_specs=pl.BlockSpec((FLAT, each * columns), lambda step: (step, 0)),
        out_shape=jax.ShapeDtypeStruct((count, each * columns), rows.dtype),
        scratch_shapes=[pltpu.VMEM((FLAT * each, columns), jnp.float32)],
        compiler_params=pltpu.CompilerParams(vmem_limit_bytes=8 * 1024 * 1024),
        cost_estimate=pl.CostEstimate(flops=1000000000, bytes_accessed=0, transcendentals=0),
    )(rows)


def condition_plain(pieces, basis, in_basis, corrections):
    high = lax.Precision.HIGH
    count, rows_here, columns = pieces[0].shape
    values = jnp.concatenate(pieces, axis=1).astype(jnp.float32)
    inner = jnp.einsum("qbc,cd->qbd", values, in_basis, precision=high)
    rotated = jnp.einsum("ba,qbd->qad", basis, inner, precision=high)
    left = jnp.einsum("ba,qad->qbd", basis, rotated / (corrections + damping_term), precision=high)
    result = jnp.einsum("qbd,ed->qbe", left, in_basis, precision=high).astype(jnp.bfloat16)
    starts = range(0, basis.shape[0], rows_here)
    return [result[:, at:at + rows_here].reshape(count, rows_here * columns) for at in starts]


def crossed(value, axis, size, mask):
    return lax.ppermute(value, axis, [(at, at ^ mask) for at in range(size)])


def exchanged(blocks, slices):
    moved = {mask: crossed(blocks[mask], "proj", slices, mask) for mask in reversed(range(1, slices))}
    return [blocks[0]] + [moved[mask] for mask in range(1, slices)]


def in_turn(blocks):
    done = []
    for block in reversed(blocks):
        done.append(after(block, *done[-1:]))
    return done[::-1]


def met(block, mask, count):
    rows = jnp.split(block, count, axis=1)
    return jnp.concatenate([rows[at ^ mask] for at in range(count)], axis=1)


def paired(blocks, mask, slices, kind):
    arrived = crossed(jnp.stack(blocks[1::2]), "proj", slices, mask)
    kept = blocks[::2]
    moved = [met(arrived[at], mask, kept[at].shape[1]).astype(jnp.float32) for at in range(len(kept))]
    return [(value.astype(jnp.float32) + other).astype(kind) for value, other in zip(kept, moved)]


def after(value, *tokens):
    return lax.optimization_barrier((value, tokens))[0]


def over_shares(rows, shares):
    near = jnp.concatenate(rows, axis=0)
    return [near] + [crossed(near, "dp", shares, mask) for mask in range(2, shares, 2)]


def products(near, far, train_flat, shares):
    contract = (((1,), (1,)), ((), ()))
    values = []
    for block in (near, far):
        value = lax.dot_general(block, train_flat, contract, preferred_element_type=jnp.float32)
        values.append(value.astype(jnp.bfloat16))
    return values


def split_shares(values, shares):
    values = [value.reshape(shares // 2, -1, value.shape[1]) for value in values]
    return [values[at % 2][at // 2] for at in range(shares)]


def turned(blocks, mask):
    bit = 1
    while bit < len(blocks):
        swap = mask // bit % 2 == 1
        blocks = [jnp.where(swap, blocks[at ^ bit], blocks[at]) for at in range(len(blocks))]
        bit *= 2
    return blocks


def body(queries, train_grads, out_basis, in_basis, corrections):
    slices = lax.axis_size("proj")
    shares = lax.axis_size("dp")
    here = lax.axis_index("proj")
    share = lax.axis_index("dp")
    count, rows_here, columns = queries.shape
    width = rows_here * columns
    owned = shares // slices
    train_count = train_grads.shape[0]
    train_flat = flatten(train_grads)
    row_blocks = out_basis.reshape(slices, rows_here, -1)
    basis = jnp.concatenate(turned([row_blocks[at] for at in range(slices)], here), axis=0)
    condition = condition_fast if rows_here % 16 == 0 else condition_plain
    parts = [count * size // sum(CHUNKS) for size in CHUNKS]
    source = queries
    half = slices // 2
    pieces, results = [], []
    for chunk, part in enumerate(parts):
        first, each = sum(parts[:chunk]), part // slices
        if chunk:
            source, pieces[0][-1], train_flat = lax.optimization_barrier((source, pieces[0][-1], train_flat))
        raw = {}
        for mask in (reversed(range(slices)) if chunk else reversed(range(slices))):
            block = lax.dynamic_slice_in_dim(source, first + (here ^ mask) * each, each, 0)
            raw[mask], source = lax.optimization_barrier((block, source))
        pieces.append(exchanged(raw, slices))
    made = condition(pieces[0], basis, in_basis, corrections)
    first_rows = exchanged(made, slices)
    first_rows[:half], pieces[1] = lax.optimization_barrier((first_rows[:half], pieces[1]))
    spread_a1 = over_shares(first_rows[:half], shares)
    made = condition(pieces[1], basis, in_basis, corrections)
    last_rows = exchanged(made, slices)
    first_rows[half:], last_rows[1] = lax.optimization_barrier((first_rows[half:], last_rows[1]))
    spread_a2 = over_shares(first_rows[half:], shares)
    last_rows[:half], spread_a1 = lax.optimization_barrier((last_rows[:half], spread_a1))
    place = here ^ (share // owned)
    spread_a1 = after(spread_a1, last_rows[1])
    near_a1 = lax.optimization_barrier(jnp.concatenate(spread_a1, axis=0))
    far_a1 = crossed(near_a1, "dp", shares, 1)
    val_a1 = products(near_a1, far_a1, train_flat, shares)
    spread_b1 = over_shares(last_rows[:half], shares)
    near_a2 = lax.optimization_barrier(jnp.concatenate(spread_a2, axis=0))
    far_a2 = crossed(near_a2, "dp", shares, 1)
    val_a2 = products(near_a2, far_a2, train_flat, shares)
    part_a1 = split_shares(val_a1, shares)
    part_a1 = [jnp.concatenate(part_a1[at * owned:(at + 1) * owned]) for at in range(slices)]
    part_a1 = [value.reshape(owned, half, -1, train_count) for value in part_a1]
    part_a2 = split_shares(val_a2, shares)
    part_a2 = [jnp.concatenate(part_a2[at * owned:(at + 1) * owned]) for at in range(slices)]
    part_a2 = [value.reshape(owned, half, -1, train_count) for value in part_a2]
    blocks = turned([jnp.concatenate(pair, axis=1) for pair in zip(part_a1, part_a2)], place)
    blocks = in_turn(blocks)
    came = exchanged(blocks, slices)
    group = after(last_rows[half:], near_a2)
    spread_b2 = over_shares(group, shares)
    spread_b1 = after(spread_b1, came[0])
    near_b1 = lax.optimization_barrier(jnp.concatenate(spread_b1, axis=0))
    far_b1 = crossed(near_b1, "dp", shares, 1)
    val_b1 = products(near_b1, far_b1, train_flat, shares)
    spread_b2 = after(spread_b2, came[0])
    near_b2 = lax.optimization_barrier(jnp.concatenate(spread_b2, axis=0))
    far_b2 = crossed(near_b2, "dp", shares, 1)
    val_b2 = products(near_b2, far_b2, train_flat, shares)
    part_b1 = split_shares(val_b1, shares)
    part_b1 = [jnp.concatenate(part_b1[at * owned:(at + 1) * owned]) for at in range(slices)]
    part_b1 = [value.reshape(owned, half, -1, train_count) for value in part_b1]
    part_b2 = split_shares(val_b2, shares)
    part_b2 = [jnp.concatenate(part_b2[at * owned:(at + 1) * owned]) for at in range(slices)]
    part_b2 = [value.reshape(owned, half, -1, train_count) for value in part_b2]
    blocks = turned([jnp.concatenate(pair, axis=1) for pair in zip(part_b1, part_b2)], place)
    blocks = in_turn(blocks)
    left = exchanged(blocks, slices)
    last = [sum(left[mask][:, at ^ mask].astype(jnp.float32) for mask in range(slices)) for at in range(slices)]
    whole = [sum(came[mask][:, at ^ mask].astype(jnp.float32) for mask in range(slices)) for at in range(slices)]
    for part, total in zip(parts, (whole, last)):
        total = jnp.stack(turned(total, here), axis=1)
        total = jnp.stack(turned([total[at] for at in range(owned)], share % owned))
        results.append(total.reshape(owned, part, train_count))
    return jnp.concatenate(results, axis=1).reshape(owned * count, train_count)


def solution(mesh):
    in_specs = (P(("groups", "dp"), "proj", None), P(("groups", "dp"), "proj", None), P(), P(), P())
    out_specs = P(("groups", "proj"), "dp")
    return jax.shard_map(body, mesh=mesh, in_specs=in_specs, out_specs=out_specs, check_vma=False)
```

```python
import functools
import jax
import jax.numpy as jnp
from jax import lax
from jax.experimental import pallas as pl
from jax.experimental.pallas import tpu as pltpu
from jax.sharding import PartitionSpec as P

damping_term = 0.05
CHUNKS = (8, 8)
BLOCK = 64


def halves(value):
    high = value.astype(jnp.bfloat16)
    return high, (value - high.astype(jnp.float32)).astype(jnp.bfloat16)


def times(left, right):
    return jnp.dot(left, right, preferred_element_type=jnp.float32)


def three_wide(matrix):
    high, low = halves(matrix)
    return jnp.concatenate([high, low, high], axis=1)


def three_deep(matrix):
    high, low = halves(matrix)
    return jnp.concatenate([high, high, low], axis=0)


def condition_kernel(slices, rows_here, *refs):
    pieces = refs[:slices][::-1]
    basis, across, right_basis, right_across, corrections = refs[slices:slices + 5]
    outs, stage = refs[slices + 5:-1], refs[-1]
    enter, leave = three_wide(across[...]), three_wide(basis[...])
    right, back = halves(right_basis[...]), halves(right_across[...])
    count, _, columns = pieces[0].shape
    out_rows = slices * rows_here
    parts = []
    for piece in pieces:
        flat = piece[...].reshape(count * rows_here, columns)
        parts.append(halves(times(flat, right[0]) + times(flat, right[1])))
    scale = jnp.concatenate([1.0 / (corrections[...] + damping_term)] * 2, axis=1)

    def gathered(at, which):
        rows = slice(at * rows_here, (at + 1) * rows_here)
        return jnp.concatenate([part[which][rows] for part in parts], axis=0)

    for at in range(0, count, 2):
        high = jnp.concatenate([gathered(at, 0), gathered(at + 1, 0)], axis=1)
        low = jnp.concatenate([gathered(at, 1), gathered(at + 1, 1)], axis=1)
        rotated = times(enter, jnp.concatenate([high, high, low], axis=0))
        result = times(leave, three_deep(rotated * scale))
        stage[at * out_rows:(at + 1) * out_rows, :] = result[:, :columns]
        stage[(at + 1) * out_rows:(at + 2) * out_rows, :] = result[:, columns:]
    high, low = halves(stage[...])
    stage[...] = times(high, back[0]) + times(low, back[0]) + times(high, back[1])
    for row in range(out_rows):
        value = stage[pl.ds(row, count, stride=out_rows), :].astype(jnp.bfloat16)
        at = row % rows_here * columns
        outs[row // rows_here][:, at:at + columns] = value


def condition_fast(pieces, basis, in_basis, corrections):
    slices = len(pieces)
    count, rows_here, columns = pieces[0].shape
    block = min(BLOCK, count)
    width = rows_here * columns
    piece_spec = pl.BlockSpec((block, rows_here, columns), lambda step: (step, 0, 0))
    out_spec = pl.BlockSpec((block, width), lambda step: (step, 0))
    whole = pl.BlockSpec(memory_space=pltpu.VMEM)
    order = basis.shape[0]
    return pl.pallas_call(
        functools.partial(condition_kernel, slices, rows_here),
        grid=(count // block,),
        in_specs=[piece_spec] * slices + [whole] * 5,
        out_specs=[out_spec] * slices,
        out_shape=[jax.ShapeDtypeStruct((count, width), jnp.bfloat16)] * slices,
        scratch_shapes=[pltpu.VMEM((block * order, columns), jnp.float32)],
        compiler_params=pltpu.CompilerParams(vmem_limit_bytes=32 * 1024 * 1024),
        cost_estimate=pl.CostEstimate(flops=0, bytes_accessed=0, transcendentals=0),
    )(*pieces[::-1], basis, basis.T, in_basis, in_basis.T, corrections)


def condition_plain(pieces, basis, in_basis, corrections):
    high = lax.Precision.HIGH
    count, rows_here, columns = pieces[0].shape
    values = jnp.concatenate(pieces, axis=1).astype(jnp.float32)
    inner = jnp.einsum("qbc,cd->qbd", values, in_basis, precision=high)
    rotated = jnp.einsum("ba,qbd->qad", basis, inner, precision=high)
    left = jnp.einsum("ba,qad->qbd", basis, rotated / (corrections + damping_term), precision=high)
    result = jnp.einsum("qbd,ed->qbe", left, in_basis, precision=high).astype(jnp.bfloat16)
    starts = range(0, basis.shape[0], rows_here)
    return [result[:, at:at + rows_here].reshape(count, rows_here * columns) for at in starts]


def crossed(value, axis, size, mask):
    return lax.ppermute(value, axis, [(at, at ^ mask) for at in range(size)])


def exchanged(blocks, slices):
    moved = {mask: crossed(blocks[mask], "proj", slices, mask) for mask in reversed(range(1, slices))}
    return [blocks[0]] + [moved[mask] for mask in range(1, slices)]


def in_turn(blocks):
    done = []
    for block in reversed(blocks):
        done.append(after(block, *done[-1:]))
    return done[::-1]


def met(block, mask, count):
    rows = jnp.split(block, count, axis=1)
    return jnp.concatenate([rows[at ^ mask] for at in range(count)], axis=1)


def paired(blocks, mask, slices, kind):
    arrived = crossed(jnp.stack(blocks[1::2]), "proj", slices, mask)
    kept = blocks[::2]
    moved = [met(arrived[at], mask, kept[at].shape[1]).astype(jnp.float32) for at in range(len(kept))]
    return [(value.astype(jnp.float32) + other).astype(kind) for value, other in zip(kept, moved)]


def after(value, *tokens):
    return lax.optimization_barrier((value, tokens))[0]


def over_shares(rows, shares):
    near = jnp.concatenate(rows, axis=0)
    return [near] + [crossed(near, "dp", shares, mask) for mask in range(2, shares, 2)]


def products(near, far, train_flat, shares):
    contract = (((1,), (1,)), ((), ()))
    values = []
    for block in (near, far):
        value = lax.dot_general(block, train_flat, contract, preferred_element_type=jnp.float32)
        values.append(value.astype(jnp.bfloat16))
    return values


def split_shares(values, shares):
    values = [value.reshape(shares // 2, -1, value.shape[1]) for value in values]
    return [values[at % 2][at // 2] for at in range(shares)]


def turned(blocks, mask):
    bit = 1
    while bit < len(blocks):
        swap = mask // bit % 2 == 1
        blocks = [jnp.where(swap, blocks[at ^ bit], blocks[at]) for at in range(len(blocks))]
        bit *= 2
    return blocks


def body(queries, train_grads, out_basis, in_basis, corrections):
    slices = lax.axis_size("proj")
    shares = lax.axis_size("dp")
    here = lax.axis_index("proj")
    share = lax.axis_index("dp")
    count, rows_here, columns = queries.shape
    width = rows_here * columns
    owned = shares // slices
    train_count = train_grads.shape[0]
    train_flat = lax.optimization_barrier(train_grads.reshape(train_count, width))
    row_blocks = out_basis.reshape(slices, rows_here, -1)
    basis = jnp.concatenate(turned([row_blocks[at] for at in range(slices)], here), axis=0)
    condition = condition_fast if rows_here % 16 == 0 else condition_plain
    parts = [count * size // sum(CHUNKS) for size in CHUNKS]
    source = queries
    half = slices // 2
    pieces, results = [], []
    for chunk, part in enumerate(parts):
        first, each = sum(parts[:chunk]), part // slices
        if chunk:
            source, pieces[0][-1], train_flat = lax.optimization_barrier((source, pieces[0][-1], train_flat))
        raw = {}
        for mask in (range(slices) if chunk else reversed(range(slices))):
            block = lax.dynamic_slice_in_dim(source, first + (here ^ mask) * each, each, 0)
            raw[mask], source = lax.optimization_barrier((block, source))
        pieces.append(exchanged(raw, slices))
    made = condition(pieces[0], basis, in_basis, corrections)
    first_rows = exchanged(made, slices)
    first_rows[:half], pieces[1] = lax.optimization_barrier((first_rows[:half], pieces[1]))
    spread_a1 = over_shares(first_rows[:half], shares)
    made = condition(pieces[1], basis, in_basis, corrections)
    last_rows = exchanged(made, slices)
    spread_a2 = over_shares(first_rows[half:], shares)
    last_rows[:half], spread_a1 = lax.optimization_barrier((last_rows[:half], spread_a1))
    place = here ^ (share // owned)
    near_a1 = lax.optimization_barrier(jnp.concatenate(spread_a1, axis=0))
    far_a1 = crossed(near_a1, "dp", shares, 1)
    val_a1 = products(near_a1, far_a1, train_flat, shares)
    spread_b1 = over_shares(last_rows[:half], shares)
    near_a2 = lax.optimization_barrier(jnp.concatenate(spread_a2, axis=0))
    far_a2 = crossed(near_a2, "dp", shares, 1)
    val_a2 = products(near_a2, far_a2, train_flat, shares)
    part_a1 = split_shares(val_a1, shares)
    part_a1 = [jnp.concatenate(part_a1[at * owned:(at + 1) * owned]) for at in range(slices)]
    part_a1 = [value.reshape(owned, half, -1, train_count) for value in part_a1]
    part_a2 = split_shares(val_a2, shares)
    part_a2 = [jnp.concatenate(part_a2[at * owned:(at + 1) * owned]) for at in range(slices)]
    part_a2 = [value.reshape(owned, half, -1, train_count) for value in part_a2]
    blocks = turned([jnp.concatenate(pair, axis=1) for pair in zip(part_a1, part_a2)], place)
    blocks = in_turn(blocks)
    came = exchanged(blocks, slices)
    group = after(last_rows[half:], near_a2)
    spread_b2 = over_shares(group, shares)
    spread_b1 = after(spread_b1, came[0])
    near_b1 = lax.optimization_barrier(jnp.concatenate(spread_b1, axis=0))
    far_b1 = crossed(near_b1, "dp", shares, 1)
    val_b1 = products(near_b1, far_b1, train_flat, shares)
    spread_b2 = after(spread_b2, came[0])
    near_b2 = lax.optimization_barrier(jnp.concatenate(spread_b2, axis=0))
    far_b2 = crossed(near_b2, "dp", shares, 1)
    val_b2 = products(near_b2, far_b2, train_flat, shares)
    part_b1 = split_shares(val_b1, shares)
    part_b1 = [jnp.concatenate(part_b1[at * owned:(at + 1) * owned]) for at in range(slices)]
    part_b1 = [value.reshape(owned, half, -1, train_count) for value in part_b1]
    part_b2 = split_shares(val_b2, shares)
    part_b2 = [jnp.concatenate(part_b2[at * owned:(at + 1) * owned]) for at in range(slices)]
    part_b2 = [value.reshape(owned, half, -1, train_count) for value in part_b2]
    blocks = turned([jnp.concatenate(pair, axis=1) for pair in zip(part_b1, part_b2)], place)
    blocks = in_turn(blocks)
    left = exchanged(blocks, slices)
    last = [sum(left[mask][:, at ^ mask].astype(jnp.float32) for mask in range(slices)) for at in range(slices)]
    came = after(came, *left[:1])
    whole = [sum(came[mask][:, at ^ mask].astype(jnp.float32) for mask in range(slices)) for at in range(slices)]
    for part, total in zip(parts, (whole, last)):
        total = jnp.stack(turned(total, here), axis=1)
        total = jnp.stack(turned([total[at] for at in range(owned)], share % owned))
        results.append(total.reshape(owned, part, train_count))
    return jnp.concatenate(results, axis=1).reshape(owned * count, train_count)


def solution(mesh):
    in_specs = (P(("groups", "dp"), "proj", None), P(("groups", "dp"), "proj", None), P(), P(), P())
    out_specs = P(("groups", "proj"), "dp")
    return jax.shard_map(body, mesh=mesh, in_specs=in_specs, out_specs=out_specs, check_vma=False)
```

```python
import functools
import jax
import jax.numpy as jnp
from jax import lax
from jax.experimental import pallas as pl
from jax.experimental.pallas import tpu as pltpu
from jax.sharding import PartitionSpec as P

damping_term = 0.05
CHUNKS = (8, 8)
BLOCK = 64


def halves(value):
    high = value.astype(jnp.bfloat16)
    return high, (value - high.astype(jnp.float32)).astype(jnp.bfloat16)


def times(left, right):
    return jnp.dot(left, right, preferred_element_type=jnp.float32)


def three_wide(matrix):
    high, low = halves(matrix)
    return jnp.concatenate([high, low, high], axis=1)


def three_deep(matrix):
    high, low = halves(matrix)
    return jnp.concatenate([high, high, low], axis=0)


def condition_kernel(slices, rows_here, *refs):
    pieces = refs[:slices][::-1]
    basis, across, right_basis, right_across, corrections = refs[slices:slices + 5]
    outs, stage = refs[slices + 5:-1], refs[-1]
    enter, leave = three_wide(across[...]), three_wide(basis[...])
    right, back = halves(right_basis[...]), halves(right_across[...])
    count, _, columns = pieces[0].shape
    out_rows = slices * rows_here
    parts = []
    for piece in pieces:
        flat = piece[...].reshape(count * rows_here, columns)
        parts.append(halves(times(flat, right[0]) + times(flat, right[1])))
    scale = jnp.concatenate([1.0 / (corrections[...] + damping_term)] * 2, axis=1)

    def gathered(at, which):
        rows = slice(at * rows_here, (at + 1) * rows_here)
        return jnp.concatenate([part[which][rows] for part in parts], axis=0)

    for at in range(0, count, 2):
        high = jnp.concatenate([gathered(at, 0), gathered(at + 1, 0)], axis=1)
        low = jnp.concatenate([gathered(at, 1), gathered(at + 1, 1)], axis=1)
        rotated = times(enter, jnp.concatenate([high, high, low], axis=0))
        result = times(leave, three_deep(rotated * scale))
        stage[at * out_rows:(at + 1) * out_rows, :] = result[:, :columns]
        stage[(at + 1) * out_rows:(at + 2) * out_rows, :] = result[:, columns:]
    high, low = halves(stage[...])
    stage[...] = times(high, back[0]) + times(low, back[0]) + times(high, back[1])
    for row in range(out_rows):
        value = stage[pl.ds(row, count, stride=out_rows), :].astype(jnp.bfloat16)
        at = row % rows_here * columns
        outs[row // rows_here][:, at:at + columns] = value


def condition_fast(pieces, basis, in_basis, corrections):
    slices = len(pieces)
    count, rows_here, columns = pieces[0].shape
    block = min(BLOCK, count)
    width = rows_here * columns
    piece_spec = pl.BlockSpec((block, rows_here, columns), lambda step: (step, 0, 0))
    out_spec = pl.BlockSpec((block, width), lambda step: (step, 0))
    whole = pl.BlockSpec(memory_space=pltpu.VMEM)
    order = basis.shape[0]
    return pl.pallas_call(
        functools.partial(condition_kernel, slices, rows_here),
        grid=(count // block,),
        in_specs=[piece_spec] * slices + [whole] * 5,
        out_specs=[out_spec] * slices,
        out_shape=[jax.ShapeDtypeStruct((count, width), jnp.bfloat16)] * slices,
        scratch_shapes=[pltpu.VMEM((block * order, columns), jnp.float32)],
        compiler_params=pltpu.CompilerParams(vmem_limit_bytes=32 * 1024 * 1024),
        cost_estimate=pl.CostEstimate(flops=0, bytes_accessed=0, transcendentals=0),
    )(*pieces[::-1], basis, basis.T, in_basis, in_basis.T, corrections)


def condition_plain(pieces, basis, in_basis, corrections):
    high = lax.Precision.HIGH
    count, rows_here, columns = pieces[0].shape
    values = jnp.concatenate(pieces, axis=1).astype(jnp.float32)
    inner = jnp.einsum("qbc,cd->qbd", values, in_basis, precision=high)
    rotated = jnp.einsum("ba,qbd->qad", basis, inner, precision=high)
    left = jnp.einsum("ba,qad->qbd", basis, rotated / (corrections + damping_term), precision=high)
    result = jnp.einsum("qbd,ed->qbe", left, in_basis, precision=high).astype(jnp.bfloat16)
    starts = range(0, basis.shape[0], rows_here)
    return [result[:, at:at + rows_here].reshape(count, rows_here * columns) for at in starts]


def crossed(value, axis, size, mask):
    return lax.ppermute(value, axis, [(at, at ^ mask) for at in range(size)])


def exchanged(blocks, slices):
    moved = {mask: crossed(blocks[mask], "proj", slices, mask) for mask in reversed(range(1, slices))}
    return [blocks[0]] + [moved[mask] for mask in range(1, slices)]


def in_turn(blocks):
    done = []
    for block in reversed(blocks):
        done.append(after(block, *done[-1:]))
    return done[::-1]


def met(block, mask, count):
    rows = jnp.split(block, count, axis=1)
    return jnp.concatenate([rows[at ^ mask] for at in range(count)], axis=1)


def paired(blocks, mask, slices, kind):
    arrived = crossed(jnp.stack(blocks[1::2]), "proj", slices, mask)
    kept = blocks[::2]
    moved = [met(arrived[at], mask, kept[at].shape[1]).astype(jnp.float32) for at in range(len(kept))]
    return [(value.astype(jnp.float32) + other).astype(kind) for value, other in zip(kept, moved)]


def after(value, *tokens):
    return lax.optimization_barrier((value, tokens))[0]


def over_shares(rows, shares):
    near = jnp.concatenate(rows, axis=0)
    return [near] + [crossed(near, "dp", shares, mask) for mask in range(2, shares, 2)]


def products(near, far, train_flat, shares):
    contract = (((1,), (1,)), ((), ()))
    values = []
    for block in (near, far):
        value = lax.dot_general(block, train_flat, contract, preferred_element_type=jnp.float32)
        values.append(value.astype(jnp.bfloat16))
    return values


def split_shares(values, shares):
    values = [value.reshape(shares // 2, -1, value.shape[1]) for value in values]
    return [values[at % 2][at // 2] for at in range(shares)]


def turned(blocks, mask):
    bit = 1
    while bit < len(blocks):
        swap = mask // bit % 2 == 1
        blocks = [jnp.where(swap, blocks[at ^ bit], blocks[at]) for at in range(len(blocks))]
        bit *= 2
    return blocks


def body(queries, train_grads, out_basis, in_basis, corrections):
    slices = lax.axis_size("proj")
    shares = lax.axis_size("dp")
    here = lax.axis_index("proj")
    share = lax.axis_index("dp")
    count, rows_here, columns = queries.shape
    width = rows_here * columns
    owned = shares // slices
    train_count = train_grads.shape[0]
    train_flat = lax.optimization_barrier(train_grads.reshape(train_count, width))
    row_blocks = out_basis.reshape(slices, rows_here, -1)
    basis = jnp.concatenate(turned([row_blocks[at] for at in range(slices)], here), axis=0)
    condition = condition_fast if rows_here % 16 == 0 else condition_plain
    parts = [count * size // sum(CHUNKS) for size in CHUNKS]
    source = queries
    half = slices // 2
    pieces, results = [], []
    for chunk, part in enumerate(parts):
        first, each = sum(parts[:chunk]), part // slices
        if chunk:
            source, pieces[0][-1], train_flat = lax.optimization_barrier((source, pieces[0][-1], train_flat))
        raw = {}
        for mask in (range(slices) if chunk else reversed(range(slices))):
            block = lax.dynamic_slice_in_dim(source, first + (here ^ mask) * each, each, 0)
            raw[mask], source = lax.optimization_barrier((block, source))
        pieces.append(exchanged(raw, slices))
    made = condition(pieces[0], basis, in_basis, corrections)
    first_rows = exchanged(made, slices)
    first_rows[:half], pieces[1] = lax.optimization_barrier((first_rows[:half], pieces[1]))
    spread_a1 = over_shares(first_rows[:half], shares)
    made = condition(pieces[1], basis, in_basis, corrections)
    last_rows = exchanged(made, slices)
    spread_a2 = over_shares(first_rows[half:], shares)
    last_rows[:half], spread_a1 = lax.optimization_barrier((last_rows[:half], spread_a1))
    place = here ^ (share // owned)
    near_a1 = lax.optimization_barrier(jnp.concatenate(spread_a1, axis=0))
    far_a1 = crossed(near_a1, "dp", shares, 1)
    val_a1 = products(near_a1, far_a1, train_flat, shares)
    spread_b1 = over_shares(last_rows[:half], shares)
    near_a2 = lax.optimization_barrier(jnp.concatenate(spread_a2, axis=0))
    far_a2 = crossed(near_a2, "dp", shares, 1)
    val_a2 = products(near_a2, far_a2, train_flat, shares)
    part_a1 = split_shares(val_a1, shares)
    part_a1 = [jnp.concatenate(part_a1[at * owned:(at + 1) * owned]) for at in range(slices)]
    part_a1 = [value.reshape(owned, half, -1, train_count) for value in part_a1]
    part_a2 = split_shares(val_a2, shares)
    part_a2 = [jnp.concatenate(part_a2[at * owned:(at + 1) * owned]) for at in range(slices)]
    part_a2 = [value.reshape(owned, half, -1, train_count) for value in part_a2]
    blocks = turned([jnp.concatenate(pair, axis=1) for pair in zip(part_a1, part_a2)], place)
    blocks = in_turn(blocks)
    came = exchanged(blocks, slices)
    group = after(last_rows[half:], near_a2)
    spread_b2 = over_shares(group, shares)
    spread_b1 = after(spread_b1, came[0])
    near_b1 = lax.optimization_barrier(jnp.concatenate(spread_b1, axis=0))
    far_b1 = crossed(near_b1, "dp", shares, 1)
    val_b1 = products(near_b1, far_b1, train_flat, shares)
    spread_b2 = after(spread_b2, came[0])
    near_b2 = lax.optimization_barrier(jnp.concatenate(spread_b2, axis=0))
    far_b2 = crossed(near_b2, "dp", shares, 1)
    val_b2 = products(near_b2, far_b2, train_flat, shares)
    part_b1 = split_shares(val_b1, shares)
    part_b1 = [jnp.concatenate(part_b1[at * owned:(at + 1) * owned]) for at in range(slices)]
    part_b1 = [value.reshape(owned, half, -1, train_count) for value in part_b1]
    part_b2 = split_shares(val_b2, shares)
    part_b2 = [jnp.concatenate(part_b2[at * owned:(at + 1) * owned]) for at in range(slices)]
    part_b2 = [value.reshape(owned, half, -1, train_count) for value in part_b2]
    blocks = turned([jnp.concatenate(pair, axis=1) for pair in zip(part_b1, part_b2)], place)
    blocks = in_turn(blocks[::-1])[::-1]
    left = exchanged(blocks, slices)
    last = [sum(left[mask][:, at ^ mask].astype(jnp.float32) for mask in range(slices)) for at in range(slices)]
    whole = [sum(came[mask][:, at ^ mask].astype(jnp.float32) for mask in range(slices)) for at in range(slices)]
    for part, total in zip(parts, (whole, last)):
        total = jnp.stack(turned(total, here), axis=1)
        total = jnp.stack(turned([total[at] for at in range(owned)], share % owned))
        results.append(total.reshape(owned, part, train_count))
    return jnp.concatenate(results, axis=1).reshape(owned * count, train_count)


def solution(mesh):
    in_specs = (P(("groups", "dp"), "proj", None), P(("groups", "dp"), "proj", None), P(), P(), P())
    out_specs = P(("groups", "proj"), "dp")
    return jax.shard_map(body, mesh=mesh, in_specs=in_specs, out_specs=out_specs, check_vma=False)
```

```python
import functools
import jax
import jax.numpy as jnp
from jax import lax
from jax.experimental import pallas as pl
from jax.experimental.pallas import tpu as pltpu
from jax.sharding import PartitionSpec as P

damping_term = 0.05
CHUNKS = (8, 8)
BLOCK = 64


def halves(value):
    high = value.astype(jnp.bfloat16)
    return high, (value - high.astype(jnp.float32)).astype(jnp.bfloat16)


def times(left, right):
    return jnp.dot(left, right, preferred_element_type=jnp.float32)


def three_wide(matrix):
    high, low = halves(matrix)
    return jnp.concatenate([high, low, high], axis=1)


def three_deep(matrix):
    high, low = halves(matrix)
    return jnp.concatenate([high, high, low], axis=0)


def condition_kernel(slices, rows_here, *refs):
    pieces = refs[:slices][::-1]
    basis, across, right_basis, right_across, corrections = refs[slices:slices + 5]
    outs, stage = refs[slices + 5:-1], refs[-1]
    enter, leave = three_wide(across[...]), three_wide(basis[...])
    right, back = halves(right_basis[...]), halves(right_across[...])
    count, _, columns = pieces[0].shape
    out_rows = slices * rows_here
    parts = []
    for piece in pieces:
        flat = piece[...].reshape(count * rows_here, columns)
        parts.append(halves(times(flat, right[0]) + times(flat, right[1])))
    scale = jnp.concatenate([1.0 / (corrections[...] + damping_term)] * 2, axis=1)

    def gathered(at, which):
        rows = slice(at * rows_here, (at + 1) * rows_here)
        return jnp.concatenate([part[which][rows] for part in parts], axis=0)

    for at in range(0, count, 2):
        high = jnp.concatenate([gathered(at, 0), gathered(at + 1, 0)], axis=1)
        low = jnp.concatenate([gathered(at, 1), gathered(at + 1, 1)], axis=1)
        rotated = times(enter, jnp.concatenate([high, high, low], axis=0))
        result = times(leave, three_deep(rotated * scale))
        stage[at * out_rows:(at + 1) * out_rows, :] = result[:, :columns]
        stage[(at + 1) * out_rows:(at + 2) * out_rows, :] = result[:, columns:]
    high, low = halves(stage[...])
    stage[...] = times(high, back[0]) + times(low, back[0]) + times(high, back[1])
    for row in range(out_rows):
        value = stage[pl.ds(row, count, stride=out_rows), :].astype(jnp.bfloat16)
        at = row % rows_here * columns
        outs[row // rows_here][:, at:at + columns] = value


def condition_fast(pieces, basis, in_basis, corrections):
    slices = len(pieces)
    count, rows_here, columns = pieces[0].shape
    block = min(BLOCK, count)
    width = rows_here * columns
    piece_spec = pl.BlockSpec((block, rows_here, columns), lambda step: (step, 0, 0))
    out_spec = pl.BlockSpec((block, width), lambda step: (step, 0))
    whole = pl.BlockSpec(memory_space=pltpu.VMEM)
    order = basis.shape[0]
    return pl.pallas_call(
        functools.partial(condition_kernel, slices, rows_here),
        grid=(count // block,),
        in_specs=[piece_spec] * slices + [whole] * 5,
        out_specs=[out_spec] * slices,
        out_shape=[jax.ShapeDtypeStruct((count, width), jnp.bfloat16)] * slices,
        scratch_shapes=[pltpu.VMEM((block * order, columns), jnp.float32)],
        compiler_params=pltpu.CompilerParams(vmem_limit_bytes=32 * 1024 * 1024),
        cost_estimate=pl.CostEstimate(flops=0, bytes_accessed=0, transcendentals=0),
    )(*pieces[::-1], basis, basis.T, in_basis, in_basis.T, corrections)


def condition_plain(pieces, basis, in_basis, corrections):
    high = lax.Precision.HIGH
    count, rows_here, columns = pieces[0].shape
    values = jnp.concatenate(pieces, axis=1).astype(jnp.float32)
    inner = jnp.einsum("qbc,cd->qbd", values, in_basis, precision=high)
    rotated = jnp.einsum("ba,qbd->qad", basis, inner, precision=high)
    left = jnp.einsum("ba,qad->qbd", basis, rotated / (corrections + damping_term), precision=high)
    result = jnp.einsum("qbd,ed->qbe", left, in_basis, precision=high).astype(jnp.bfloat16)
    starts = range(0, basis.shape[0], rows_here)
    return [result[:, at:at + rows_here].reshape(count, rows_here * columns) for at in starts]


def crossed(value, axis, size, mask):
    return lax.ppermute(value, axis, [(at, at ^ mask) for at in range(size)])


def exchanged(blocks, slices):
    moved = {mask: crossed(blocks[mask], "proj", slices, mask) for mask in reversed(range(1, slices))}
    return [blocks[0]] + [moved[mask] for mask in range(1, slices)]


def in_turn(blocks):
    done = []
    for block in reversed(blocks):
        done.append(after(block, *done[-1:]))
    return done[::-1]


def met(block, mask, count):
    rows = jnp.split(block, count, axis=1)
    return jnp.concatenate([rows[at ^ mask] for at in range(count)], axis=1)


def paired(blocks, mask, slices, kind):
    arrived = crossed(jnp.stack(blocks[1::2]), "proj", slices, mask)
    kept = blocks[::2]
    moved = [met(arrived[at], mask, kept[at].shape[1]).astype(jnp.float32) for at in range(len(kept))]
    return [(value.astype(jnp.float32) + other).astype(kind) for value, other in zip(kept, moved)]


def after(value, *tokens):
    return lax.optimization_barrier((value, tokens))[0]


def over_shares(rows, shares):
    near = jnp.concatenate(rows, axis=0)
    return [near] + [crossed(near, "dp", shares, mask) for mask in range(2, shares, 2)]


def products(near, far, train_flat, shares):
    contract = (((1,), (1,)), ((), ()))
    values = []
    for block in (near, far):
        value = lax.dot_general(block, train_flat, contract, preferred_element_type=jnp.float32)
        values.append(value.astype(jnp.bfloat16))
    return values


def split_shares(values, shares):
    values = [value.reshape(shares // 2, -1, value.shape[1]) for value in values]
    return [values[at % 2][at // 2] for at in range(shares)]


def turned(blocks, mask):
    bit = 1
    while bit < len(blocks):
        swap = mask // bit % 2 == 1
        blocks = [jnp.where(swap, blocks[at ^ bit], blocks[at]) for at in range(len(blocks))]
        bit *= 2
    return blocks


def body(queries, train_grads, out_basis, in_basis, corrections):
    slices = lax.axis_size("proj")
    shares = lax.axis_size("dp")
    here = lax.axis_index("proj")
    share = lax.axis_index("dp")
    count, rows_here, columns = queries.shape
    width = rows_here * columns
    owned = shares // slices
    train_count = train_grads.shape[0]
    train_flat = lax.optimization_barrier(train_grads.reshape(train_count, width))
    row_blocks = out_basis.reshape(slices, rows_here, -1)
    basis = jnp.concatenate(turned([row_blocks[at] for at in range(slices)], here), axis=0)
    condition = condition_fast if rows_here % 16 == 0 else condition_plain
    parts = [count * size // sum(CHUNKS) for size in CHUNKS]
    source = queries
    half = slices // 2
    pieces, results = [], []
    for chunk, part in enumerate(parts):
        first, each = sum(parts[:chunk]), part // slices
        if chunk:
            source, pieces[0][-1], train_flat = lax.optimization_barrier((source, pieces[0][-1], train_flat))
        raw = {}
        for mask in (range(slices) if chunk else reversed(range(slices))):
            block = lax.dynamic_slice_in_dim(source, first + (here ^ mask) * each, each, 0)
            raw[mask], source = lax.optimization_barrier((block, source))
        pieces.append(exchanged(raw, slices))
    made = condition(pieces[0], basis, in_basis, corrections)
    first_rows = exchanged(made, slices)
    first_rows[:half], pieces[1] = lax.optimization_barrier((first_rows[:half], pieces[1]))
    spread_a1 = over_shares(first_rows[:half], shares)
    made = condition(pieces[1], basis, in_basis, corrections)
    last_rows = exchanged(made, slices)
    spread_a2 = over_shares(first_rows[half:], shares)
    last_rows[:half], spread_a1 = lax.optimization_barrier((last_rows[:half], spread_a1))
    place = here ^ (share // owned)
    near_a1 = lax.optimization_barrier(jnp.concatenate(spread_a1, axis=0))
    far_a1 = crossed(near_a1, "dp", shares, 1)
    val_a1 = products(near_a1, far_a1, train_flat, shares)
    spread_b1 = over_shares(last_rows[:half], shares)
    near_a2 = lax.optimization_barrier(jnp.concatenate(spread_a2, axis=0))
    far_a2 = crossed(near_a2, "dp", shares, 1)
    val_a2 = products(near_a2, far_a2, train_flat, shares)
    part_a1 = split_shares(val_a1, shares)
    part_a1 = [jnp.concatenate(part_a1[at * owned:(at + 1) * owned]) for at in range(slices)]
    part_a1 = [value.reshape(owned, half, -1, train_count) for value in part_a1]
    part_a2 = split_shares(val_a2, shares)
    part_a2 = [jnp.concatenate(part_a2[at * owned:(at + 1) * owned]) for at in range(slices)]
    part_a2 = [value.reshape(owned, half, -1, train_count) for value in part_a2]
    blocks = turned([jnp.concatenate(pair, axis=1) for pair in zip(part_a1, part_a2)], place)
    blocks = in_turn(blocks)
    came = exchanged(blocks, slices)
    group = after(last_rows[half:], near_a2)
    spread_b2 = over_shares(group, shares)
    spread_b1 = after(spread_b1, came[0])
    near_b1 = lax.optimization_barrier(jnp.concatenate(spread_b1, axis=0))
    far_b1 = crossed(near_b1, "dp", shares, 1)
    val_b1 = products(near_b1, far_b1, train_flat, shares)
    spread_b2 = after(spread_b2, came[0])
    near_b2 = lax.optimization_barrier(jnp.concatenate(spread_b2, axis=0))
    far_b2 = crossed(near_b2, "dp", shares, 1)
    val_b2 = products(near_b2, far_b2, train_flat, shares)
    part_b1 = split_shares(val_b1, shares)
    part_b1 = [jnp.concatenate(part_b1[at * owned:(at + 1) * owned]) for at in range(slices)]
    part_b1 = [value.reshape(owned, half, -1, train_count) for value in part_b1]
    part_b2 = split_shares(val_b2, shares)
    part_b2 = [jnp.concatenate(part_b2[at * owned:(at + 1) * owned]) for at in range(slices)]
    part_b2 = [value.reshape(owned, half, -1, train_count) for value in part_b2]
    blocks = turned([jnp.concatenate(pair, axis=1) for pair in zip(part_b1, part_b2)], place)
    blocks = in_turn(blocks)
    left = exchanged(blocks, slices)
    last = [sum(left[mask][:, at ^ mask].astype(jnp.float32) for mask in range(slices)) for at in range(slices)]
    came = after(came, *left[:1])
    whole = [sum(came[mask][:, at ^ mask].astype(jnp.float32) for mask in range(slices)) for at in range(slices)]
    for part, total in zip(parts, (whole, last)):
        total = jnp.stack(turned(total, here), axis=1)
        total = jnp.stack(turned([total[at] for at in range(owned)], share % owned))
        results.append(total.reshape(owned, part, train_count))
    scores = jnp.pad(results[0], ((0, 0), (0, count - parts[0]), (0, 0)))
    scores = lax.optimization_barrier(scores)
    scores = lax.dynamic_update_slice_in_dim(scores, results[1], parts[0], 1)
    return scores.reshape(owned * count, train_count)


def solution(mesh):
    in_specs = (P(("groups", "dp"), "proj", None), P(("groups", "dp"), "proj", None), P(), P(), P())
    out_specs = P(("groups", "proj"), "dp")
    return jax.shard_map(body, mesh=mesh, in_specs=in_specs, out_specs=out_specs, check_vma=False)
```

```python
import functools
import jax
import jax.numpy as jnp
from jax import lax
from jax.experimental import pallas as pl
from jax.experimental.pallas import tpu as pltpu
from jax.sharding import PartitionSpec as P

damping_term = 0.05
CHUNKS = (8, 8)
BLOCK = 64


def halves(value):
    high = value.astype(jnp.bfloat16)
    return high, (value - high.astype(jnp.float32)).astype(jnp.bfloat16)


def times(left, right):
    return jnp.dot(left, right, preferred_element_type=jnp.float32)


def three_wide(matrix):
    high, low = halves(matrix)
    return jnp.concatenate([high, low, high], axis=1)


def three_deep(matrix):
    high, low = halves(matrix)
    return jnp.concatenate([high, high, low], axis=0)


def condition_kernel(slices, rows_here, *refs):
    pieces = refs[:slices][::-1]
    basis, across, right_basis, right_across, corrections = refs[slices:slices + 5]
    outs, stage = refs[slices + 5:-1], refs[-1]
    enter, leave = three_wide(across[...]), three_wide(basis[...])
    right, back = halves(right_basis[...]), halves(right_across[...])
    count, _, columns = pieces[0].shape
    out_rows = slices * rows_here
    parts = []
    for piece in pieces:
        flat = piece[...].reshape(count * rows_here, columns)
        parts.append(halves(times(flat, right[0]) + times(flat, right[1])))
    scale = jnp.concatenate([1.0 / (corrections[...] + damping_term)] * 2, axis=1)

    def gathered(at, which):
        rows = slice(at * rows_here, (at + 1) * rows_here)
        return jnp.concatenate([part[which][rows] for part in parts], axis=0)

    for at in range(0, count, 2):
        high = jnp.concatenate([gathered(at, 0), gathered(at + 1, 0)], axis=1)
        low = jnp.concatenate([gathered(at, 1), gathered(at + 1, 1)], axis=1)
        rotated = times(enter, jnp.concatenate([high, high, low], axis=0))
        result = times(leave, three_deep(rotated * scale))
        stage[at * out_rows:(at + 1) * out_rows, :] = result[:, :columns]
        stage[(at + 1) * out_rows:(at + 2) * out_rows, :] = result[:, columns:]
    high, low = halves(stage[...])
    stage[...] = times(high, back[0]) + times(low, back[0]) + times(high, back[1])
    for row in range(out_rows):
        value = stage[pl.ds(row, count, stride=out_rows), :].astype(jnp.bfloat16)
        at = row % rows_here * columns
        outs[row // rows_here][:, at:at + columns] = value


def condition_fast(pieces, basis, in_basis, corrections):
    slices = len(pieces)
    count, rows_here, columns = pieces[0].shape
    block = min(BLOCK, count)
    width = rows_here * columns
    piece_spec = pl.BlockSpec((block, rows_here, columns), lambda step: (step, 0, 0))
    out_spec = pl.BlockSpec((block, width), lambda step: (step, 0))
    whole = pl.BlockSpec(memory_space=pltpu.VMEM)
    order = basis.shape[0]
    return pl.pallas_call(
        functools.partial(condition_kernel, slices, rows_here),
        grid=(count // block,),
        in_specs=[piece_spec] * slices + [whole] * 5,
        out_specs=[out_spec] * slices,
        out_shape=[jax.ShapeDtypeStruct((count, width), jnp.bfloat16)] * slices,
        scratch_shapes=[pltpu.VMEM((block * order, columns), jnp.float32)],
        compiler_params=pltpu.CompilerParams(vmem_limit_bytes=32 * 1024 * 1024),
        cost_estimate=pl.CostEstimate(flops=0, bytes_accessed=0, transcendentals=0),
    )(*pieces[::-1], basis, basis.T, in_basis, in_basis.T, corrections)


def condition_plain(pieces, basis, in_basis, corrections):
    high = lax.Precision.HIGH
    count, rows_here, columns = pieces[0].shape
    values = jnp.concatenate(pieces, axis=1).astype(jnp.float32)
    inner = jnp.einsum("qbc,cd->qbd", values, in_basis, precision=high)
    rotated = jnp.einsum("ba,qbd->qad", basis, inner, precision=high)
    left = jnp.einsum("ba,qad->qbd", basis, rotated / (corrections + damping_term), precision=high)
    result = jnp.einsum("qbd,ed->qbe", left, in_basis, precision=high).astype(jnp.bfloat16)
    starts = range(0, basis.shape[0], rows_here)
    return [result[:, at:at + rows_here].reshape(count, rows_here * columns) for at in starts]


def crossed(value, axis, size, mask):
    return lax.ppermute(value, axis, [(at, at ^ mask) for at in range(size)])


def exchanged(blocks, slices):
    moved = {mask: crossed(blocks[mask], "proj", slices, mask) for mask in reversed(range(1, slices))}
    return [blocks[0]] + [moved[mask] for mask in range(1, slices)]


def in_turn(blocks):
    done = []
    for block in reversed(blocks):
        done.append(after(block, *done[-1:]))
    return done[::-1]


def met(block, mask, count):
    rows = jnp.split(block, count, axis=1)
    return jnp.concatenate([rows[at ^ mask] for at in range(count)], axis=1)


def paired(blocks, mask, slices, kind):
    arrived = crossed(jnp.stack(blocks[1::2]), "proj", slices, mask)
    kept = blocks[::2]
    moved = [met(arrived[at], mask, kept[at].shape[1]).astype(jnp.float32) for at in range(len(kept))]
    return [(value.astype(jnp.float32) + other).astype(kind) for value, other in zip(kept, moved)]


def after(value, *tokens):
    return lax.optimization_barrier((value, tokens))[0]


def over_shares(rows, shares):
    near = jnp.concatenate(rows, axis=0)
    return [near] + [crossed(near, "dp", shares, mask) for mask in range(2, shares, 2)]


def products(near, far, train_flat, shares):
    contract = (((1,), (1,)), ((), ()))
    values = []
    for block in (near, far):
        value = lax.dot_general(block, train_flat, contract, preferred_element_type=jnp.float32)
        values.append(value.astype(jnp.bfloat16))
    return values


def split_shares(values, shares):
    values = [value.reshape(shares // 2, -1, value.shape[1]) for value in values]
    return [values[at % 2][at // 2] for at in range(shares)]


def turned(blocks, mask):
    bit = 1
    while bit < len(blocks):
        swap = mask // bit % 2 == 1
        blocks = [jnp.where(swap, blocks[at ^ bit], blocks[at]) for at in range(len(blocks))]
        bit *= 2
    return blocks


def body(queries, train_grads, out_basis, in_basis, corrections):
    slices = lax.axis_size("proj")
    shares = lax.axis_size("dp")
    here = lax.axis_index("proj")
    share = lax.axis_index("dp")
    count, rows_here, columns = queries.shape
    width = rows_here * columns
    owned = shares // slices
    train_count = train_grads.shape[0]
    train_flat = lax.optimization_barrier(train_grads.reshape(train_count, width))
    row_blocks = out_basis.reshape(slices, rows_here, -1)
    basis = jnp.concatenate(turned([row_blocks[at] for at in range(slices)], here), axis=0)
    condition = condition_fast if rows_here % 16 == 0 else condition_plain
    parts = [count * size // sum(CHUNKS) for size in CHUNKS]
    source = queries
    half = slices // 2
    pieces, results = [], []
    for chunk, part in enumerate(parts):
        first, each = sum(parts[:chunk]), part // slices
        if chunk:
            source, pieces[0][-1], train_flat = lax.optimization_barrier((source, pieces[0][-1], train_flat))
        raw = {}
        for mask in (range(slices) if chunk else reversed(range(slices))):
            block = lax.dynamic_slice_in_dim(source, first + (here ^ mask) * each, each, 0)
            raw[mask], source = lax.optimization_barrier((block, source))
        pieces.append(exchanged(raw, slices))
    made = condition(pieces[0], basis, in_basis, corrections)
    first_rows = exchanged(made, slices)
    first_rows[:half], pieces[1] = lax.optimization_barrier((first_rows[:half], pieces[1]))
    spread_a1 = over_shares(first_rows[:half], shares)
    made = condition(pieces[1], basis, in_basis, corrections)
    last_rows = exchanged(made, slices)
    spread_a2 = over_shares(first_rows[half:], shares)
    last_rows[:half], spread_a1 = lax.optimization_barrier((last_rows[:half], spread_a1))
    place = here ^ (share // owned)
    near_a1 = lax.optimization_barrier(jnp.concatenate(spread_a1, axis=0))
    far_a1 = crossed(near_a1, "dp", shares, 1)
    val_a1 = products(near_a1, far_a1, train_flat, shares)
    spread_b1 = over_shares(last_rows[:half], shares)
    near_a2 = lax.optimization_barrier(jnp.concatenate(spread_a2, axis=0))
    far_a2 = crossed(near_a2, "dp", shares, 1)
    val_a2 = products(near_a2, far_a2, train_flat, shares)
    part_a1 = split_shares(val_a1, shares)
    part_a1 = [jnp.concatenate(part_a1[at * owned:(at + 1) * owned]) for at in range(slices)]
    part_a1 = [value.reshape(owned, half, -1, train_count) for value in part_a1]
    part_a2 = split_shares(val_a2, shares)
    part_a2 = [jnp.concatenate(part_a2[at * owned:(at + 1) * owned]) for at in range(slices)]
    part_a2 = [value.reshape(owned, half, -1, train_count) for value in part_a2]
    blocks = turned([jnp.concatenate(pair, axis=1) for pair in zip(part_a1, part_a2)], place)
    blocks = in_turn(blocks)
    came = exchanged(blocks, slices)
    group = after(last_rows[half:], near_a2)
    spread_b2 = over_shares(group, shares)
    spread_b1 = after(spread_b1, came[0])
    near_b1 = lax.optimization_barrier(jnp.concatenate(spread_b1, axis=0))
    far_b1 = crossed(near_b1, "dp", shares, 1)
    spread_b2 = after(spread_b2, came[0])
    near_b2 = lax.optimization_barrier(jnp.concatenate(spread_b2, axis=0))
    far_b2 = crossed(near_b2, "dp", shares, 1)
    both = lax.optimization_barrier(jnp.concatenate([far_b1, near_b2], axis=0))
    joint = products(both, far_b2, train_flat, shares)
    cut = far_b1.shape[0]
    val_b1 = [products(near_b1, near_b1, train_flat, shares)[0], joint[0][:cut]]
    val_b2 = [joint[0][cut:], joint[1]]
    part_b1 = split_shares(val_b1, shares)
    part_b1 = [jnp.concatenate(part_b1[at * owned:(at + 1) * owned]) for at in range(slices)]
    part_b1 = [value.reshape(owned, half, -1, train_count) for value in part_b1]
    part_b2 = split_shares(val_b2, shares)
    part_b2 = [jnp.concatenate(part_b2[at * owned:(at + 1) * owned]) for at in range(slices)]
    part_b2 = [value.reshape(owned, half, -1, train_count) for value in part_b2]
    blocks = turned([jnp.concatenate(pair, axis=1) for pair in zip(part_b1, part_b2)], place)
    blocks = in_turn(blocks)
    left = exchanged(blocks, slices)
    last = [sum(left[mask][:, at ^ mask].astype(jnp.float32) for mask in range(slices)) for at in range(slices)]
    came = after(came, *left[:1])
    whole = [sum(came[mask][:, at ^ mask].astype(jnp.float32) for mask in range(slices)) for at in range(slices)]
    for part, total in zip(parts, (whole, last)):
        total = jnp.stack(turned(total, here), axis=1)
        total = jnp.stack(turned([total[at] for at in range(owned)], share % owned))
        results.append(total.reshape(owned, part, train_count))
    return jnp.concatenate(results, axis=1).reshape(owned * count, train_count)


def solution(mesh):
    in_specs = (P(("groups", "dp"), "proj", None), P(("groups", "dp"), "proj", None), P(), P(), P())
    out_specs = P(("groups", "proj"), "dp")
    return jax.shard_map(body, mesh=mesh, in_specs=in_specs, out_specs=out_specs, check_vma=False)
```

```python
import functools
import jax
import jax.numpy as jnp
from jax import lax
from jax.experimental import pallas as pl
from jax.experimental.pallas import tpu as pltpu
from jax.sharding import PartitionSpec as P

damping_term = 0.05
CHUNKS = (8, 8)
BLOCK = 64


def halves(value):
    high = value.astype(jnp.bfloat16)
    return high, (value - high.astype(jnp.float32)).astype(jnp.bfloat16)


def times(left, right):
    return jnp.dot(left, right, preferred_element_type=jnp.float32)


def three_wide(matrix):
    high, low = halves(matrix)
    return jnp.concatenate([high, low, high], axis=1)


def three_deep(matrix):
    high, low = halves(matrix)
    return jnp.concatenate([high, high, low], axis=0)


def condition_kernel(slices, rows_here, *refs):
    pieces = refs[:slices][::-1]
    basis, across, right_basis, right_across, corrections = refs[slices:slices + 5]
    outs, stage = refs[slices + 5:-1], refs[-1]
    enter, leave = three_wide(across[...]), three_wide(basis[...])
    right, back = halves(right_basis[...]), halves(right_across[...])
    count, _, columns = pieces[0].shape
    out_rows = slices * rows_here
    parts = []
    for piece in pieces:
        flat = piece[...].reshape(count * rows_here, columns)
        parts.append(halves(times(flat, right[0]) + times(flat, right[1])))
    scale = jnp.concatenate([1.0 / (corrections[...] + damping_term)] * 2, axis=1)

    def gathered(at, which):
        rows = slice(at * rows_here, (at + 1) * rows_here)
        return jnp.concatenate([part[which][rows] for part in parts], axis=0)

    for at in range(0, count, 2):
        high = jnp.concatenate([gathered(at, 0), gathered(at + 1, 0)], axis=1)
        low = jnp.concatenate([gathered(at, 1), gathered(at + 1, 1)], axis=1)
        rotated = times(enter, jnp.concatenate([high, high, low], axis=0))
        result = times(leave, three_deep(rotated * scale))
        stage[at * out_rows:(at + 1) * out_rows, :] = result[:, :columns]
        stage[(at + 1) * out_rows:(at + 2) * out_rows, :] = result[:, columns:]
    high, low = halves(stage[...])
    stage[...] = times(high, back[0]) + times(low, back[0]) + times(high, back[1])
    for row in range(out_rows):
        value = stage[pl.ds(row, count, stride=out_rows), :].astype(jnp.bfloat16)
        at = row % rows_here * columns
        outs[row // rows_here][:, at:at + columns] = value


def condition_fast(pieces, basis, in_basis, corrections):
    slices = len(pieces)
    count, rows_here, columns = pieces[0].shape
    block = min(BLOCK, count)
    width = rows_here * columns
    piece_spec = pl.BlockSpec((block, rows_here, columns), lambda step: (step, 0, 0))
    out_spec = pl.BlockSpec((block, width), lambda step: (step, 0))
    whole = pl.BlockSpec(memory_space=pltpu.VMEM)
    order = basis.shape[0]
    return pl.pallas_call(
        functools.partial(condition_kernel, slices, rows_here),
        grid=(count // block,),
        in_specs=[piece_spec] * slices + [whole] * 5,
        out_specs=[out_spec] * slices,
        out_shape=[jax.ShapeDtypeStruct((count, width), jnp.bfloat16)] * slices,
        scratch_shapes=[pltpu.VMEM((block * order, columns), jnp.float32)],
        compiler_params=pltpu.CompilerParams(vmem_limit_bytes=32 * 1024 * 1024),
        cost_estimate=pl.CostEstimate(flops=0, bytes_accessed=0, transcendentals=0),
    )(*pieces[::-1], basis, basis.T, in_basis, in_basis.T, corrections)


def condition_plain(pieces, basis, in_basis, corrections):
    high = lax.Precision.HIGH
    count, rows_here, columns = pieces[0].shape
    values = jnp.concatenate(pieces, axis=1).astype(jnp.float32)
    inner = jnp.einsum("qbc,cd->qbd", values, in_basis, precision=high)
    rotated = jnp.einsum("ba,qbd->qad", basis, inner, precision=high)
    left = jnp.einsum("ba,qad->qbd", basis, rotated / (corrections + damping_term), precision=high)
    result = jnp.einsum("qbd,ed->qbe", left, in_basis, precision=high).astype(jnp.bfloat16)
    starts = range(0, basis.shape[0], rows_here)
    return [result[:, at:at + rows_here].reshape(count, rows_here * columns) for at in starts]


def crossed(value, axis, size, mask):
    return lax.ppermute(value, axis, [(at, at ^ mask) for at in range(size)])


def exchanged(blocks, slices):
    moved = {mask: crossed(blocks[mask], "proj", slices, mask) for mask in reversed(range(1, slices))}
    return [blocks[0]] + [moved[mask] for mask in range(1, slices)]


def in_turn(blocks):
    done = []
    for block in reversed(blocks):
        done.append(after(block, *done[-1:]))
    return done[::-1]


def met(block, mask, count):
    rows = jnp.split(block, count, axis=1)
    return jnp.concatenate([rows[at ^ mask] for at in range(count)], axis=1)


def paired(blocks, mask, slices, kind):
    arrived = crossed(jnp.stack(blocks[1::2]), "proj", slices, mask)
    kept = blocks[::2]
    moved = [met(arrived[at], mask, kept[at].shape[1]).astype(jnp.float32) for at in range(len(kept))]
    return [(value.astype(jnp.float32) + other).astype(kind) for value, other in zip(kept, moved)]


def after(value, *tokens):
    return lax.optimization_barrier((value, tokens))[0]


def over_shares(rows, shares):
    near = jnp.concatenate(rows, axis=0)
    return [near] + [crossed(near, "dp", shares, mask) for mask in range(2, shares, 2)]


def products(near, far, train_flat, shares):
    contract = (((1,), (1,)), ((), ()))
    values = []
    for block in (near, far):
        value = lax.dot_general(block, train_flat, contract, preferred_element_type=jnp.float32)
        values.append(value.astype(jnp.bfloat16))
    return values


def split_shares(values, shares):
    values = [value.reshape(shares // 2, -1, value.shape[1]) for value in values]
    return [values[at % 2][at // 2] for at in range(shares)]


def turned(blocks, mask):
    bit = 1
    while bit < len(blocks):
        swap = mask // bit % 2 == 1
        blocks = [jnp.where(swap, blocks[at ^ bit], blocks[at]) for at in range(len(blocks))]
        bit *= 2
    return blocks


def body(queries, train_grads, out_basis, in_basis, corrections):
    slices = lax.axis_size("proj")
    shares = lax.axis_size("dp")
    here = lax.axis_index("proj")
    share = lax.axis_index("dp")
    count, rows_here, columns = queries.shape
    width = rows_here * columns
    owned = shares // slices
    train_count = train_grads.shape[0]
    train_flat = lax.optimization_barrier(train_grads.reshape(train_count, width))
    row_blocks = out_basis.reshape(slices, rows_here, -1)
    basis = jnp.concatenate(turned([row_blocks[at] for at in range(slices)], here), axis=0)
    condition = condition_fast if rows_here % 16 == 0 else condition_plain
    parts = [count * size // sum(CHUNKS) for size in CHUNKS]
    source = queries
    half = slices // 2
    pieces, results = [], []
    for chunk, part in enumerate(parts):
        first, each = sum(parts[:chunk]), part // slices
        if chunk:
            source, pieces[0][-1], train_flat = lax.optimization_barrier((source, pieces[0][-1], train_flat))
        raw = {}
        for mask in (reversed(range(slices)) if chunk else reversed(range(slices))):
            block = lax.dynamic_slice_in_dim(source, first + (here ^ mask) * each, each, 0)
            raw[mask], source = lax.optimization_barrier((block, source))
        pieces.append(exchanged(raw, slices))
    made = condition(pieces[0], basis, in_basis, corrections)
    first_rows = exchanged(made, slices)
    first_rows[:half], pieces[1] = lax.optimization_barrier((first_rows[:half], pieces[1]))
    spread_a1 = over_shares(first_rows[:half], shares)
    made = condition(pieces[1], basis, in_basis, corrections)
    last_rows = exchanged(made, slices)
    spread_a2 = over_shares(first_rows[half:], shares)
    last_rows[:half], spread_a1 = lax.optimization_barrier((last_rows[:half], spread_a1))
    place = here ^ (share // owned)
    near_a1 = lax.optimization_barrier(jnp.concatenate(spread_a1, axis=0))
    far_a1 = crossed(near_a1, "dp", shares, 1)
    val_a1 = products(near_a1, far_a1, train_flat, shares)
    spread_b1 = over_shares(last_rows[:half], shares)
    near_a2 = lax.optimization_barrier(jnp.concatenate(spread_a2, axis=0))
    far_a2 = crossed(near_a2, "dp", shares, 1)
    val_a2 = products(near_a2, far_a2, train_flat, shares)
    part_a1 = split_shares(val_a1, shares)
    part_a1 = [jnp.concatenate(part_a1[at * owned:(at + 1) * owned]) for at in range(slices)]
    part_a1 = [value.reshape(owned, half, -1, train_count) for value in part_a1]
    part_a2 = split_shares(val_a2, shares)
    part_a2 = [jnp.concatenate(part_a2[at * owned:(at + 1) * owned]) for at in range(slices)]
    part_a2 = [value.reshape(owned, half, -1, train_count) for value in part_a2]
    blocks = turned([jnp.concatenate(pair, axis=1) for pair in zip(part_a1, part_a2)], place)
    blocks = in_turn(blocks)
    came = exchanged(blocks, slices)
    group = after(last_rows[half:], near_a2)
    spread_b2 = over_shares(group, shares)
    spread_b1 = after(spread_b1, came[0])
    near_b1 = lax.optimization_barrier(jnp.concatenate(spread_b1, axis=0))
    far_b1 = crossed(near_b1, "dp", shares, 1)
    val_b1 = products(near_b1, far_b1, train_flat, shares)
    spread_b2 = after(spread_b2, came[0])
    near_b2 = lax.optimization_barrier(jnp.concatenate(spread_b2, axis=0))
    far_b2 = crossed(near_b2, "dp", shares, 1)
    val_b2 = products(near_b2, far_b2, train_flat, shares)
    part_b1 = split_shares(val_b1, shares)
    part_b1 = [jnp.concatenate(part_b1[at * owned:(at + 1) * owned]) for at in range(slices)]
    part_b1 = [value.reshape(owned, half, -1, train_count) for value in part_b1]
    part_b2 = split_shares(val_b2, shares)
    part_b2 = [jnp.concatenate(part_b2[at * owned:(at + 1) * owned]) for at in range(slices)]
    part_b2 = [value.reshape(owned, half, -1, train_count) for value in part_b2]
    blocks = turned([jnp.concatenate(pair, axis=1) for pair in zip(part_b1, part_b2)], place)
    blocks = in_turn(blocks)
    left = exchanged(blocks, slices)
    last = [sum(left[mask][:, at ^ mask].astype(jnp.float32) for mask in range(slices)) for at in range(slices)]
    whole = [sum(came[mask][:, at ^ mask].astype(jnp.float32) for mask in range(slices)) for at in range(slices)]
    for part, total in zip(parts, (whole, last)):
        total = jnp.stack(turned(total, here), axis=1)
        total = jnp.stack(turned([total[at] for at in range(owned)], share % owned))
        results.append(total.reshape(owned, part, train_count))
    return jnp.concatenate(results, axis=1).reshape(owned * count, train_count)


def solution(mesh):
    in_specs = (P(("groups", "dp"), "proj", None), P(("groups", "dp"), "proj", None), P(), P(), P())
    out_specs = P(("groups", "proj"), "dp")
    return jax.shard_map(body, mesh=mesh, in_specs=in_specs, out_specs=out_specs, check_vma=False)
```
